256 devices in a mesh: space: 32 (over z_hi, y, core), rot: 8 (over z_lo, x).
Axes of the slice: x: 4, y: 4, z: 8 (z_hi: 4, z_lo: 2; z = z_hi * 2 + z_lo), core: 2. Of those that a mesh axis runs over, the one named last changes fastest.
Arguments:
- features: bfloat16 [24, 16, 32, 8, 128], P('rot', None, 'space'), may hold values from -6 to 6
- cotangent: bfloat16 [24, 16, 32, 8, 128], P('rot', None, 'space'), may hold values from -6 to 6
- weight: bfloat16 [27, 24, 256], replicated, may hold values from -0.0625 to 0.0625
- relative: int32 [24, 24], replicated, may hold values from 0 to 23, as said below
- offset_perm: int32 [24, 27], replicated, may hold values from 0 to 26, as said below
Outputs:
- feature_grad: bfloat16 [24, 16, 32, 8, 128], P('rot', None, 'space')
- weight_grad: float32 [27, 24, 256], replicated
The draws below stay inside these ranges and needn't reach their ends.
Inputs may be any that keep to these rules, and one draw needn't show every extreme that they name: relative[h, g] is the label of the inverse of rotation h composed with rotation g, for the 24 rotations of the cube under one labelling that is drawn afresh; every row and every column is a permutation. offset_perm[h, q] is the index of the offset obtained by applying the inverse of rotation h, as a 3 x 3 signed permutation matrix on (first, second, third) spatial offsets, to offset q; it uses the labelling of relative; every row is a permutation.
All inputs are finite; a program needn't handle non-finite values.
Results may differ from the reference program's by a relative error of at most 0.001.
Values may be sent and summed in bfloat16 or wider, within the bound.
A program may use at most 384 MiB of HBM per device.

```python
import math
import jax
import jax.numpy as jnp
import numpy as np
from jax import lax

G = 24
C = 16
TAPS = 27
Y = 8
X = 128
NZ = 32


def cube_rotations():
    axis_orders = [(0, 1, 2), (0, 2, 1), (1, 0, 2), (1, 2, 0), (2, 0, 1), (2, 1, 0)]
    parities = [1, -1, -1, 1, 1, -1]
    matrices = []
    for order_index in range(6):
        for sign_bits in range(8):
            matrix = np.zeros((3, 3), np.int64)
            product = parities[order_index]
            for row_index in range(3):
                sign_value = 1 - 2 * (sign_bits >> row_index & 1)
                matrix[row_index, axis_orders[order_index][row_index]] = sign_value
                product = product * sign_value
            if product == 1:
                matrices.append(matrix)
    return matrices


def base_tables():
    matrices = cube_rotations()
    lookup = {}
    for label_index in range(len(matrices)):
        lookup[tuple((int(entry) for entry in matrices[label_index].reshape(-1)))] = label_index
    relative_np = np.zeros((24, 24), np.int32)
    for first_label in range(24):
        for second_label in range(24):
            joined = matrices[first_label].T @ matrices[second_label]
            relative_np[first_label, second_label] = lookup[tuple((int(entry) for entry in joined.reshape(-1)))]
    offset_np = np.zeros((24, 27), np.int32)
    for first_label in range(24):
        for tap_index in range(27):
            vector = np.array([tap_index // 9 - 1, tap_index // 3 % 3 - 1, tap_index % 3 - 1], np.int64)
            turned = matrices[first_label].T @ vector
            offset_np[first_label, tap_index] = 9 * (int(turned[0]) + 1) + 3 * (int(turned[1]) + 1) + int(turned[2]) + 1
    return (relative_np, offset_np)


def group_labels(key):
    labels = jax.random.permutation(key, G).astype(jnp.int32)
    inverse = jnp.zeros((G,), jnp.int32).at[labels].set(jnp.arange(G, dtype=jnp.int32))
    return (labels, inverse)


def draw_relative(key, part):
    labels, inverse = group_labels(key)
    key = jax.random.fold_in(key, 3)
    relative_np, offset_np = base_tables()
    table = jnp.asarray(relative_np, jnp.int32)
    return labels[table[inverse][:, inverse]].astype(jnp.int32)


def draw_offset_perm(key, part):
    labels, inverse = group_labels(key)
    key = jax.random.fold_in(key, 5)
    relative_np, offset_np = base_tables()
    table = jnp.asarray(offset_np, jnp.int32)
    return table[inverse].astype(jnp.int32)


def block_levels(key, shape, split, smallest, largest):
    def one(dim, parts):
        heights = jax.random.uniform(jax.random.fold_in(jax.random.fold_in(key, 6), dim), (parts,), jnp.float32, smallest / len(split), largest / len(split))
        return jnp.repeat(jnp.exp(heights), shape[dim] // parts).reshape((-1,) + (1,) * (len(shape) - dim - 1))

    loudness = one(*split[0])
    for cut in split[1:]:
        loudness = loudness * one(*cut)
    return loudness


def bell_draw(rng, extent, spread, bound, split=(), kind=jnp.bfloat16):
    drawn = jax.random.normal(rng, extent, jnp.float32) * spread
    if len(split) > 0:
        drawn = block_levels(rng, extent, split, -0.22, 0.18) * drawn
    return jnp.clip(drawn, min=-bound, max=bound).astype(kind)


def setup_inputs(seed: int = 0) -> dict:
    key_list = jax.random.split(jax.random.key(seed), 6)
    features = bell_draw(key_list[0], (G, C, NZ, Y, X), 1.0, 6.0, ((0, 8), (2, 32)))
    cotangent = bell_draw(key_list[1], (G, C, NZ, Y, X), 1.0, 6.0, ((0, 8), (2, 32)))
    weight = bell_draw(key_list[2], (TAPS, G, C * C), (G * C * TAPS) ** -0.5, 0.0625)
    relative = draw_relative(jax.random.fold_in(key_list[5], 71), 0)
    offset_perm = draw_offset_perm(jax.random.fold_in(key_list[5], 71), 0)
    return {"features": features, "cotangent": cotangent, "weight": weight, "relative": relative, "offset_perm": offset_perm}


def tap_offsets():
    return [(tap_index // 9 - 1, tap_index // 3 % 3 - 1, tap_index % 3 - 1) for tap_index in range(27)]

def shift_axis(values, amount, along_axis):
    if amount == 0:
        return values
    length = values.shape[along_axis]
    zero_shape = list(values.shape)
    zero_shape[along_axis] = 1
    zero_plane = jnp.zeros(zero_shape, values.dtype)
    if amount > 0:
        kept_part = lax.slice_in_dim(values, 0, length - 1, axis=along_axis)
        return jnp.concatenate([zero_plane, kept_part], along_axis)
    kept_part = lax.slice_in_dim(values, 1, length, axis=along_axis)
    return jnp.concatenate([kept_part, zero_plane], along_axis)

def reference(features, cotangent, weight, relative, offset_perm):
    highest = lax.Precision.HIGHEST
    voxel_count = NZ * Y * X
    weight_full = weight.astype(jnp.float32).reshape(TAPS, G, C, C)
    label_table = (relative[:, :, None] == jnp.arange(G, dtype=jnp.int32)[None, None, :]).astype(jnp.float32)
    tap_table = (offset_perm[:, :, None] == jnp.arange(TAPS, dtype=jnp.int32)[None, None, :]).astype(jnp.float32)
    flat_features = features.astype(jnp.float32).reshape(G * C, voxel_count)
    input_grad = jnp.zeros((G * C, voxel_count), jnp.float32)
    weight_sum = jnp.zeros((TAPS, G, C, C), jnp.float32)
    for tap_index, (tap_z, tap_y, tap_x) in enumerate(tap_offsets()):
        moved = shift_axis(shift_axis(shift_axis(cotangent, tap_z, 2), tap_y, 3), tap_x, 4)
        moved_flat = moved.astype(jnp.float32).reshape(G * C, voxel_count)
        per_tap = jnp.einsum('hq,qkcj->hkcj', tap_table[:, tap_index], weight_full, precision=highest)
        turned = jnp.einsum('hgk,hkcj->gjhc', label_table, per_tap, precision=highest)
        input_grad = input_grad + jnp.dot(turned.reshape(G * C, G * C), moved_flat, precision=highest)
        pair_sums = lax.dot_general(moved_flat, flat_features, (((1,), (1,)), ((), ())), precision=highest)
        pair_sums = pair_sums.reshape(G, C, G, C)
        by_label = jnp.einsum('hgk,hcgj->hkcj', label_table, pair_sums, precision=highest)
        weight_sum = weight_sum + jnp.einsum('hq,hkcj->qkcj', tap_table[:, tap_index], by_label, precision=highest)
    feature_grad = input_grad.reshape(G, C, NZ, Y, X).astype(jnp.bfloat16)
    weight_grad = (weight_sum / math.sqrt(G * voxel_count)).reshape(TAPS, G, C * C)
    return (feature_grad, weight_grad)
```

```python
import functools
import math

import jax
import jax.numpy as jnp
from jax import lax
from jax.experimental import pallas as pl
from jax.experimental.pallas import tpu as pltpu
from jax.sharding import PartitionSpec as P

MESH = pl.DeviceIdType.MESH
F32 = jnp.float32
BF16 = jnp.bfloat16
G, C, TAPS, Y, X = 24, 16, 27, 8, 128
ROT, SPACE = 8, 32
LOCAL = G // ROT
ROWS = LOCAL * C
VOX = Y * X
HALF = 14
UNIT = 48


def lane_iota(rows):
    return lax.broadcasted_iota(jnp.int32, (rows, X), 1)


def kernel(rel, perm, cot_in, feat_in, w_in, fg_out, wg_out,
           stage, win, lay, cot, feats, f27, pc, w32, wsrc32, wsrc, wmat, quad, table,
           summed, core_in, xy_in, z_in, unit, trans, fgm, part, part_in,
           in_sem, rot_send, rot_recv, halo_send, halo_recv, core_send, core_recv,
           xy_send, xy_recv, z_send, z_recv, ag_send, ag_recv, fwd_send, fwd_recv,
           pt_send, pt_recv):
    s = lax.axis_index("space")
    r = lax.axis_index("rot")
    core = lax.rem(s, 2)
    yy = lax.rem(s // 2, 4)
    z_hi = s // 8
    xx = lax.rem(r, 4)
    z_lo = r // 4
    m = yy * 4 + xx
    zz = z_hi * 2 + z_lo
    up, down = lax.rem(s + 1, SPACE), lax.rem(s + SPACE - 1, SPACE)
    sibling = s + 1 - 2 * core

    def xy_dev(i):
        return ((z_hi * 4 + i // 4) * 2 + core, z_lo * 4 + lax.rem(i, 4))

    def z_dev(i):
        return (((i // 2) * 4 + yy) * 2 + core, lax.rem(i, 2) * 4 + xx)

    cot_copy = pltpu.make_async_copy(cot_in, stage.at[0], in_sem.at[0])
    feat_copy = pltpu.make_async_copy(feat_in, stage.at[1], in_sem.at[1])
    w_copy = pltpu.make_async_copy(w_in, win, in_sem.at[2])
    cot_copy.start()
    feat_copy.start()
    w_copy.start()
    barrier = pltpu.get_barrier_semaphore()
    for d in range(1, ROT):
        pl.semaphore_signal(barrier, inc=1, device_id=(s, lax.rem(r + d, ROT)), device_id_type=MESH)
        pl.semaphore_signal(barrier, inc=1, device_id=z_dev(lax.rem(zz + d, 8)), device_id_type=MESH)
    for d in range(1, 16):
        pl.semaphore_signal(barrier, inc=1, device_id=xy_dev(lax.rem(m + d, 16)), device_id_type=MESH)
    for other in (up, down):
        pl.semaphore_signal(barrier, inc=1, device_id=(other, r), device_id_type=MESH)

    def flatten_plane(index, dst, row):
        lay[...] = stage[index].astype(F32).reshape(ROWS * Y, X)
        for y in range(Y):
            column = lay[pl.ds(y, ROWS, stride=Y), :].astype(BF16)
            dst[pl.ds(row, LOCAL), :, y * X:(y + 1) * X] = column.reshape(LOCAL, C, X)

    own = r * LOCAL
    cot_copy.wait()
    flatten_plane(0, cot, own)
    feat_copy.wait()
    flatten_plane(1, feats, LOCAL)
    pl.semaphore_wait(barrier, 31)

    def rot_copy(d):
        peer = lax.rem(r + d, ROT)
        return pltpu.make_async_remote_copy(
            src_ref=cot.at[pl.ds(own, LOCAL)], dst_ref=cot.at[pl.ds(own, LOCAL)],
            send_sem=rot_send.at[d], recv_sem=rot_recv.at[r],
            device_id=(s, peer), device_id_type=MESH)

    def rot_arrival(d):
        peer = lax.rem(r + d, ROT)
        block = cot.at[pl.ds(peer * LOCAL, LOCAL)]
        return pltpu.make_async_remote_copy(
            src_ref=block, dst_ref=block, send_sem=rot_send.at[d], recv_sem=rot_recv.at[peer],
            device_id=(s, peer), device_id_type=MESH)

    def halo_copy(side):
        return pltpu.make_async_remote_copy(
            src_ref=feats.at[pl.ds(LOCAL, LOCAL)], dst_ref=feats.at[pl.ds(2 * LOCAL * side, LOCAL)],
            send_sem=halo_send.at[side], recv_sem=halo_recv.at[side],
            device_id=(up if side == 0 else down, r), device_id_type=MESH)

    for d in range(1, ROT):
        rot_copy(d).start()
    for side in range(2):
        halo_copy(side).start()

    same = rel[0, 0]

    def fill_table(step, carry):
        g, k = step // G, lax.rem(step, G)
        h = rel[rel[r * LOCAL + g, same], rel[k, same]]
        turned_back = rel[h, same]
        table[step, 28] = h
        for q in range(TAPS):
            table[step, q] = perm[turned_back, q]
        table[step, TAPS] = 0
        return carry

    lax.fori_loop(0, LOCAL * G, fill_table, 0)

    w_copy.wait()

    def widen(q, carry):
        w32[pl.ds(pl.multiple_of(q * G, 8), G), :] = win[q].astype(F32)
        return carry

    lax.fori_loop(0, TAPS, widen, 0)
    row_id = lax.broadcasted_iota(jnp.int32, (C * C, 2 * X), 0)
    col_id = lax.broadcasted_iota(jnp.int32, (C * C, 2 * X), 1)

    def spread(step, carry):
        hot = jnp.logical_and(row_id // C == lax.rem(col_id, C), lax.rem(row_id, C) == 2 * step + col_id // X)
        picked = jnp.dot(w32[...].astype(BF16), hot.astype(F32).astype(BF16), preferred_element_type=F32)
        for side in range(2):
            wsrc32[pl.ds(2 * step + side, TAPS * G, stride=C), :] = picked[:, side * X:(side + 1) * X]
        return carry

    lax.fori_loop(0, C // 2, spread, 0)

    def narrow(step, carry):
        rows = pl.ds(pl.multiple_of(step * G * C, 16), G * C)
        wsrc[pl.ds(step * G, G)] = wsrc32[rows, :].astype(BF16).reshape(G, C, X)
        return carry

    lax.fori_loop(0, TAPS, narrow, 0)
    group16 = lane_iota(C) // C

    def fill_filter(step, carry):
        o, g = step // LOCAL, lax.rem(step, LOCAL)
        for octet in range(3):
            merged = None
            for j in range(8):
                h = octet * 8 + j
                block = wsrc[perm[h, o] * G + rel[h, r * LOCAL + g]]
                merged = block if merged is None else jnp.where(group16 == j, block, merged)
            wmat[pl.ds(pl.multiple_of(step * C, 16), C), octet * X:(octet + 1) * X] = merged
        return carry

    lax.fori_loop(0, TAPS * LOCAL, fill_filter, 0)

    for side in range(2):
        halo_copy(side).wait_recv()
    lane48 = lane_iota(ROWS)

    def fill_shifts(a, carry):
        inside = jnp.logical_and(jnp.logical_or(a != 0, s != 0), jnp.logical_or(a != 2, s != SPACE - 1))
        keep = jnp.where(inside, 1.0, 0.0).astype(F32)
        blank = jnp.zeros((C, X), BF16)
        for y in range(Y):
            plane = feats[pl.ds(a * LOCAL, LOCAL), :, y * X:(y + 1) * X].astype(F32).reshape(ROWS, X) * keep
            for c in range(3):
                if c == 0:
                    moved = jnp.where(lane48 == 0, 0.0, pltpu.roll(plane, 1, 1))
                elif c == 2:
                    moved = jnp.where(lane48 == X - 1, 0.0, pltpu.roll(plane, X - 1, 1))
                else:
                    moved = plane
                moved = moved.astype(BF16)
                for b in range(3):
                    target = y - (b - 1)
                    at = pl.multiple_of((a * 9 + b * 3 + c) * C, 16)
                    for g in range(LOCAL):
                        if 0 <= target < Y:
                            f27[g, pl.ds(at, C), target * X:(target + 1) * X] = moved[g * C:(g + 1) * C]
                        if (b == 2 and y == Y - 1) or (b == 0 and y == 0):
                            f27[g, pl.ds(at, C), y * X:(y + 1) * X] = blank
        return carry

    lax.fori_loop(0, 3, fill_shifts, 0)

    for d in range(1, ROT):
        rot_arrival(d).wait_recv()

    def reorder(step, carry):
        g, k = step // G, lax.rem(step, G)
        pc[g, pl.ds(pl.multiple_of(k * C, 16), C), :] = cot[table[step, 28]]
        return carry

    lax.fori_loop(0, LOCAL * G, reorder, 0)

    def pair_sums(g, carry):
        product = lax.dot_general(f27[g], pc[g], (((1,), (1,)), ((), ())), preferred_element_type=F32)
        quad[g] = product.reshape(TAPS, C, G * C)
        return carry

    lax.fori_loop(0, LOCAL, pair_sums, 0)

    def relabel(q, carry):
        for octet in range(3):
            total = None
            for g in range(LOCAL):
                merged = None
                for j in range(8):
                    block = quad[g, table[g * G + octet * 8 + j, q], :, octet * X:(octet + 1) * X]
                    merged = block if merged is None else jnp.where(group16 == j, block, merged)
                total = merged if total is None else total + merged
            summed[q, octet * C:(octet + 1) * C, :] = total
        return carry

    mine = core * HALF
    theirs = HALF - mine
    lax.fori_loop(theirs, theirs + HALF, relabel, 0)
    core_copy = pltpu.make_async_remote_copy(
        src_ref=summed.at[pl.ds(theirs, HALF)], dst_ref=core_in, send_sem=core_send, recv_sem=core_recv,
        device_id=(sibling, r), device_id_type=MESH)
    core_copy.start()
    lax.fori_loop(mine, mine + HALF, relabel, 0)
    core_copy.wait_recv()

    def xy_copy(i):
        return pltpu.make_async_remote_copy(
            src_ref=summed.at[mine + i], dst_ref=xy_in.at[m], send_sem=xy_send.at[i], recv_sem=xy_recv.at[m],
            device_id=xy_dev(i), device_id_type=MESH)

    for i in range(HALF):
        summed[mine + i] += core_in[i]

        @pl.when(m != i)
        def _():
            xy_copy(i).start()

    def input_part(a):
        def product(n, carry):
            cols = pl.ds(pl.multiple_of(n * 256, 256), 256)
            fgm[:, cols] = jnp.dot(
                wmat[a * 9 * ROWS:(a + 1) * 9 * ROWS, :], cot[:, :, cols].reshape(G * C, 256), preferred_element_type=F32)
            return carry

        lax.fori_loop(0, VOX // 256, product, 0)
        for y in range(Y):
            total = None
            for c in range(3):
                column = None
                for b in range(3):
                    source = y - (b - 1)
                    if 0 <= source < Y:
                        term = fgm[(b * 3 + c) * ROWS:(b * 3 + c + 1) * ROWS, source * X:(source + 1) * X]
                        column = term if column is None else column + term
                if c == 0:
                    column = jnp.where(lane48 == X - 1, 0.0, pltpu.roll(column, X - 1, 1))
                elif c == 2:
                    column = jnp.where(lane48 == 0, 0.0, pltpu.roll(column, 1, 1))
                total = column if total is None else total + column
            part[a, :, y * X:(y + 1) * X] = total

    def part_copy(side):
        return pltpu.make_async_remote_copy(
            src_ref=part.at[2 - 2 * side], dst_ref=part_in.at[side], send_sem=pt_send.at[side],
            recv_sem=pt_recv.at[side], device_id=(up if side == 0 else down, r), device_id_type=MESH)

    input_part(2)
    part_copy(0).start()
    input_part(0)
    part_copy(1).start()

    def z_copy(d):
        peer = lax.rem(zz + d, 8)
        return pltpu.make_async_remote_copy(
            src_ref=unit, dst_ref=z_in.at[zz], send_sem=z_send.at[d], recv_sem=z_recv.at[zz],
            device_id=z_dev(peer), device_id_type=MESH)

    @pl.when(m < HALF)
    def _():
        unit[...] = summed[mine + m]
        for d in range(1, 16):
            peer = lax.rem(m + d, 16)
            pltpu.make_async_remote_copy(
                src_ref=summed.at[0], dst_ref=xy_in.at[peer], send_sem=xy_send.at[0], recv_sem=xy_recv.at[peer],
                device_id=xy_dev(peer), device_id_type=MESH).wait_recv()
            unit[...] += xy_in[peer]
        z_in[zz] = unit[...]
        for d in range(1, 8):
            z_copy(d).start()

    input_part(1)

    def ag_copy(d):
        peer = lax.rem(m + d, 16)
        return pltpu.make_async_remote_copy(
            src_ref=wg_out.at[mine + m], dst_ref=wg_out.at[mine + m], send_sem=ag_send.at[d], recv_sem=ag_recv.at[m],
            device_id=xy_dev(peer), device_id_type=MESH)

    def forward(i):
        return pltpu.make_async_remote_copy(
            src_ref=wg_out.at[mine + i], dst_ref=wg_out.at[mine + i], send_sem=fwd_send.at[i], recv_sem=fwd_recv.at[i],
            device_id=(sibling, r), device_id_type=MESH)

    @pl.when(m < HALF)
    def _():
        for d in range(1, 8):
            peer = lax.rem(zz + d, 8)
            pltpu.make_async_remote_copy(
                src_ref=unit, dst_ref=z_in.at[peer], send_sem=z_send.at[d], recv_sem=z_recv.at[peer],
                device_id=z_dev(peer), device_id_type=MESH).wait_recv()
        total = z_in[0]
        for i in range(1, 8):
            total = total + z_in[i]
        total = total * (1.0 / math.sqrt(G * SPACE * VOX))
        blank = jnp.zeros((X - C, X), F32)
        for octet in range(3):
            trans[...] = jnp.concatenate([total[octet * C:(octet + 1) * C], blank], 0).T
            for side in range(2):
                joined = None
                for j in range(8):
                    rows = trans[pl.ds(side * 8 + j, 8, stride=C), :]
                    rows = rows if j == 0 else pltpu.roll(rows, j * C, 1)
                    joined = rows if joined is None else joined + rows
                wg_out[mine + m, octet * 8:(octet + 1) * 8, side * X:(side + 1) * X] = joined
        for d in range(1, 16):
            ag_copy(d).start()
        forward(m).start()

    for side in range(2):
        part_copy(side).wait_recv()
    low = jnp.where(s > 0, 1.0, 0.0).astype(F32)
    high = jnp.where(s < SPACE - 1, 1.0, 0.0).astype(F32)
    for y in range(Y):
        cols = slice(y * X, (y + 1) * X)
        lay[pl.ds(y, ROWS, stride=Y), :] = part[1, :, cols] + low * part_in[0, :, cols] + high * part_in[1, :, cols]
    fg_out[...] = lay[...].reshape(ROWS, Y, X).astype(BF16)

    for i in range(HALF):
        @pl.when(m != i)
        def _():
            pltpu.make_async_remote_copy(
                src_ref=wg_out.at[mine + i], dst_ref=wg_out.at[mine + i], send_sem=ag_send.at[0],
                recv_sem=ag_recv.at[i], device_id=xy_dev(i), device_id_type=MESH).wait_recv()
            forward(i).start()
    for i in range(HALF):
        pltpu.make_async_remote_copy(
            src_ref=wg_out.at[theirs + i], dst_ref=wg_out.at[theirs + i], send_sem=fwd_send.at[i],
            recv_sem=fwd_recv.at[i], device_id=(sibling, r), device_id_type=MESH).wait_recv()

    for d in range(1, ROT):
        rot_copy(d).wait_send()
    for side in range(2):
        halo_copy(side).wait_send()
        part_copy(side).wait_send()
    core_copy.wait_send()
    for i in range(HALF):
        forward(i).wait_send()

        @pl.when(m != i)
        def _():
            xy_copy(i).wait_send()

    @pl.when(m < HALF)
    def _():
        for d in range(1, 8):
            z_copy(d).wait_send()
        for d in range(1, 16):
            ag_copy(d).wait_send()


def local(features, cotangent, weight, relative, offset_perm):
    any_spec = pl.BlockSpec(memory_space=pl.ANY)
    smem = pl.BlockSpec(memory_space=pltpu.SMEM)
    vmem = pl.BlockSpec(memory_space=pltpu.VMEM)
    dma = pltpu.SemaphoreType.DMA
    fg, wg = pl.pallas_call(
        kernel,
        out_shape=(
            jax.ShapeDtypeStruct((ROWS, Y, X), BF16),
            jax.ShapeDtypeStruct((2 * HALF, G, C * C), F32),
        ),
        in_specs=[smem, smem, any_spec, any_spec, any_spec],
        out_specs=(vmem, vmem),
        scratch_shapes=[
            pltpu.VMEM((2, ROWS, Y, X), BF16),
            pltpu.VMEM((TAPS, G, C * C), BF16),
            pltpu.VMEM((ROWS * Y, X), F32),
            pltpu.VMEM((G, C, VOX), BF16),
            pltpu.VMEM((3 * LOCAL, C, VOX), BF16),
            pltpu.VMEM((LOCAL, TAPS * C, VOX), BF16),
            pltpu.VMEM((LOCAL, G * C, VOX), BF16),
            pltpu.VMEM((TAPS * G, C * C), F32),
            pltpu.VMEM((TAPS * G * C, X), F32),
            pltpu.VMEM((TAPS * G, C, X), BF16),
            pltpu.VMEM((TAPS * ROWS, G * C), BF16),
            pltpu.VMEM((LOCAL, TAPS, C, G * C), F32),
            pltpu.SMEM((LOCAL * G, 32), jnp.int32),
            pltpu.VMEM((2 * HALF, UNIT, X), F32),
            pltpu.VMEM((HALF, UNIT, X), F32),
            pltpu.VMEM((16, UNIT, X), F32),
            pltpu.VMEM((8, UNIT, X), F32),
            pltpu.VMEM((UNIT, X), F32),
            pltpu.VMEM((X, X), F32),
            pltpu.VMEM((9 * ROWS, VOX), F32),
            pltpu.VMEM((3, ROWS, VOX), F32),
            pltpu.VMEM((2, ROWS, VOX), F32),
            dma((3,)), dma((8,)), dma((8,)), dma((2,)), dma((2,)), dma, dma,
            dma((16,)), dma((16,)), dma((8,)), dma((8,)), dma((16,)), dma((16,)), dma((16,)), dma((16,)),
            dma((2,)), dma((2,)),
        ],
        compiler_params=pltpu.CompilerParams(
            collective_id=0, has_side_effects=True, vmem_limit_bytes=48 * 1024 * 1024
        ),
    )(
        relative, offset_perm,
        cotangent.reshape(ROWS, Y, X), features.reshape(ROWS, Y, X), weight,
    )
    return fg.reshape(features.shape), wg[:TAPS]


def solution(mesh):
    field = P("rot", None, "space", None, None)
    return jax.shard_map(
        local,
        mesh=mesh,
        in_specs=(field, field, P(), P(), P()),
        out_specs=(field, P()),
        check_vma=False,
    )
```

```python
import functools
import math

import jax
import jax.numpy as jnp
from jax import lax
from jax.experimental import pallas as pl
from jax.experimental.pallas import tpu as pltpu
from jax.sharding import PartitionSpec as P

MESH = pl.DeviceIdType.MESH
F32 = jnp.float32
BF16 = jnp.bfloat16
G, C, TAPS, Y, X = 24, 16, 27, 8, 128
ROT, SPACE = 8, 32
LOCAL = G // ROT
ROWS = LOCAL * C
VOX = Y * X
HALF = 14
UNIT = 48


def lane_iota(rows):
    return lax.broadcasted_iota(jnp.int32, (rows, X), 1)


def kernel(rel_in, perm_in, cot_in, feat_in, w_in, fg_out, wg_out,
           rel, perm, stage, fg_stage, wgv, win, lay, cot, feats, f27, pc, w32, w16, wsrc32, wsrc, wmat, quad, table,
           give, keep, core_in, xy_in, z_in, unit, trans, fgm, part, part_in,
           in_sem, rot_send, rot_recv, halo_send, halo_recv, core_send, core_recv,
           xy_send, xy_recv, z_send, z_recv, ag_send, ag_recv, fwd_send, fwd_recv,
           pt_send, pt_recv, out_sem):
    s = lax.axis_index("space")
    r = lax.axis_index("rot")
    core = lax.rem(s, 2)
    yy = lax.rem(s // 2, 4)
    z_hi = s // 8
    xx = lax.rem(r, 4)
    z_lo = r // 4
    m = yy * 4 + xx
    zz = z_hi * 2 + z_lo
    up, down = lax.rem(s + 1, SPACE), lax.rem(s + SPACE - 1, SPACE)
    sibling = s + 1 - 2 * core

    def xy_dev(i):
        return ((z_hi * 4 + i // 4) * 2 + core, z_lo * 4 + lax.rem(i, 4))

    def z_dev(i):
        return (((i // 2) * 4 + yy) * 2 + core, lax.rem(i, 2) * 4 + xx)

    cot_copy = pltpu.make_async_copy(cot_in, stage.at[0], in_sem.at[0])
    feat_copy = pltpu.make_async_copy(feat_in, stage.at[1], in_sem.at[1])
    w_copy = pltpu.make_async_copy(w_in, win, in_sem.at[2])
    cot_copy.start()
    feat_copy.start()
    rel_copy = pltpu.make_async_copy(rel_in, rel, in_sem.at[3])
    perm_copy = pltpu.make_async_copy(perm_in, perm, in_sem.at[4])
    rel_copy.start()
    perm_copy.start()
    w_copy.start()
    barrier = pltpu.get_barrier_semaphore()
    for d in range(1, ROT):
        pl.semaphore_signal(barrier, inc=1, device_id=(s, lax.rem(r + d, ROT)), device_id_type=MESH)
        pl.semaphore_signal(barrier, inc=1, device_id=z_dev(lax.rem(zz + d, 8)), device_id_type=MESH)
    for d in range(1, 16):
        pl.semaphore_signal(barrier, inc=1, device_id=xy_dev(lax.rem(m + d, 16)), device_id_type=MESH)
    for other in (up, down):
        pl.semaphore_signal(barrier, inc=1, device_id=(other, r), device_id_type=MESH)

    def flatten_plane(index, dst, row):
        lay[...] = stage[index].astype(F32).reshape(ROWS * Y, X)
        for y in range(Y):
            column = lay[pl.ds(y, ROWS, stride=Y), :].astype(BF16)
            dst[pl.ds(row, LOCAL), :, y * X:(y + 1) * X] = column.reshape(LOCAL, C, X)

    own = r * LOCAL
    cot_copy.wait()
    flatten_plane(0, cot, own)
    feat_copy.wait()
    flatten_plane(1, feats, LOCAL)
    pl.semaphore_wait(barrier, 31)

    def rot_copy(d):
        peer = lax.rem(z_lo + d // 4, 2) * 4 + lax.rem(xx + d % 4, 4)
        return pltpu.make_async_remote_copy(
            src_ref=cot.at[pl.ds(own, LOCAL)], dst_ref=cot.at[pl.ds(own, LOCAL)],
            send_sem=rot_send, recv_sem=rot_recv, device_id=(s, peer), device_id_type=MESH)

    def whole(buffer, count, sent, got):
        some = buffer.at[pl.ds(0, count)]
        return pltpu.make_async_remote_copy(
            src_ref=some, dst_ref=some, send_sem=sent, recv_sem=got, device_id=(up, r), device_id_type=MESH)

    rot_all = whole(cot, G - LOCAL, rot_send, rot_recv)
    halo_all = whole(feats, 2 * LOCAL, halo_send, halo_recv)
    part_all = whole(part_in, 2, pt_send, pt_recv)

    def halo_copy(side):
        return pltpu.make_async_remote_copy(
            src_ref=feats.at[pl.ds(LOCAL, LOCAL)], dst_ref=feats.at[pl.ds(2 * LOCAL * side, LOCAL)],
            send_sem=halo_send, recv_sem=halo_recv,
            device_id=(up if side == 0 else down, r), device_id_type=MESH)

    for d in (6, 5, 7, 2, 4, 1, 3):
        rot_copy(d).start()
    for side in range(2):
        halo_copy(side).start()

    rel_copy.wait()
    perm_copy.wait()
    same = rel[0, 0]

    def fill_table(k, carry):
        for g in range(LOCAL):
            h = rel[rel[r * LOCAL + g, same], rel[k, same]]
            turned_back = rel[h, same]
            table[g * G + k, 28] = h
            for q in range(TAPS):
                table[g * G + k, q] = perm[turned_back, q]
            table[g * G + k, TAPS] = 0
        return carry

    lax.fori_loop(0, G, fill_table, 0)

    w_copy.wait()

    def widen(q, carry):
        w32[pl.ds(pl.multiple_of(q * G, 8), G), :] = win[q].astype(F32)
        return carry

    lax.fori_loop(0, TAPS, widen, 0)
    w32[TAPS * G:, :] = jnp.zeros((8, C * C), F32)
    w16[...] = w32[...].astype(BF16)
    row_id = lax.broadcasted_iota(jnp.int32, (C * C, 2 * X), 0)
    col_id = lax.broadcasted_iota(jnp.int32, (C * C, 2 * X), 1)
    same_co = row_id // C == lax.rem(col_id, C)
    row_ci = lax.rem(row_id, C) - col_id // X

    def spread(step, carry):
        hot = jnp.where(jnp.logical_and(same_co, row_ci == 2 * step), 1.0, 0.0).astype(BF16)
        picked = jnp.dot(w16[...], hot, preferred_element_type=F32)
        for side in range(2):
            wsrc32[pl.ds(2 * step + side, TAPS * G, stride=C), :] = picked[:TAPS * G, side * X:(side + 1) * X]
        return carry

    lax.fori_loop(0, C // 2, spread, 0)

    def narrow(step, carry):
        rows = pl.ds(pl.multiple_of(step * G * C, 16), G * C)
        wsrc[pl.ds(step * G, G)] = wsrc32[rows, :].astype(BF16).reshape(G, C, X)
        return carry

    lax.fori_loop(0, TAPS, narrow, 0)
    group16 = lane_iota(C) // C

    halo_all.wait_recv()
    lane48 = lane_iota(ROWS)

    def fill_shifts(a, carry):
        inside = jnp.logical_and(jnp.logical_or(a != 0, s != 0), jnp.logical_or(a != 2, s != SPACE - 1))
        keep = jnp.where(inside, 1.0, 0.0).astype(F32)
        blank = jnp.zeros((C, X), BF16)
        for y in range(Y):
            plane = feats[pl.ds(a * LOCAL, LOCAL), :, y * X:(y + 1) * X].astype(F32).reshape(ROWS, X) * keep
            for c in range(3):
                if c == 0:
                    moved = jnp.where(lane48 == 0, 0.0, pltpu.roll(plane, 1, 1))
                elif c == 2:
                    moved = jnp.where(lane48 == X - 1, 0.0, pltpu.roll(plane, X - 1, 1))
                else:
                    moved = plane
                moved = moved.astype(BF16)
                for b in range(3):
                    target = y - (b - 1)
                    at = pl.multiple_of((a * 9 + b * 3 + c) * C, 16)
                    for g in range(LOCAL):
                        if 0 <= target < Y:
                            f27[g, pl.ds(at, C), target * X:(target + 1) * X] = moved[g * C:(g + 1) * C]
                        if (b == 2 and y == Y - 1) or (b == 0 and y == 0):
                            f27[g, pl.ds(at, C), y * X:(y + 1) * X] = blank
        return carry

    lax.fori_loop(0, 3, fill_shifts, 0)

    rot_all.wait_recv()

    def reorder(k, carry):
        for g in range(LOCAL):
            pc[g, pl.ds(pl.multiple_of(k * C, 16), C), :] = cot[table[g * G + k, 28]]
        return carry

    lax.fori_loop(0, G, reorder, 0)

    def pair_sums(g, carry):
        product = lax.dot_general(f27[g], pc[g], (((1,), (1,)), ((), ())), preferred_element_type=F32)
        for octet in range(3):
            quad[g, octet] = product[:, octet * X:(octet + 1) * X].reshape(TAPS, C, X)
        return carry

    lax.fori_loop(0, LOCAL, pair_sums, 0)

    def relabel(q):
        octets = []
        for octet in range(3):
            total = None
            for g in range(LOCAL):
                merged = None
                for j in range(8):
                    block = quad[g, octet, table[g * G + octet * 8 + j, q]]
                    merged = block if merged is None else jnp.where(group16 == j, block, merged)
                total = merged if total is None else total + merged
            octets.append(total)
        return octets

    mine = core * HALF
    theirs = HALF - mine

    def owner(step):
        row, column = 3 - step // 4, 3 - lax.rem(step, 4)
        dx = column + jnp.where(column == 3, -1, jnp.where(column == 2, 1, 0))
        dy = row + jnp.where(row == 3, -1, jnp.where(row == 2, 1, 0))
        return lax.rem(yy + dy, 4) * 4 + lax.rem(xx + dx, 4)

    def xy_copy(step):
        return pltpu.make_async_remote_copy(
            src_ref=keep.at[step], dst_ref=xy_in.at[m], send_sem=xy_send, recv_sem=xy_recv,
            device_id=xy_dev(owner(step)), device_id_type=MESH)

    def core_copy(chunk):
        return pltpu.make_async_remote_copy(
            src_ref=give.at[pl.ds(chunk * 4, 4)], dst_ref=core_in.at[pl.ds(chunk * 4, 4)],
            send_sem=core_send, recv_sem=core_recv.at[chunk],
            device_id=(sibling, r), device_id_type=MESH)

    def chunk_sums(chunk, first, dst):
        for step in range(chunk * 4, chunk * 4 + 4):
            octets = relabel(first + jnp.minimum(owner(step), HALF - 1))
            for octet in range(3):
                dst[step, octet * C:(octet + 1) * C, :] = octets[octet]

    def give_chunk(chunk):
        chunk_sums(chunk, theirs, give)
        core_copy(chunk).start()

    def keep_chunk(chunk):
        chunk_sums(chunk, mine, keep)
        core_copy(chunk).wait_recv()
        for step in range(chunk * 4, chunk * 4 + 4):
            keep[step] += core_in[step]
            if step < 15:
                @pl.when(owner(step) < HALF)
                def _():
                    xy_copy(step).start()

    give_chunk(0)
    give_chunk(1)
    keep_chunk(0)
    give_chunk(2)
    keep_chunk(1)
    give_chunk(3)
    keep_chunk(2)
    keep_chunk(3)

    def fill_filter(o, carry):
        for octet in range(3):
            turned = [perm[octet * 8 + j, o] * G for j in range(8)]
            for g in range(LOCAL):
                merged = None
                for j in range(8):
                    block = wsrc[turned[j] + rel[octet * 8 + j, r * LOCAL + g]]
                    merged = block if merged is None else jnp.where(group16 == j, block, merged)
                wmat[o, g * C:(g + 1) * C, octet * X:(octet + 1) * X] = merged
        return carry

    lax.fori_loop(0, TAPS, fill_filter, 0)

    def input_part(a):
        def product(n, carry):
            cols = pl.ds(pl.multiple_of(n * 256, 256), 256)
            fgm[:, cols] = jnp.dot(
                wmat[a * 9:(a + 1) * 9].reshape(9 * ROWS, G * C), cot[:, :, cols].reshape(G * C, 256), preferred_element_type=F32)
            return carry

        lax.fori_loop(0, VOX // 256, product, 0)
        for y in range(Y):
            total = None
            for c in range(3):
                column = None
                for b in range(3):
                    source = y - (b - 1)
                    if 0 <= source < Y:
                        term = fgm[(b * 3 + c) * ROWS:(b * 3 + c + 1) * ROWS, source * X:(source + 1) * X]
                        column = term if column is None else column + term
                if c == 0:
                    column = jnp.where(lane48 == X - 1, 0.0, pltpu.roll(column, X - 1, 1))
                elif c == 2:
                    column = jnp.where(lane48 == 0, 0.0, pltpu.roll(column, 1, 1))
                total = column if total is None else total + column
            part[a, :, y * X:(y + 1) * X] = total

    def part_copy(side):
        return pltpu.make_async_remote_copy(
            src_ref=part.at[2 - 2 * side], dst_ref=part_in.at[side], send_sem=pt_send,
            recv_sem=pt_recv, device_id=(up if side == 0 else down, r), device_id_type=MESH)

    def z_copy(d):
        peer = lax.rem(zz + d, 8)
        return pltpu.make_async_remote_copy(
            src_ref=unit, dst_ref=z_in.at[zz], send_sem=z_send, recv_sem=z_recv,
            device_id=z_dev(peer), device_id_type=MESH)

    @pl.when(m < HALF)
    def _():
        unit[...] = keep[15]
        whole(xy_in, 15, xy_send, xy_recv).wait_recv()
        for d in range(1, 16):
            unit[...] += xy_in[lax.rem(m + d, 16)]
        z_in[zz] = unit[...]
        for d in (4, 3, 5, 2, 6, 1, 7):
            z_copy(d).start()

    input_part(2)
    part_copy(0).start()
    input_part(0)
    part_copy(1).start()
    input_part(1)

    def ag_copy(d):
        return pltpu.make_async_remote_copy(
            src_ref=wgv.at[m], dst_ref=wgv.at[m], send_sem=ag_send, recv_sem=ag_recv.at[m],
            device_id=xy_dev(lax.rem(yy + d // 4, 4) * 4 + lax.rem(xx + d % 4, 4)), device_id_type=MESH)

    def forward(i):
        return pltpu.make_async_remote_copy(
            src_ref=wgv.at[i], dst_ref=wg_out.at[mine + i], send_sem=fwd_send, recv_sem=fwd_recv,
            device_id=(sibling, r), device_id_type=MESH)

    def write(i):
        return pltpu.make_async_copy(wgv.at[i], wg_out.at[mine + i], out_sem)

    @pl.when(m < HALF)
    def _():
        whole(z_in, 7, z_send, z_recv).wait_recv()
        total = z_in[0]
        for i in range(1, 8):
            total = total + z_in[i]
        blank = jnp.zeros((X - C, X), F32)
        for octet in range(3):
            trans[...] = jnp.concatenate([total[octet * C:(octet + 1) * C], blank], 0).T
            for side in range(2):
                joined = None
                for j in range(8):
                    rows = trans[pl.ds(side * 8 + j, 8, stride=C), :]
                    rows = rows if j == 0 else pltpu.roll(rows, j * C, 1)
                    joined = rows if joined is None else joined + rows
                wgv[m, octet * 8:(octet + 1) * 8, side * X:(side + 1) * X] = joined
        for d in (10, 9, 11, 6, 14, 5, 7, 13, 15, 8, 2, 1, 3, 4, 12):
            ag_copy(d).start()
        forward(m).start()
        write(m).start()

    part_all.wait_recv()
    low = jnp.where(s > 0, 1.0, 0.0).astype(F32)
    high = jnp.where(s < SPACE - 1, 1.0, 0.0).astype(F32)
    for y in range(Y):
        cols = slice(y * X, (y + 1) * X)
        lay[pl.ds(y, ROWS, stride=Y), :] = part[1, :, cols] + low * part_in[0, :, cols] + high * part_in[1, :, cols]
    fg_stage[...] = lay[...].reshape(ROWS, Y, X).astype(BF16)
    fg_copy = pltpu.make_async_copy(fg_stage, fg_out, in_sem.at[0])
    fg_copy.start()

    for i in range(HALF):
        @pl.when(m != i)
        def _():
            pltpu.make_async_remote_copy(
                src_ref=wgv.at[i], dst_ref=wgv.at[i], send_sem=ag_send,
                recv_sem=ag_recv.at[i], device_id=xy_dev(i), device_id_type=MESH).wait_recv()
            forward(i).start()
            write(i).start()

    forward_all = whole(wgv, HALF, fwd_send, fwd_recv)
    forward_all.wait_recv()

    rot_all.wait_send()
    halo_all.wait_send()
    part_all.wait_send()
    whole(give, 16, core_send, core_recv.at[0]).wait_send()
    forward_all.wait_send()
    pltpu.make_async_copy(wgv.at[pl.ds(0, HALF)], wg_out.at[pl.ds(0, HALF)], out_sem).wait()
    fg_copy.wait()

    @pl.when(m < HALF)
    def _():
        whole(keep, HALF - 1, xy_send, xy_recv).wait_send()
        whole(z_in, 7, z_send, z_recv).wait_send()
        whole(xy_in, 15, ag_send, ag_recv.at[0]).wait_send()

    @pl.when(m >= HALF)
    def _():
        whole(keep, HALF, xy_send, xy_recv).wait_send()


def local(features, cotangent, weight, relative, offset_perm):
    any_spec = pl.BlockSpec(memory_space=pl.ANY)
    dma = pltpu.SemaphoreType.DMA
    fg, wg = pl.pallas_call(
        kernel,
        out_shape=(
            jax.ShapeDtypeStruct((ROWS, Y, X), BF16),
            jax.ShapeDtypeStruct((2 * HALF, G, C * C), F32),
        ),
        in_specs=[any_spec] * 5,
        out_specs=(any_spec, any_spec),
        scratch_shapes=[
            pltpu.SMEM((G, G), jnp.int32),
            pltpu.SMEM((G, TAPS), jnp.int32),
            pltpu.VMEM((2, ROWS, Y, X), BF16),
            pltpu.VMEM((ROWS, Y, X), BF16),
            pltpu.VMEM((16, G, C * C), F32),
            pltpu.VMEM((TAPS, G, C * C), BF16),
            pltpu.VMEM((ROWS * Y, X), F32),
            pltpu.VMEM((G, C, VOX), BF16),
            pltpu.VMEM((3 * LOCAL, C, VOX), BF16),
            pltpu.VMEM((LOCAL, TAPS * C, VOX), BF16),
            pltpu.VMEM((LOCAL, G * C, VOX), BF16),
            pltpu.VMEM((656, C * C), F32),
            pltpu.VMEM((656, C * C), BF16),
            pltpu.VMEM((TAPS * G * C, X), F32),
            pltpu.VMEM((TAPS * G, C, X), BF16),
            pltpu.VMEM((TAPS, ROWS, G * C), BF16),
            pltpu.VMEM((LOCAL, 3, TAPS, C, X), F32),
            pltpu.SMEM((LOCAL * G, 32), jnp.int32),
            pltpu.VMEM((16, UNIT, X), F32),
            pltpu.VMEM((16, UNIT, X), F32),
            pltpu.VMEM((16, UNIT, X), F32),
            pltpu.VMEM((16, UNIT, X), F32),
            pltpu.VMEM((8, UNIT, X), F32),
            pltpu.VMEM((UNIT, X), F32),
            pltpu.VMEM((X, X), F32),
            pltpu.VMEM((9 * ROWS, VOX), F32),
            pltpu.VMEM((3, ROWS, VOX), F32),
            pltpu.VMEM((2, ROWS, VOX), F32),
            dma((5,)), dma, dma, dma, dma, dma, dma((4,)),
            dma, dma, dma, dma, dma, dma((16,)), dma, dma, dma, dma, dma,
        ],
        compiler_params=pltpu.CompilerParams(
            collective_id=0, has_side_effects=True, vmem_limit_bytes=63 * 1024 * 1024
        ),
    )(
        relative, offset_perm,
        cotangent.reshape(ROWS, Y, X), features.reshape(ROWS, Y, X), weight,
    )
    return fg.reshape(features.shape), wg[:TAPS] * (1.0 / math.sqrt(G * SPACE * VOX))


def solution(mesh):
    field = P("rot", None, "space", None, None)
    return jax.shard_map(
        local,
        mesh=mesh,
        in_specs=(field, field, P(), P(), P()),
        out_specs=(field, P()),
        check_vma=False,
    )
```

```python
import functools
import math

import jax
import jax.numpy as jnp
from jax import lax
from jax.experimental import pallas as pl
from jax.experimental.pallas import tpu as pltpu
from jax.sharding import PartitionSpec as P

MESH = pl.DeviceIdType.MESH
F32 = jnp.float32
BF16 = jnp.bfloat16
G, C, TAPS, Y, X = 24, 16, 27, 8, 128
ROT, SPACE = 8, 32
LOCAL = G // ROT
ROWS = LOCAL * C
VOX = Y * X
HALF = 14
UNIT = 48


def lane_iota(rows):
    return lax.broadcasted_iota(jnp.int32, (rows, X), 1)


def kernel(rel_in, perm_in, cot_in, feat_in, w_in, fg_out, wg_out,
           rel, perm, stage, win, lay, cot, feats, f27, pc, w32, w16, wsrc, wmat, quad, table,
           give, keep, core_in, xy_in, z_in, unit, trans, fgm, part, part_in,
           in_sem, rot_send, rot_recv, halo_send, halo_recv, core_send, core_recv,
           xy_send, xy_recv, z_send, z_recv, ag_send, ag_recv, fwd_send, fwd_recv,
           pt_send, pt_recv):
    s = lax.axis_index("space")
    r = lax.axis_index("rot")
    core = lax.rem(s, 2)
    yy = lax.rem(s // 2, 4)
    z_hi = s // 8
    xx = lax.rem(r, 4)
    z_lo = r // 4
    m = lax.rem(yy * 4 + xx + 8, 16)
    zz = z_hi * 2 + z_lo
    up, down = lax.rem(s + 1, SPACE), lax.rem(s + SPACE - 1, SPACE)
    sibling = s + 1 - 2 * core

    def xy_dev(i):
        return ((z_hi * 4 + lax.rem(i // 4 + 2, 4)) * 2 + core, z_lo * 4 + lax.rem(i, 4))

    def z_dev(i):
        return (((i // 2) * 4 + yy) * 2 + core, lax.rem(i, 2) * 4 + xx)

    cot_copy = pltpu.make_async_copy(cot_in, stage.at[0], in_sem.at[0])
    feat_copy = pltpu.make_async_copy(feat_in, stage.at[1], in_sem.at[1])
    w_copy = pltpu.make_async_copy(w_in, win, in_sem.at[2])
    cot_copy.start()
    feat_copy.start()
    rel_copy = pltpu.make_async_copy(rel_in, rel, in_sem.at[3])
    perm_copy = pltpu.make_async_copy(perm_in, perm, in_sem.at[4])
    rel_copy.start()
    perm_copy.start()
    w_copy.start()
    barrier = pltpu.get_barrier_semaphore()
    for d in range(1, ROT):
        pl.semaphore_signal(barrier, inc=1, device_id=(s, lax.rem(r + d, ROT)), device_id_type=MESH)
        pl.semaphore_signal(barrier, inc=1, device_id=z_dev(lax.rem(zz + d, 8)), device_id_type=MESH)
    for d in range(1, 16):
        pl.semaphore_signal(barrier, inc=1, device_id=xy_dev(lax.rem(m + d, 16)), device_id_type=MESH)
    for other in (up, down):
        pl.semaphore_signal(barrier, inc=1, device_id=(other, r), device_id_type=MESH)

    def flatten_plane(index, dst, row):
        lay[...] = stage[index].astype(F32).reshape(ROWS * Y, X)
        for y in range(Y):
            column = lay[pl.ds(y, ROWS, stride=Y), :].astype(BF16)
            dst[pl.ds(row, LOCAL), :, y * X:(y + 1) * X] = column.reshape(LOCAL, C, X)

    own = r * LOCAL
    cot_copy.wait()
    flatten_plane(0, cot, own)
    feat_copy.wait()
    flatten_plane(1, feats, LOCAL)
    pl.semaphore_wait(barrier, 31)

    def rot_copy(d):
        peer = lax.rem(z_lo + d // 4, 2) * 4 + lax.rem(xx + d % 4, 4)
        return pltpu.make_async_remote_copy(
            src_ref=cot.at[pl.ds(own, LOCAL)], dst_ref=cot.at[pl.ds(own, LOCAL)],
            send_sem=rot_send, recv_sem=rot_recv, device_id=(s, peer), device_id_type=MESH)

    def whole(buffer, count, sent, got):
        some = buffer.at[pl.ds(0, count)]
        return pltpu.make_async_remote_copy(
            src_ref=some, dst_ref=some, send_sem=sent, recv_sem=got, device_id=(up, r), device_id_type=MESH)

    rot_all = whole(cot, G - LOCAL, rot_send, rot_recv)

    def halo_copy(side):
        return pltpu.make_async_remote_copy(
            src_ref=feats.at[pl.ds(LOCAL, LOCAL)], dst_ref=feats.at[pl.ds(2 * LOCAL * side, LOCAL)],
            send_sem=halo_send, recv_sem=halo_recv,
            device_id=(up if side == 0 else down, r), device_id_type=MESH)

    def each_side(act):
        @pl.when(s < SPACE - 1)
        def _():
            act(0)

        @pl.when(s > 0)
        def _():
            act(1)

    def both_sides(buffer, size, sent, got, act):
        inside = jnp.logical_and(s > 0, s < SPACE - 1)

        @pl.when(inside)
        def _():
            act(whole(buffer, 2 * size, sent, got))

        @pl.when(jnp.logical_not(inside))
        def _():
            act(whole(buffer, size, sent, got))

    @pl.when(s == 0)
    def _():
        feats[0:LOCAL] = jnp.zeros((LOCAL, C, VOX), BF16)
        part_in[0] = jnp.zeros((ROWS, VOX), F32)

    @pl.when(s == SPACE - 1)
    def _():
        feats[2 * LOCAL:] = jnp.zeros((LOCAL, C, VOX), BF16)
        part_in[1] = jnp.zeros((ROWS, VOX), F32)

    each_side(lambda side: halo_copy(side).start())
    for d in (6, 5, 7, 2, 4, 1, 3):
        rot_copy(d).start()

    rel_copy.wait()
    perm_copy.wait()
    same = rel[0, 0]

    def fill_table(k, carry):
        for g in range(LOCAL):
            h = rel[rel[r * LOCAL + g, same], rel[k, same]]
            turned_back = rel[h, same]
            table[g * G + k, 28] = h
            for q in range(HALF):
                turned = perm[turned_back, q]
                table[g * G + k, q] = turned
                table[g * G + k, TAPS - 1 - q] = TAPS - 1 - turned
            table[g * G + k, TAPS] = 0
        return carry

    lax.fori_loop(0, G, fill_table, 0)

    w_copy.wait()

    def widen(q, carry):
        w32[pl.ds(pl.multiple_of(q * G, 8), G), :] = win[q].astype(F32)
        return carry

    lax.fori_loop(0, TAPS, widen, 0)
    w32[TAPS * G:, :] = jnp.zeros((8, C * C), F32)
    w16[...] = w32[...].astype(BF16)
    row_id = lax.broadcasted_iota(jnp.int32, (C * C, 2 * X), 0)
    col_id = lax.broadcasted_iota(jnp.int32, (C * C, 2 * X), 1)
    same_co = row_id // C == lax.rem(col_id, C)
    row_ci = lax.rem(row_id, C) - col_id // X

    rows = wsrc.reshape(TAPS * G * C, X)

    def spread(step, carry):
        hot = jnp.where(jnp.logical_and(same_co, row_ci == 2 * step), 1.0, 0.0).astype(BF16)
        picked = jnp.dot(w16[...], hot, preferred_element_type=F32)
        for side in range(2):
            rows[pl.ds(2 * step + side, TAPS * G, stride=C), :] = picked[:TAPS * G, side * X:(side + 1) * X]
        return carry

    lax.fori_loop(0, C // 2, spread, 0)

    group16 = lane_iota(C) // C

    def fill_filter(o, carry):
        for octet in range(3):
            turned = [perm[octet * 8 + j, o] * G for j in range(8)]
            for g in range(LOCAL):
                merged, facing = None, None
                for j in range(8):
                    k = rel[octet * 8 + j, r * LOCAL + g]
                    block = wsrc[turned[j] + k]
                    merged = block if merged is None else jnp.where(group16 == j, block, merged)
                    block = wsrc[(TAPS - 1) * G - turned[j] + k]
                    facing = block if facing is None else jnp.where(group16 == j, block, facing)
                wmat[o, g * C:(g + 1) * C, octet * X:(octet + 1) * X] = merged.astype(BF16)
                wmat[TAPS - 1 - o, g * C:(g + 1) * C, octet * X:(octet + 1) * X] = facing.astype(BF16)
        return carry

    lax.fori_loop(0, HALF, fill_filter, 0)

    both_sides(feats, LOCAL, halo_send, halo_recv, lambda copy: copy.wait_recv())
    lane48 = lane_iota(ROWS)

    def fill_shifts(a, carry):
        blank = jnp.zeros((C, X), BF16)
        for y in range(Y):
            plane = feats[pl.ds(a * LOCAL, LOCAL), :, y * X:(y + 1) * X].astype(F32).reshape(ROWS, X)
            for c in range(3):
                if c == 0:
                    moved = jnp.where(lane48 == 0, 0.0, pltpu.roll(plane, 1, 1))
                elif c == 2:
                    moved = jnp.where(lane48 == X - 1, 0.0, pltpu.roll(plane, X - 1, 1))
                else:
                    moved = plane
                moved = moved.astype(BF16)
                for b in range(3):
                    target = y - (b - 1)
                    at = pl.multiple_of((a * 9 + b * 3 + c) * C, 16)
                    for g in range(LOCAL):
                        if 0 <= target < Y:
                            f27[g, pl.ds(at, C), target * X:(target + 1) * X] = moved[g * C:(g + 1) * C]
                        if (b == 2 and y == Y - 1) or (b == 0 and y == 0):
                            f27[g, pl.ds(at, C), y * X:(y + 1) * X] = blank
        return carry

    lax.fori_loop(0, 3, fill_shifts, 0)

    rot_all.wait_recv()

    def reorder(k, carry):
        for g in range(LOCAL):
            pc[g, pl.ds(pl.multiple_of(k * C, 16), C), :] = cot[table[g * G + k, 28]]
        return carry

    lax.fori_loop(0, G, reorder, 0)

    def pair_sums(g, carry):
        product = lax.dot_general(f27[g], pc[g], (((1,), (1,)), ((), ())), preferred_element_type=F32)
        for octet in range(3):
            quad[g, octet] = product[:, octet * X:(octet + 1) * X].reshape(TAPS, C, X)
        return carry

    lax.fori_loop(0, LOCAL, pair_sums, 0)

    def relabel(q):
        octets = []
        for octet in range(3):
            total = None
            for g in range(LOCAL):
                merged = None
                for j in range(8):
                    block = quad[g, octet, table[g * G + octet * 8 + j, q]]
                    merged = block if merged is None else jnp.where(group16 == j, block, merged)
                total = merged if total is None else total + merged
            octets.append(total)
        return octets

    mine = core * HALF
    theirs = HALF - mine

    def owner(step):
        row, column = 3 - step // 4, 3 - lax.rem(step, 4)
        dx = column + jnp.where(column == 3, -1, jnp.where(column == 2, 1, 0))
        dy = row + jnp.where(row == 3, -1, jnp.where(row == 2, 1, 0))
        return lax.rem(yy + dy + 2, 4) * 4 + lax.rem(xx + dx, 4)

    def xy_copy(step):
        return pltpu.make_async_remote_copy(
            src_ref=keep.at[step], dst_ref=xy_in.at[m], send_sem=xy_send, recv_sem=xy_recv,
            device_id=xy_dev(owner(step)), device_id_type=MESH)

    def core_copy(chunk):
        return pltpu.make_async_remote_copy(
            src_ref=give.at[pl.ds(chunk * 4, 4)], dst_ref=core_in.at[pl.ds(chunk * 4, 4)],
            send_sem=core_send, recv_sem=core_recv.at[chunk],
            device_id=(sibling, r), device_id_type=MESH)

    def chunk_sums(chunk, first, dst):
        for step in range(chunk * 4, chunk * 4 + 4):
            octets = relabel(first + jnp.minimum(owner(step), HALF - 1))
            for octet in range(3):
                dst[step, octet * C:(octet + 1) * C, :] = octets[octet]

    def give_chunk(chunk):
        chunk_sums(chunk, theirs, give)
        core_copy(chunk).start()

    def keep_chunk(chunk):
        chunk_sums(chunk, mine, keep)
        core_copy(chunk).wait_recv()
        for step in range(chunk * 4, chunk * 4 + 4):
            keep[step] += core_in[step]
            if step < 15:
                @pl.when(owner(step) < HALF)
                def _():
                    xy_copy(step).start()

    give_chunk(0)
    give_chunk(1)
    keep_chunk(0)
    give_chunk(2)
    keep_chunk(1)
    give_chunk(3)
    keep_chunk(2)
    keep_chunk(3)

    def input_part(a):
        def product(n, carry):
            cols = pl.ds(pl.multiple_of(n * 256, 256), 256)
            fgm[:, cols] = jnp.dot(
                wmat[a * 9:(a + 1) * 9].reshape(9 * ROWS, G * C), cot[:, :, cols].reshape(G * C, 256), preferred_element_type=F32)
            return carry

        lax.fori_loop(0, VOX // 256, product, 0)
        for y in range(Y):
            total = None
            for c in range(3):
                column = None
                for b in range(3):
                    source = y - (b - 1)
                    if 0 <= source < Y:
                        term = fgm[(b * 3 + c) * ROWS:(b * 3 + c + 1) * ROWS, source * X:(source + 1) * X]
                        column = term if column is None else column + term
                if c == 0:
                    column = jnp.where(lane48 == X - 1, 0.0, pltpu.roll(column, X - 1, 1))
                elif c == 2:
                    column = jnp.where(lane48 == 0, 0.0, pltpu.roll(column, 1, 1))
                total = column if total is None else total + column
            part[a, :, y * X:(y + 1) * X] = total

    def part_copy(side):
        return pltpu.make_async_remote_copy(
            src_ref=part.at[2 - 2 * side], dst_ref=part_in.at[side], send_sem=pt_send,
            recv_sem=pt_recv, device_id=(up if side == 0 else down, r), device_id_type=MESH)

    def far(side):
        return lax.rem(s, 8) == (7 if side == 0 else 0)

    def send_part(side, when):
        @pl.when(jnp.logical_and(when, s < SPACE - 1 if side == 0 else s > 0))
        def _():
            part_copy(side).start()

    input_part(2)
    send_part(0, jnp.logical_not(far(0)))
    input_part(0)
    send_part(1, jnp.logical_not(far(1)))
    input_part(1)

    def z_copy(d):
        peer = lax.rem(zz + d, 8)
        return pltpu.make_async_remote_copy(
            src_ref=unit, dst_ref=z_in.at[zz], send_sem=z_send, recv_sem=z_recv,
            device_id=z_dev(peer), device_id_type=MESH)

    @pl.when(m < HALF)
    def _():
        unit[...] = keep[15]
        whole(xy_in, 15, xy_send, xy_recv).wait_recv()
        for d in range(1, 16):
            unit[...] += xy_in[lax.rem(m + d, 16)]
        z_in[zz] = unit[...]
        for d in (4, 3, 5, 2, 6, 1, 7):
            z_copy(d).start()


    def ag_copy(d):
        return pltpu.make_async_remote_copy(
            src_ref=wg_out.at[mine + m], dst_ref=wg_out.at[mine + m], send_sem=ag_send, recv_sem=ag_recv.at[m],
            device_id=xy_dev(lax.rem(yy + d // 4 + 2, 4) * 4 + lax.rem(xx + d % 4, 4)), device_id_type=MESH)

    def arrival(i):
        return pltpu.make_async_remote_copy(
            src_ref=wg_out.at[mine + i], dst_ref=wg_out.at[mine + i], send_sem=ag_send, recv_sem=ag_recv.at[i],
            device_id=(up, r), device_id_type=MESH)

    def forward(i):
        return pltpu.make_async_remote_copy(
            src_ref=wg_out.at[mine + i], dst_ref=wg_out.at[mine + i], send_sem=fwd_send, recv_sem=fwd_recv,
            device_id=(sibling, r), device_id_type=MESH)

    @pl.when(m < HALF)
    def _():
        whole(z_in, 7, z_send, z_recv).wait_recv()
        total = z_in[0]
        for i in range(1, 8):
            total = total + z_in[i]
        total = total * (1.0 / math.sqrt(G * SPACE * VOX))
        blank = jnp.zeros((X - C, X), F32)
        for octet in range(3):
            trans[...] = jnp.concatenate([total[octet * C:(octet + 1) * C], blank], 0).T
            for side in range(2):
                joined = None
                for j in range(8):
                    rows = trans[pl.ds(side * 8 + j, 8, stride=C), :]
                    rows = rows if j == 0 else pltpu.roll(rows, j * C, 1)
                    joined = rows if joined is None else joined + rows
                wg_out[mine + m, octet * 8:(octet + 1) * 8, side * X:(side + 1) * X] = joined
        for d in (10, 9, 11, 6, 14, 5, 7, 13, 15, 8, 2, 1, 3, 4, 12):
            ag_copy(d).start()
        forward(m).start()

    for side in range(2):
        send_part(side, far(side))

    both_sides(part_in, 1, pt_send, pt_recv, lambda copy: copy.wait_recv())
    for y in range(Y):
        cols = slice(y * X, (y + 1) * X)
        lay[pl.ds(y, ROWS, stride=Y), :] = part[1, :, cols] + part_in[0, :, cols] + part_in[1, :, cols]
    fg_out[...] = lay[...].reshape(ROWS, Y, X).astype(BF16)
    for i in range(HALF):
        @pl.when(m != i)
        def _():
            arrival(i).wait_recv()
            forward(i).start()

    forward_all = whole(wg_out, HALF, fwd_send, fwd_recv)
    forward_all.wait_recv()

    rot_all.wait_send()
    both_sides(feats, LOCAL, halo_send, halo_recv, lambda copy: copy.wait_send())
    both_sides(part_in, 1, pt_send, pt_recv, lambda copy: copy.wait_send())
    whole(give, 16, core_send, core_recv.at[0]).wait_send()
    forward_all.wait_send()

    @pl.when(m < HALF)
    def _():
        whole(keep, HALF - 1, xy_send, xy_recv).wait_send()
        whole(z_in, 7, z_send, z_recv).wait_send()
        whole(xy_in, 15, ag_send, ag_recv.at[0]).wait_send()

    @pl.when(m >= HALF)
    def _():
        whole(keep, HALF, xy_send, xy_recv).wait_send()


def finish(fg_in, wg_in, fg_out, wg_out, sem):
    pieces = [pltpu.make_async_copy(fg_in, fg_out, sem.at[0])]
    for i in range(3):
        some = pl.ds(9 * i, 9)
        pieces.append(pltpu.make_async_copy(wg_in.at[some], wg_out.at[some], sem.at[i + 1]))
    for copy in pieces:
        copy.start()
    for copy in pieces:
        copy.wait()


def local(features, cotangent, weight, relative, offset_perm):
    any_spec = pl.BlockSpec(memory_space=pl.ANY)
    vmem = pl.BlockSpec(memory_space=pltpu.VMEM)
    hbm = functools.partial(pltpu.with_memory_space_constraint, memory_space=pltpu.HBM)
    dma = pltpu.SemaphoreType.DMA
    fg, wg = pl.pallas_call(
        kernel,
        out_shape=(
            pltpu.VMEM((ROWS, Y, X), BF16),
            pltpu.VMEM((2 * HALF, G, C * C), F32),
        ),
        in_specs=[any_spec] * 5,
        out_specs=(vmem, vmem),
        scratch_shapes=[
            pltpu.SMEM((G, G), jnp.int32),
            pltpu.SMEM((G, TAPS), jnp.int32),
            pltpu.VMEM((2, ROWS, Y, X), BF16),
            pltpu.VMEM((TAPS, G, C * C), BF16),
            pltpu.VMEM((ROWS * Y, X), F32),
            pltpu.VMEM((G, C, VOX), BF16),
            pltpu.VMEM((3 * LOCAL, C, VOX), BF16),
            pltpu.VMEM((LOCAL, TAPS * C, VOX), BF16),
            pltpu.VMEM((LOCAL, G * C, VOX), BF16),
            pltpu.VMEM((656, C * C), F32),
            pltpu.VMEM((656, C * C), BF16),
            pltpu.VMEM((TAPS * G, C, X), F32),
            pltpu.VMEM((TAPS, ROWS, G * C), BF16),
            pltpu.VMEM((LOCAL, 3, TAPS, C, X), F32),
            pltpu.SMEM((LOCAL * G, 32), jnp.int32),
            pltpu.VMEM((16, UNIT, X), F32),
            pltpu.VMEM((16, UNIT, X), F32),
            pltpu.VMEM((16, UNIT, X), F32),
            pltpu.VMEM((16, UNIT, X), F32),
            pltpu.VMEM((8, UNIT, X), F32),
            pltpu.VMEM((UNIT, X), F32),
            pltpu.VMEM((X, X), F32),
            pltpu.VMEM((9 * ROWS, VOX), F32),
            pltpu.VMEM((3, ROWS, VOX), F32),
            pltpu.VMEM((2, ROWS, VOX), F32),
            dma((5,)), dma, dma, dma, dma, dma, dma((4,)),
            dma, dma, dma, dma, dma, dma((16,)), dma, dma, dma, dma,
        ],
        compiler_params=pltpu.CompilerParams(
            collective_id=0, has_side_effects=True, vmem_limit_bytes=48 * 1024 * 1024
        ),
    )(
        hbm(relative), hbm(offset_perm),
        hbm(cotangent.reshape(ROWS, Y, X)), hbm(features.reshape(ROWS, Y, X)), hbm(weight),
    )
    fg, wg = pl.pallas_call(
        finish,
        out_shape=(
            jax.ShapeDtypeStruct((ROWS, Y, X), BF16),
            jax.ShapeDtypeStruct((TAPS, G, C * C), F32),
        ),
        in_specs=[vmem] * 2,
        out_specs=(any_spec, any_spec),
        scratch_shapes=[dma((4,))],
        compiler_params=pltpu.CompilerParams(vmem_limit_bytes=8 * 1024 * 1024),
    )(fg, wg)
    return fg.reshape(features.shape), wg


def solution(mesh):
    field = P("rot", None, "space", None, None)
    return jax.shard_map(
        local,
        mesh=mesh,
        in_specs=(field, field, P(), P(), P()),
        out_specs=(field, P()),
        check_vma=False,
    )
```

```python
import functools
import math

import jax
import jax.numpy as jnp
from jax import lax
from jax.experimental import pallas as pl
from jax.experimental.pallas import tpu as pltpu
from jax.sharding import PartitionSpec as P

MESH = pl.DeviceIdType.MESH
F32 = jnp.float32
BF16 = jnp.bfloat16
G, C, TAPS, Y, X = 24, 16, 27, 8, 128
ROT, SPACE = 8, 32
LOCAL = G // ROT
ROWS = LOCAL * C
VOX = Y * X
HALF = 14
UNIT = 48


def lane_iota(rows):
    return lax.broadcasted_iota(jnp.int32, (rows, X), 1)


def turn(blocks, flips, swap, once, twice):
    def at(a, b, c):
        return blocks[a * 9 + b * 3 + c]

    digits = [(a, b, c) for a in range(3) for b in range(3) for c in range(3)]
    for axis in range(3):
        step = (9, 3, 1)[axis]
        blocks = [
            v if digits[o][axis] == 1 else jnp.where(flips[axis], blocks[o + 2 * step * (1 - digits[o][axis])], v)
            for o, v in enumerate(blocks)
        ]
    blocks = [at(a, b, c) if a == b else jnp.where(swap, at(b, a, c), at(a, b, c)) for a, b, c in digits]
    return [
        at(a, b, c) if a == b == c else jnp.where(once, at(b, c, a), jnp.where(twice, at(c, a, b), at(a, b, c)))
        for a, b, c in digits
    ]


def kernel(rel_in, perm_in, cot_in, feat_in, w_in, fg_out, wg_out,
           rel, perm, stage, win, lay, cot_low, cot_high, feats, f27, pc, w32, w16, wsrc, wturn, wmat, quad, table, turns,
           sums, core_in, xy_in, z_in, unit, trans, fgm, part, part_in,
           in_sem, rot_send, rot_recv, halo_send, halo_recv, core_send, core_recv,
           xy_send, xy_recv, z_send, z_recv, ag_send, ag_recv, fwd_send, fwd_recv,
           pt_send, pt_recv):
    s = lax.axis_index("space")
    r = lax.axis_index("rot")
    core = lax.rem(s, 2)
    yy = lax.rem(s // 2, 4)
    z_hi = s // 8
    xx = lax.rem(r, 4)
    z_lo = r // 4
    m = lax.rem(yy * 4 + xx + 8, 16)
    zz = z_hi * 2 + z_lo
    up, down = lax.rem(s + 1, SPACE), lax.rem(s + SPACE - 1, SPACE)
    sibling = s + 1 - 2 * core

    def xy_dev(i):
        return ((z_hi * 4 + lax.rem(i // 4 + 2, 4)) * 2 + core, z_lo * 4 + lax.rem(i, 4))

    def z_dev(i):
        return (((i // 2) * 4 + yy) * 2 + core, lax.rem(i, 2) * 4 + xx)

    barrier = pltpu.get_barrier_semaphore()
    for d in (4, 3, 5, 2, 6, 1, 7):
        pl.semaphore_signal(barrier, inc=1, device_id=z_dev(lax.rem(zz + d, 8)), device_id_type=MESH)
    for d in (10, 9, 11, 6, 14, 5, 7, 13, 15, 8, 2, 1, 3, 4, 12):
        near = lax.rem(yy + d // 4 + 2, 4) * 4 + lax.rem(xx + d % 4, 4)
        pl.semaphore_signal(barrier, inc=1, device_id=xy_dev(near), device_id_type=MESH)
    for d in (6, 5, 7, 2, 4, 1, 3):
        peer = lax.rem(z_lo + d // 4, 2) * 4 + lax.rem(xx + d % 4, 4)
        pl.semaphore_signal(barrier, inc=1, device_id=(s, peer), device_id_type=MESH)
    for other in (up, down):
        pl.semaphore_signal(barrier, inc=1, device_id=(other, r), device_id_type=MESH)
    cot_copy = pltpu.make_async_copy(cot_in, stage.at[0], in_sem.at[0])
    feat_copy = pltpu.make_async_copy(feat_in, stage.at[1], in_sem.at[1])
    w_copy = pltpu.make_async_copy(w_in, win, in_sem.at[2])
    cot_copy.start()
    feat_copy.start()
    rel_copy = pltpu.make_async_copy(rel_in, rel, in_sem.at[3])
    perm_copy = pltpu.make_async_copy(perm_in, perm, in_sem.at[4])
    rel_copy.start()
    perm_copy.start()
    w_copy.start()
    cot = (cot_low, cot_high)

    def flatten_plane(index, place):
        lay[...] = stage[index].astype(F32).reshape(ROWS * Y, X)
        for y in range(Y):
            column = lay[pl.ds(y, ROWS, stride=Y), :].astype(BF16)
            place(y, column.reshape(LOCAL, C, X))

    own = r * LOCAL
    cot_copy.wait()

    def place_cot(y, column):
        at = y % 4 * X
        cot[y // 4][pl.ds(own, LOCAL), :, at:at + X] = column

    flatten_plane(0, place_cot)
    feat_copy.wait()

    def place_feats(y, column):
        feats[LOCAL:2 * LOCAL, :, y * X:(y + 1) * X] = column

    flatten_plane(1, place_feats)
    pl.semaphore_wait(barrier, 31)

    def rot_copy(d, half):
        peer = lax.rem(z_lo + d // 4, 2) * 4 + lax.rem(xx + d % 4, 4)
        block = cot[half].at[pl.ds(own, LOCAL)]
        return pltpu.make_async_remote_copy(
            src_ref=block, dst_ref=block, send_sem=rot_send, recv_sem=rot_recv.at[half],
            device_id=(s, peer), device_id_type=MESH)

    def whole(buffer, count, sent, got):
        some = buffer.at[pl.ds(0, count)]
        return pltpu.make_async_remote_copy(
            src_ref=some, dst_ref=some, send_sem=sent, recv_sem=got, device_id=(up, r), device_id_type=MESH)

    rot_all = [whole(cot[half], G - LOCAL, rot_send, rot_recv.at[half]) for half in range(2)]

    def halo_copy(side):
        return pltpu.make_async_remote_copy(
            src_ref=feats.at[pl.ds(LOCAL, LOCAL)], dst_ref=feats.at[pl.ds(2 * LOCAL * side, LOCAL)],
            send_sem=halo_send, recv_sem=halo_recv,
            device_id=(up if side == 0 else down, r), device_id_type=MESH)

    def each_side(act):
        @pl.when(s < SPACE - 1)
        def _():
            act(0)

        @pl.when(s > 0)
        def _():
            act(1)

    def both_sides(buffer, size, sent, got, act):
        inside = jnp.logical_and(s > 0, s < SPACE - 1)

        @pl.when(inside)
        def _():
            act(whole(buffer, 2 * size, sent, got))

        @pl.when(jnp.logical_not(inside))
        def _():
            act(whole(buffer, size, sent, got))

    @pl.when(s == 0)
    def _():
        feats[0:LOCAL] = jnp.zeros((LOCAL, C, VOX), BF16)
        part_in[0] = jnp.zeros((ROWS, VOX), F32)

    @pl.when(s == SPACE - 1)
    def _():
        feats[2 * LOCAL:] = jnp.zeros((LOCAL, C, VOX), BF16)
        part_in[1] = jnp.zeros((ROWS, VOX), F32)

    each_side(lambda side: halo_copy(side).start())
    for half in range(2):
        for d in (6, 5, 7, 2, 4, 1, 3):
            rot_copy(d, half).start()

    rel_copy.wait()
    perm_copy.wait()
    same = rel[0, 0]

    group8 = lane_iota(8) // C
    basis = (22, 16, 14)

    def keep_turn(slot, images):
        sizes = [jnp.abs(v) for v in images]
        once, twice = sizes[0] == 1, sizes[1] == 1
        none = jnp.logical_not(jnp.logical_or(once, twice))
        swap = jnp.logical_or(
            jnp.logical_and(none, sizes[1] == 9),
            jnp.logical_or(jnp.logical_and(once, sizes[2] == 9), jnp.logical_and(twice, sizes[0] == 9)))
        lowest = [jnp.minimum(jnp.minimum(jnp.where(sizes[0] == n, images[0], n), jnp.where(sizes[1] == n, images[1], n)),
                              jnp.where(sizes[2] == n, images[2], n)) < 0 for n in (9, 3, 1)]
        for i, mask in enumerate((*lowest, swap, once, twice)):
            turns[slot, i] = jnp.where(mask, 1, 0)

    def turn_of(slot):
        f0, f1, f2, swap, once, twice = [turns[slot, i] != 0 for i in range(6)]
        return (f0, f1, f2), swap, once, twice

    def fill_turns(slot, carry):
        g, octet = slot // 3, lax.rem(slot, 3)
        base = rel[r * LOCAL + g, same]
        images = [jnp.zeros((8, X), jnp.int32) for _ in basis]
        for j in range(8):
            k = octet * 8 + j
            h = rel[base, rel[k, same]]
            back = rel[h, same]
            table[g * G + k] = h
            images = [jnp.where(group8 == j, perm[back, o] - 13, v) for v, o in zip(images, basis)]
        keep_turn(slot, images)
        return carry

    lax.fori_loop(0, LOCAL * 3, fill_turns, 0)

    def fill_own_turns(octet, carry):
        images = [jnp.zeros((8, X), jnp.int32) for _ in basis]
        for j in range(8):
            images = [jnp.where(group8 == j, perm[octet * 8 + j, o] - 13, v) for v, o in zip(images, basis)]
        keep_turn(LOCAL * 3 + octet, images)
        return carry

    lax.fori_loop(0, 3, fill_own_turns, 0)

    w_copy.wait()

    def widen(q, carry):
        w32[pl.ds(pl.multiple_of(q * G, 8), G), :] = win[q].astype(F32)
        return carry

    lax.fori_loop(0, TAPS, widen, 0)
    w32[TAPS * G:, :] = jnp.zeros((8, C * C), F32)
    w16[...] = w32[...].astype(BF16)
    row_id = lax.broadcasted_iota(jnp.int32, (C * C, 2 * X), 0)
    col_id = lax.broadcasted_iota(jnp.int32, (C * C, 2 * X), 1)
    same_co = row_id // C == lax.rem(col_id, C)
    row_ci = lax.rem(row_id, C) - col_id // X

    rows = wsrc.reshape(TAPS * G * C, X)

    def spread(step, carry):
        hot = jnp.where(jnp.logical_and(same_co, row_ci == 2 * step), 1.0, 0.0).astype(BF16)
        picked = jnp.dot(w16[...], hot, preferred_element_type=F32)
        for side in range(2):
            rows[pl.ds(2 * step + side, TAPS * G, stride=C), :] = picked[:TAPS * G, side * X:(side + 1) * X]
        return carry

    lax.fori_loop(0, C // 2, spread, 0)


    def fill_filter(step, carry):
        g, octet = step // 3, lax.rem(step, 3)
        labels = [rel[octet * 8 + j, r * LOCAL + g] for j in range(8)]
        turned = turn_of(LOCAL * 3 + octet)
        lanes = pl.ds(pl.multiple_of(octet * X, X), X)
        for part_of in range(2):
            blocks = []
            for q in range(TAPS):
                merged = None
                for j in range(8):
                    block = wsrc[q, labels[j], 8 * part_of:8 * part_of + 8]
                    merged = block if merged is None else jnp.where(group8 == j, block, merged)
                blocks.append(merged)
            at = pl.ds(pl.multiple_of(g * C + 8 * part_of, 8), 8)
            for o, block in enumerate(turn(blocks, *turned)):
                wturn[o, at, lanes] = block
        return carry

    lax.fori_loop(0, LOCAL * 3, fill_filter, 0)

    both_sides(feats, LOCAL, halo_send, halo_recv, lambda copy: copy.wait_recv())
    lane48 = lane_iota(ROWS)

    def fill_shifts(a, carry):
        blank = jnp.zeros((C, X), BF16)
        for y in range(Y):
            plane = feats[pl.ds(a * LOCAL, LOCAL), :, y * X:(y + 1) * X].astype(F32).reshape(ROWS, X)
            for c in range(3):
                if c == 0:
                    moved = jnp.where(lane48 == 0, 0.0, pltpu.roll(plane, 1, 1))
                elif c == 2:
                    moved = jnp.where(lane48 == X - 1, 0.0, pltpu.roll(plane, X - 1, 1))
                else:
                    moved = plane
                moved = moved.astype(BF16)
                for b in range(3):
                    target = y - (b - 1)
                    at = pl.multiple_of((a * 9 + b * 3 + c) * C, 16)
                    for g in range(LOCAL):
                        if 0 <= target < Y:
                            f27[g, pl.ds(at, C), target * X:(target + 1) * X] = moved[g * C:(g + 1) * C]
                        if (b == 2 and y == Y - 1) or (b == 0 and y == 0):
                            f27[g, pl.ds(at, C), y * X:(y + 1) * X] = blank
        return carry

    lax.fori_loop(0, 3, fill_shifts, 0)

    for half in range(2):
        voxels = slice(half * VOX // 2, (half + 1) * VOX // 2)
        rot_all[half].wait_recv()

        def reorder(k, carry):
            for g in range(LOCAL):
                pc[g, pl.ds(pl.multiple_of(k * C, 16), C), voxels] = cot[half][table[g * G + k]]
            return carry

        lax.fori_loop(0, G, reorder, 0)

        def pair_sums(g, carry):
            product = lax.dot_general(
                f27[g, :, voxels], pc[g, :, voxels], (((1,), (1,)), ((), ())), preferred_element_type=F32)
            for octet in range(3):
                some = product[:, octet * X:(octet + 1) * X].reshape(TAPS, C, X)
                if half == 0:
                    quad[g, octet] = some
                else:
                    quad[g, octet] += some
            return carry

        lax.fori_loop(0, LOCAL, pair_sums, 0)

    def relabel(step, carry):
        octet, part_of = step // 2, lax.rem(step, 2)
        at = pl.ds(pl.multiple_of(octet * C + 8 * part_of, 8), 8)
        half_at = pl.ds(pl.multiple_of(8 * part_of, 8), 8)
        for g in range(LOCAL):
            turned = turn([quad[g, octet, o, half_at] for o in range(TAPS)], *turn_of(g * 3 + octet))
            for q in range(TAPS):
                if g == 0:
                    sums[q // HALF, q % HALF, at] = turned[q]
                else:
                    sums[q // HALF, q % HALF, at] += turned[q]
        return carry

    sums[1, HALF - 1] = jnp.zeros((UNIT, X), F32)
    for i in range(HALF, 16):
        for half in range(2):
            sums[half, i] = jnp.zeros((UNIT, X), F32)
    lax.fori_loop(0, 6, relabel, 0)

    mine = core * HALF

    def row_of(chunk):
        dy = (2, 3, 1, 0)[chunk]
        return lax.rem(yy + dy + 2, 4)

    def owner(step):
        row, column = 3 - step // 4, 3 - step % 4
        return row_of(step // 4) * 4 + lax.rem(xx + (2, 3, 1, 0)[step % 4], 4)

    def xy_copy(step):
        return pltpu.make_async_remote_copy(
            src_ref=sums.at[core, owner(step)], dst_ref=xy_in.at[m], send_sem=xy_send, recv_sem=xy_recv,
            device_id=xy_dev(owner(step)), device_id_type=MESH)

    def core_copy(chunk):
        return pltpu.make_async_remote_copy(
            src_ref=sums.at[1 - core, pl.ds(row_of(chunk) * 4, 4)], dst_ref=core_in.at[pl.ds(row_of(chunk) * 4, 4)],
            send_sem=core_send, recv_sem=core_recv.at[chunk],
            device_id=(sibling, r), device_id_type=MESH)

    for chunk in range(4):
        core_copy(chunk).start()
    for chunk in range(4):
        core_copy(chunk).wait_recv()
        for step in range(chunk * 4, chunk * 4 + 4):
            i = owner(step)
            sums[core, i] += core_in[i]
            if step < 15:
                @pl.when(i < HALF)
                def _():
                    xy_copy(step).start()

    def input_part(a):
        wmat[...] = wturn[pl.ds(a * 9, 9)].reshape(9 * ROWS, G * C).astype(BF16)

        for half in range(2):
            def product(n, carry):
                cols = pl.ds(pl.multiple_of(n * 256, 256), 256)
                fgm[half, :, cols] = jnp.dot(
                    wmat[...], cot[half][:, :, cols].reshape(G * C, 256), preferred_element_type=F32)
                return carry

            lax.fori_loop(0, 2, product, 0)
        for y in range(Y):
            total = None
            for c in range(3):
                column = None
                for b in range(3):
                    source = y - (b - 1)
                    if 0 <= source < Y:
                        at = source % 4 * X
                        term = fgm[source // 4, (b * 3 + c) * ROWS:(b * 3 + c + 1) * ROWS, at:at + X]
                        column = term if column is None else column + term
                if c == 0:
                    column = jnp.where(lane48 == X - 1, 0.0, pltpu.roll(column, X - 1, 1))
                elif c == 2:
                    column = jnp.where(lane48 == 0, 0.0, pltpu.roll(column, 1, 1))
                total = column if total is None else total + column
            part[a, :, y * X:(y + 1) * X] = total

    def part_copy(side):
        return pltpu.make_async_remote_copy(
            src_ref=part.at[2 - 2 * side], dst_ref=part_in.at[side], send_sem=pt_send,
            recv_sem=pt_recv, device_id=(up if side == 0 else down, r), device_id_type=MESH)

    crosses_z = lax.rem(s, 8) == 7 * core

    def send_part(side):
        @pl.when(s < SPACE - 1 if side == 0 else s > 0)
        def _():
            part_copy(side).start()

    def send_out(when):
        for side in range(2):
            @pl.when(jnp.logical_and(core == 1 - side, when))
            def _():
                send_part(side)

    input_part(2 * core)
    send_out(crosses_z)
    input_part(2 - 2 * core)
    for side in range(2):
        @pl.when(core == side)
        def _():
            send_part(side)

    input_part(1)

    def z_copy(d):
        peer = lax.rem(zz + d, 8)
        return pltpu.make_async_remote_copy(
            src_ref=unit, dst_ref=z_in.at[zz], send_sem=z_send, recv_sem=z_recv,
            device_id=z_dev(peer), device_id_type=MESH)

    @pl.when(m < HALF)
    def _():
        unit[...] = sums[core, m]
        whole(xy_in, 15, xy_send, xy_recv).wait_recv()
        for d in range(1, 16):
            unit[...] += xy_in[lax.rem(m + d, 16)]
        z_in[zz] = unit[...]
        for d in (4, 3, 5, 2, 6, 1, 7):
            z_copy(d).start()


    send_out(jnp.logical_not(crosses_z))

    def ag_copy(d):
        return pltpu.make_async_remote_copy(
            src_ref=wg_out.at[mine + m], dst_ref=wg_out.at[mine + m], send_sem=ag_send, recv_sem=ag_recv.at[m],
            device_id=xy_dev(lax.rem(yy + d // 4 + 2, 4) * 4 + lax.rem(xx + d % 4, 4)), device_id_type=MESH)

    def arrival(i):
        return pltpu.make_async_remote_copy(
            src_ref=wg_out.at[mine + i], dst_ref=wg_out.at[mine + i], send_sem=ag_send, recv_sem=ag_recv.at[i],
            device_id=(up, r), device_id_type=MESH)

    def forward(i):
        return pltpu.make_async_remote_copy(
            src_ref=wg_out.at[mine + i], dst_ref=wg_out.at[mine + i], send_sem=fwd_send, recv_sem=fwd_recv,
            device_id=(sibling, r), device_id_type=MESH)

    @pl.when(m < HALF)
    def _():
        whole(z_in, 7, z_send, z_recv).wait_recv()
        total = z_in[0]
        for i in range(1, 8):
            total = total + z_in[i]
        total = total * (1.0 / math.sqrt(G * SPACE * VOX))
        blank = jnp.zeros((X - C, X), F32)
        for octet in range(3):
            trans[...] = jnp.concatenate([total[octet * C:(octet + 1) * C], blank], 0).T
            for side in range(2):
                joined = None
                for j in range(8):
                    rows = trans[pl.ds(side * 8 + j, 8, stride=C), :]
                    rows = rows if j == 0 else pltpu.roll(rows, j * C, 1)
                    joined = rows if joined is None else joined + rows
                wg_out[mine + m, octet * 8:(octet + 1) * 8, side * X:(side + 1) * X] = joined
        for d in (10, 9, 11, 6, 14, 5, 7, 13, 15, 8, 2, 1, 3, 4, 12):
            ag_copy(d).start()
        forward(m).start()

    both_sides(part_in, 1, pt_send, pt_recv, lambda copy: copy.wait_recv())
    for y in range(Y):
        cols = slice(y * X, (y + 1) * X)
        lay[pl.ds(y, ROWS, stride=Y), :] = part[1, :, cols] + part_in[0, :, cols] + part_in[1, :, cols]
    fg_out[...] = lay[...].reshape(ROWS, Y, X).astype(BF16)
    for i in range(HALF):
        @pl.when(m != i)
        def _():
            arrival(i).wait_recv()
            forward(i).start()

    forward_all = whole(wg_out, HALF, fwd_send, fwd_recv)
    forward_all.wait_recv()

    for half in range(2):
        rot_all[half].wait_send()
    both_sides(feats, LOCAL, halo_send, halo_recv, lambda copy: copy.wait_send())
    both_sides(part_in, 1, pt_send, pt_recv, lambda copy: copy.wait_send())
    whole(core_in, 16, core_send, core_recv.at[0]).wait_send()
    forward_all.wait_send()

    @pl.when(m < HALF)
    def _():
        whole(core_in, HALF - 1, xy_send, xy_recv).wait_send()
        whole(z_in, 7, z_send, z_recv).wait_send()
        whole(xy_in, 15, ag_send, ag_recv.at[0]).wait_send()

    @pl.when(m >= HALF)
    def _():
        whole(core_in, HALF, xy_send, xy_recv).wait_send()


def finish(fg_in, wg_in, fg_out, wg_out, sem):
    pieces = [pltpu.make_async_copy(fg_in, fg_out, sem.at[0])]
    for i in range(3):
        some = pl.ds(9 * i, 9)
        pieces.append(pltpu.make_async_copy(wg_in.at[some], wg_out.at[some], sem.at[i + 1]))
    for copy in pieces:
        copy.start()
    for copy in pieces:
        copy.wait()


def local(features, cotangent, weight, relative, offset_perm):
    any_spec = pl.BlockSpec(memory_space=pl.ANY)
    vmem = pl.BlockSpec(memory_space=pltpu.VMEM)
    hbm = functools.partial(pltpu.with_memory_space_constraint, memory_space=pltpu.HBM)
    dma = pltpu.SemaphoreType.DMA
    fg, wg = pl.pallas_call(
        kernel,
        out_shape=(
            pltpu.VMEM((ROWS, Y, X), BF16),
            pltpu.VMEM((2 * HALF, G, C * C), F32),
        ),
        in_specs=[any_spec] * 5,
        out_specs=(vmem, vmem),
        scratch_shapes=[
            pltpu.SMEM((G, G), jnp.int32),
            pltpu.SMEM((G, TAPS), jnp.int32),
            pltpu.VMEM((2, ROWS, Y, X), BF16),
            pltpu.VMEM((TAPS, G, C * C), BF16),
            pltpu.VMEM((ROWS * Y, X), F32),
            pltpu.VMEM((G, C, VOX // 2), BF16),
            pltpu.VMEM((G, C, VOX // 2), BF16),
            pltpu.VMEM((3 * LOCAL, C, VOX), BF16),
            pltpu.VMEM((LOCAL, TAPS * C, VOX), BF16),
            pltpu.VMEM((LOCAL, G * C, VOX), BF16),
            pltpu.VMEM((656, C * C), F32),
            pltpu.VMEM((656, C * C), BF16),
            pltpu.VMEM((TAPS, G, C, X), F32),
            pltpu.VMEM((TAPS, ROWS, G * C), F32),
            pltpu.VMEM((9 * ROWS, G * C), BF16),
            pltpu.VMEM((LOCAL, 3, TAPS, C, X), F32),
            pltpu.SMEM((LOCAL * G,), jnp.int32),
            pltpu.VMEM((12, 6, 8, X), jnp.int32),
            pltpu.VMEM((2, 16, UNIT, X), F32),
            pltpu.VMEM((16, UNIT, X), F32),
            pltpu.VMEM((16, UNIT, X), F32),
            pltpu.VMEM((8, UNIT, X), F32),
            pltpu.VMEM((UNIT, X), F32),
            pltpu.VMEM((X, X), F32),
            pltpu.VMEM((2, 9 * ROWS, VOX // 2), F32),
            pltpu.VMEM((3, ROWS, VOX), F32),
            pltpu.VMEM((2, ROWS, VOX), F32),
            dma((5,)), dma, dma((2,)), dma, dma, dma, dma((4,)),
            dma, dma, dma, dma, dma, dma((16,)), dma, dma, dma, dma,
        ],
        compiler_params=pltpu.CompilerParams(
            collective_id=0, has_side_effects=True, vmem_limit_bytes=48 * 1024 * 1024
        ),
    )(
        hbm(relative), hbm(offset_perm),
        hbm(cotangent.reshape(ROWS, Y, X)), hbm(features.reshape(ROWS, Y, X)), hbm(weight),
    )
    fg, wg = pl.pallas_call(
        finish,
        out_shape=(
            jax.ShapeDtypeStruct((ROWS, Y, X), BF16),
            jax.ShapeDtypeStruct((TAPS, G, C * C), F32),
        ),
        in_specs=[vmem] * 2,
        out_specs=(any_spec, any_spec),
        scratch_shapes=[dma((4,))],
        compiler_params=pltpu.CompilerParams(vmem_limit_bytes=8 * 1024 * 1024),
    )(fg, wg)
    return fg.reshape(features.shape), wg


def solution(mesh):
    field = P("rot", None, "space", None, None)
    return jax.shard_map(
        local,
        mesh=mesh,
        in_specs=(field, field, P(), P(), P()),
        out_specs=(field, P()),
        check_vma=False,
    )
```

```python
import functools
import math

import jax
import jax.numpy as jnp
from jax import lax
from jax.experimental import pallas as pl
from jax.experimental.pallas import tpu as pltpu
from jax.sharding import PartitionSpec as P

MESH = pl.DeviceIdType.MESH
F32 = jnp.float32
BF16 = jnp.bfloat16
G, C, TAPS, Y, X = 24, 16, 27, 8, 128
ROT, SPACE = 8, 32
LOCAL = G // ROT
ROWS = LOCAL * C
VOX = Y * X
PARTS = ((0, 4), (4, 8))
SHARES = (11, 16)
UNIT = 48


def lane_iota(rows):
    return lax.broadcasted_iota(jnp.int32, (rows, X), 1)


def turn(blocks, flips, swap, once, twice):
    def at(a, b, c):
        return blocks[a * 9 + b * 3 + c]

    digits = [(a, b, c) for a in range(3) for b in range(3) for c in range(3)]
    for axis in range(3):
        step = (9, 3, 1)[axis]
        blocks = [
            v if digits[o][axis] == 1 else jnp.where(flips[axis], blocks[o + 2 * step * (1 - digits[o][axis])], v)
            for o, v in enumerate(blocks)
        ]
    blocks = [at(a, b, c) if a == b else jnp.where(swap, at(b, a, c), at(a, b, c)) for a, b, c in digits]
    return [
        at(a, b, c) if a == b == c else jnp.where(once, at(b, c, a), jnp.where(twice, at(c, a, b), at(a, b, c)))
        for a, b, c in digits
    ]


def kernel(rel_in, perm_in, cot_in, feat_in, w_in, fg_out, wg_out,
           rel, perm, stage, win, lay, cot_0, cot_1, feats, f27, pc, w32, w16, wsrc, wturn, wmat, quad, table, turns,
           sums, core_in, xy_in, z_in, unit, trans, fgm, part, part_in, passing,
           in_sem, rot_send, rot_recv, across_recv, halo_send, halo_recv, core_send, core_recv,
           xy_send, xy_recv, z_send, z_recv, ag_send, ag_recv, fwd_send, fwd_recv,
           pt_send, pt_recv, pass_send, pass_recv):
    s = lax.axis_index("space")
    r = lax.axis_index("rot")
    core = lax.rem(s, 2)
    yy = lax.rem(s // 2, 4)
    z_hi = s // 8
    xx = lax.rem(r, 4)
    z_lo = r // 4
    m = lax.rem(yy * 4 + xx + 8, 16)
    zz = z_hi * 2 + z_lo
    up, down = lax.rem(s + 1, SPACE), lax.rem(s + SPACE - 1, SPACE)
    sibling = s + 1 - 2 * core

    def xy_dev(i):
        return ((z_hi * 4 + lax.rem(i // 4 + 2, 4)) * 2 + core, z_lo * 4 + lax.rem(i, 4))

    def z_dev(i):
        return (((i // 2) * 4 + yy) * 2 + core, lax.rem(i, 2) * 4 + xx)

    barrier = pltpu.get_barrier_semaphore()
    for d in (4, 3, 5, 2, 6, 1, 7):
        pl.semaphore_signal(barrier, inc=1, device_id=z_dev(lax.rem(zz + d, 8)), device_id_type=MESH)
    for d in (10, 9, 11, 6, 14, 5, 7, 13, 15, 8, 2, 1, 3, 4, 12):
        near = lax.rem(yy + d // 4 + 2, 4) * 4 + lax.rem(xx + d % 4, 4)
        pl.semaphore_signal(barrier, inc=1, device_id=xy_dev(near), device_id_type=MESH)
    for d in (6, 5, 7, 2, 4, 1, 3):
        peer = lax.rem(z_lo + d // 4, 2) * 4 + lax.rem(xx + d % 4, 4)
        pl.semaphore_signal(barrier, inc=1, device_id=(s, peer), device_id_type=MESH)
    for other in (up, down):
        pl.semaphore_signal(barrier, inc=1, device_id=(other, r), device_id_type=MESH)
    at_end = lax.rem(s, 8) == 7 * core

    @pl.when(at_end)
    def _():
        pl.semaphore_signal(barrier, inc=1, device_id=(s + 7 - 14 * core, r), device_id_type=MESH)

    cot_copy = pltpu.make_async_copy(cot_in, stage.at[0], in_sem.at[0])
    feat_copy = pltpu.make_async_copy(feat_in, stage.at[1], in_sem.at[1])
    w_copy = pltpu.make_async_copy(w_in, win, in_sem.at[2])
    cot_copy.start()
    feat_copy.start()
    rel_copy = pltpu.make_async_copy(rel_in, rel, in_sem.at[3])
    perm_copy = pltpu.make_async_copy(perm_in, perm, in_sem.at[4])
    rel_copy.start()
    perm_copy.start()
    w_copy.start()
    cot = (cot_0, cot_1)
    part_of_row = [n for n, (first, last) in enumerate(PARTS) for _ in range(first, last)]
    parts = range(len(PARTS))

    def flatten_plane(index, place):
        lay[...] = stage[index].astype(F32).reshape(ROWS * Y, X)
        for y in range(Y):
            column = lay[pl.ds(y, ROWS, stride=Y), :].astype(BF16)
            place(y, column.reshape(LOCAL, C, X))

    own = r * LOCAL
    cot_copy.wait()

    def place_cot(y, column):
        n = part_of_row[y]
        at = (y - PARTS[n][0]) * X
        cot[n][pl.ds(own, LOCAL), :, at:at + X] = column

    flatten_plane(0, place_cot)
    feat_copy.wait()

    def place_feats(y, column):
        feats[LOCAL:2 * LOCAL, :, y * X:(y + 1) * X] = column

    flatten_plane(1, place_feats)
    pl.semaphore_wait(barrier, jnp.where(at_end, 32, 31))

    across = lax.rem(r + 4, ROT)

    def across_copy(half):
        block = cot[half].at[pl.ds(own, LOCAL)]
        return pltpu.make_async_remote_copy(
            src_ref=block, dst_ref=block, send_sem=rot_send, recv_sem=across_recv.at[half],
            device_id=(s, across), device_id_type=MESH)

    def rot_copy(owner_of, d, half):
        block = cot[half].at[pl.ds(owner_of * LOCAL, LOCAL)]
        return pltpu.make_async_remote_copy(
            src_ref=block, dst_ref=block, send_sem=rot_send, recv_sem=rot_recv.at[half],
            device_id=(s, z_lo * 4 + lax.rem(xx + d, 4)), device_id_type=MESH)

    def whole(buffer, count, sent, got):
        some = buffer.at[pl.ds(0, count)]
        return pltpu.make_async_remote_copy(
            src_ref=some, dst_ref=some, send_sem=sent, recv_sem=got, device_id=(up, r), device_id_type=MESH)

    rot_sent = [whole(cot[half], G - LOCAL, rot_send, rot_recv.at[half]) for half in parts]
    rot_all = [whole(cot[half], G - 2 * LOCAL, rot_send, rot_recv.at[half]) for half in parts]

    def halo_copy(side):
        return pltpu.make_async_remote_copy(
            src_ref=feats.at[pl.ds(LOCAL, LOCAL)], dst_ref=feats.at[pl.ds(2 * LOCAL * side, LOCAL)],
            send_sem=halo_send, recv_sem=halo_recv,
            device_id=(up if side == 0 else down, r), device_id_type=MESH)

    def each_side(act):
        @pl.when(s < SPACE - 1)
        def _():
            act(0)

        @pl.when(s > 0)
        def _():
            act(1)

    def both_sides(buffer, size, sent, got, act):
        inside = jnp.logical_and(s > 0, s < SPACE - 1)

        @pl.when(inside)
        def _():
            act(whole(buffer, 2 * size, sent, got))

        @pl.when(jnp.logical_not(inside))
        def _():
            act(whole(buffer, size, sent, got))

    @pl.when(s == 0)
    def _():
        feats[0:LOCAL] = jnp.zeros((LOCAL, C, VOX), BF16)
        part_in[0] = jnp.zeros((ROWS, VOX), F32)

    @pl.when(s == SPACE - 1)
    def _():
        feats[2 * LOCAL:] = jnp.zeros((LOCAL, C, VOX), BF16)
        part_in[1] = jnp.zeros((ROWS, VOX), F32)

    each_side(lambda side: halo_copy(side).start())
    for half in parts:
        across_copy(half).start()
    for half in parts:
        for d in (2, 1, 3):
            rot_copy(r, d, half).start()

    rel_copy.wait()
    perm_copy.wait()
    same = rel[0, 0]

    group8 = lane_iota(8) // C
    basis = (22, 16, 14)

    def keep_turn(slot, images):
        sizes = [jnp.abs(v) for v in images]
        once, twice = sizes[0] == 1, sizes[1] == 1
        none = jnp.logical_not(jnp.logical_or(once, twice))
        swap = jnp.logical_or(
            jnp.logical_and(none, sizes[1] == 9),
            jnp.logical_or(jnp.logical_and(once, sizes[2] == 9), jnp.logical_and(twice, sizes[0] == 9)))
        lowest = [jnp.minimum(jnp.minimum(jnp.where(sizes[0] == n, images[0], n), jnp.where(sizes[1] == n, images[1], n)),
                              jnp.where(sizes[2] == n, images[2], n)) < 0 for n in (9, 3, 1)]
        for i, mask in enumerate((*lowest, swap, once, twice)):
            turns[slot, i] = jnp.where(mask, 1, 0)

    def turn_of(slot):
        f0, f1, f2, swap, once, twice = [turns[slot, i] != 0 for i in range(6)]
        return (f0, f1, f2), swap, once, twice

    def fill_turns(slot, carry):
        g, octet = slot // 3, lax.rem(slot, 3)
        base = rel[r * LOCAL + g, same]
        images = [jnp.zeros((8, X), jnp.int32) for _ in basis]
        for j in range(8):
            k = octet * 8 + j
            h = rel[base, rel[k, same]]
            back = rel[h, same]
            table[g * G + k] = h
            images = [jnp.where(group8 == j, perm[back, o] - 13, v) for v, o in zip(images, basis)]
        keep_turn(slot, images)
        return carry

    lax.fori_loop(0, LOCAL * 3, fill_turns, 0)

    def fill_own_turns(octet, carry):
        images = [jnp.zeros((8, X), jnp.int32) for _ in basis]
        for j in range(8):
            images = [jnp.where(group8 == j, perm[octet * 8 + j, o] - 13, v) for v, o in zip(images, basis)]
        keep_turn(LOCAL * 3 + octet, images)
        return carry

    lax.fori_loop(0, 3, fill_own_turns, 0)

    w_copy.wait()

    def widen(q, carry):
        w32[pl.ds(pl.multiple_of(q * G, 8), G), :] = win[q].astype(F32)
        return carry

    lax.fori_loop(0, TAPS, widen, 0)
    w32[TAPS * G:, :] = jnp.zeros((8, C * C), F32)
    w16[...] = w32[...].astype(BF16)
    row_id = lax.broadcasted_iota(jnp.int32, (C * C, 2 * X), 0)
    col_id = lax.broadcasted_iota(jnp.int32, (C * C, 2 * X), 1)
    same_co = row_id // C == lax.rem(col_id, C)
    row_ci = lax.rem(row_id, C) - col_id // X

    rows = wsrc.reshape(TAPS * G * C, X)

    def spread(step, carry):
        hot = jnp.where(jnp.logical_and(same_co, row_ci == 2 * step), 1.0, 0.0).astype(BF16)
        picked = jnp.dot(w16[...], hot, preferred_element_type=F32)
        for side in range(2):
            rows[pl.ds(2 * step + side, TAPS * G, stride=C), :] = picked[:TAPS * G, side * X:(side + 1) * X]
        return carry

    lax.fori_loop(0, C // 2, spread, 0)


    for half in parts:
        whole(cot[half], LOCAL, rot_send, across_recv.at[half]).wait_recv()
        for d in (2, 1, 3):
            rot_copy(across, d, half).start()

    def fill_filter(step, carry):
        g, octet = step // 3, lax.rem(step, 3)
        labels = [rel[octet * 8 + j, r * LOCAL + g] for j in range(8)]
        turned = turn_of(LOCAL * 3 + octet)
        lanes = pl.ds(pl.multiple_of(octet * X, X), X)
        for part_of in range(2):
            blocks = []
            for q in range(TAPS):
                merged = None
                for j in range(8):
                    block = wsrc[q, labels[j], 8 * part_of:8 * part_of + 8]
                    merged = block if merged is None else jnp.where(group8 == j, block, merged)
                blocks.append(merged)
            at = pl.ds(pl.multiple_of(g * C + 8 * part_of, 8), 8)
            for o, block in enumerate(turn(blocks, *turned)):
                wturn[o, at, lanes] = block
        return carry

    lax.fori_loop(0, LOCAL * 3, fill_filter, 0)

    both_sides(feats, LOCAL, halo_send, halo_recv, lambda copy: copy.wait_recv())
    lane48 = lane_iota(ROWS)

    def fill_shifts(a, carry):
        blank = jnp.zeros((C, X), BF16)
        for y in range(Y):
            plane = feats[pl.ds(a * LOCAL, LOCAL), :, y * X:(y + 1) * X].astype(F32).reshape(ROWS, X)
            for c in range(3):
                if c == 0:
                    moved = jnp.where(lane48 == 0, 0.0, pltpu.roll(plane, 1, 1))
                elif c == 2:
                    moved = jnp.where(lane48 == X - 1, 0.0, pltpu.roll(plane, X - 1, 1))
                else:
                    moved = plane
                moved = moved.astype(BF16)
                for b in range(3):
                    target = y - (b - 1)
                    at = pl.multiple_of((a * 9 + b * 3 + c) * C, 16)
                    for g in range(LOCAL):
                        if 0 <= target < Y:
                            f27[g, pl.ds(at, C), target * X:(target + 1) * X] = moved[g * C:(g + 1) * C]
                        if (b == 2 and y == Y - 1) or (b == 0 and y == 0):
                            f27[g, pl.ds(at, C), y * X:(y + 1) * X] = blank
        return carry

    lax.fori_loop(0, 3, fill_shifts, 0)

    for half in parts:
        voxels = slice(PARTS[half][0] * X, PARTS[half][1] * X)
        rot_all[half].wait_recv()

        def reorder(k, carry):
            for g in range(LOCAL):
                pc[g, pl.ds(pl.multiple_of(k * C, 16), C), voxels] = cot[half][table[g * G + k]]
            return carry

        lax.fori_loop(0, G, reorder, 0)

        def pair_sums(g, carry):
            product = lax.dot_general(
                f27[g, :, voxels], pc[g, :, voxels], (((1,), (1,)), ((), ())), preferred_element_type=F32)
            for octet in range(3):
                some = product[:, octet * X:(octet + 1) * X].reshape(TAPS, C, X)
                if half == 0:
                    quad[g, octet] = some
                else:
                    quad[g, octet] += some
            return carry

        lax.fori_loop(0, LOCAL, pair_sums, 0)

    def relabel(step, carry):
        octet, part_of = step // 2, lax.rem(step, 2)
        at = pl.ds(pl.multiple_of(octet * C + 8 * part_of, 8), 8)
        half_at = pl.ds(pl.multiple_of(8 * part_of, 8), 8)
        for g in range(LOCAL):
            turned = turn([quad[g, octet, o, half_at] for o in range(TAPS)], *turn_of(g * 3 + octet))
            for q in range(TAPS):
                if g == 0:
                    sums[int(q >= SHARES[0]), q - SHARES[0] * int(q >= SHARES[0]), at] = turned[q]
                else:
                    sums[int(q >= SHARES[0]), q - SHARES[0] * int(q >= SHARES[0]), at] += turned[q]
        return carry

    for i in range(SHARES[0], 16):
        sums[0, i] = jnp.zeros((UNIT, X), F32)
    lax.fori_loop(0, 6, relabel, 0)

    mine = core * SHARES[0]
    share = SHARES[0] + core * (SHARES[1] - SHARES[0])

    def by_core(act):
        for side in range(2):
            @pl.when(core == side)
            def _():
                act(SHARES[side])


    def row_of(chunk):
        dy = (2, 3, 1, 0)[chunk]
        return lax.rem(yy + dy + 2, 4)

    def owner(step):
        row, column = 3 - step // 4, 3 - step % 4
        return row_of(step // 4) * 4 + lax.rem(xx + (2, 3, 1, 0)[step % 4], 4)

    def xy_copy(step):
        return pltpu.make_async_remote_copy(
            src_ref=sums.at[core, owner(step)], dst_ref=xy_in.at[m], send_sem=xy_send, recv_sem=xy_recv,
            device_id=xy_dev(owner(step)), device_id_type=MESH)

    def core_copy(chunk):
        return pltpu.make_async_remote_copy(
            src_ref=sums.at[1 - core, pl.ds(row_of(chunk) * 4, 4)], dst_ref=core_in.at[pl.ds(row_of(chunk) * 4, 4)],
            send_sem=core_send, recv_sem=core_recv.at[chunk],
            device_id=(sibling, r), device_id_type=MESH)

    for chunk in range(4):
        core_copy(chunk).start()
    for chunk in range(4):
        core_copy(chunk).wait_recv()
        for step in range(chunk * 4, chunk * 4 + 4):
            i = owner(step)
            sums[core, i] += core_in[i]
            if step < 15:
                @pl.when(i < share)
                def _():
                    xy_copy(step).start()

    def input_part(a):
        wmat[...] = wturn[pl.ds(a * 9, 9)].reshape(9 * ROWS, G * C).astype(BF16)

        for n in parts:
            for at in range(0, (PARTS[n][1] - PARTS[n][0]) * X, 256):
                first = PARTS[n][0] * X + at
                fgm[:, first:first + 256] = jnp.dot(
                    wmat[...], cot[n][:, :, at:at + 256].reshape(G * C, 256), preferred_element_type=F32)
        for y in range(Y):
            total = None
            for c in range(3):
                column = None
                for b in range(3):
                    source = y - (b - 1)
                    if 0 <= source < Y:
                        term = fgm[(b * 3 + c) * ROWS:(b * 3 + c + 1) * ROWS, source * X:(source + 1) * X]
                        column = term if column is None else column + term
                if c == 0:
                    column = jnp.where(lane48 == X - 1, 0.0, pltpu.roll(column, X - 1, 1))
                elif c == 2:
                    column = jnp.where(lane48 == 0, 0.0, pltpu.roll(column, 1, 1))
                total = column if total is None else total + column
            part[a, :, y * X:(y + 1) * X] = total

    def part_copy(side):
        return pltpu.make_async_remote_copy(
            src_ref=part.at[2 - 2 * side], dst_ref=part_in.at[side], send_sem=pt_send,
            recv_sem=pt_recv, device_id=(up if side == 0 else down, r), device_id_type=MESH)

    crosses_z = at_end
    onward = s + 8 * (2 * core - 1)
    behind = s - 8 * (2 * core - 1)
    relays = jnp.logical_and(crosses_z, jnp.logical_and(behind >= 0, behind < SPACE))

    def along_z():
        return pltpu.make_async_remote_copy(
            src_ref=part.at[2 * core], dst_ref=passing, send_sem=pt_send, recv_sem=pass_recv,
            device_id=(onward, r), device_id_type=MESH)

    def along_y():
        return pltpu.make_async_remote_copy(
            src_ref=passing, dst_ref=part_in.at[1 - core], send_sem=pass_send, recv_sem=pt_recv,
            device_id=(s + 7 - 14 * core, r), device_id_type=MESH)

    def send_part(side, when):
        @pl.when(jnp.logical_and(s < SPACE - 1 if side == 0 else s > 0, when))
        def _():
            part_copy(side).start()

    input_part(2 * core)

    @pl.when(jnp.logical_and(crosses_z, jnp.logical_and(onward >= 0, onward < SPACE)))
    def _():
        along_z().start()

    input_part(2 - 2 * core)
    input_part(1)

    def z_copy(d):
        peer = lax.rem(zz + d, 8)
        return pltpu.make_async_remote_copy(
            src_ref=unit, dst_ref=z_in.at[zz], send_sem=z_send, recv_sem=z_recv,
            device_id=z_dev(peer), device_id_type=MESH)

    @pl.when(m < share)
    def _():
        unit[...] = sums[core, m]
        whole(xy_in, 15, xy_send, xy_recv).wait_recv()
        for d in range(1, 16):
            unit[...] += xy_in[lax.rem(m + d, 16)]
        z_in[zz] = unit[...]
        for d in (4, 3, 5, 2, 6, 1, 7):
            z_copy(d).start()


    for side in range(2):
        send_part(side, jnp.logical_not(jnp.logical_and(crosses_z, core == 1 - side)))

    @pl.when(relays)
    def _():
        along_z().wait_recv()
        along_y().start()

    def ag_copy(d):
        return pltpu.make_async_remote_copy(
            src_ref=wg_out.at[mine + m], dst_ref=wg_out.at[mine + m], send_sem=ag_send, recv_sem=ag_recv.at[m],
            device_id=xy_dev(lax.rem(yy + d // 4 + 2, 4) * 4 + lax.rem(xx + d % 4, 4)), device_id_type=MESH)

    def arrival(i):
        return pltpu.make_async_remote_copy(
            src_ref=wg_out.at[mine + i], dst_ref=wg_out.at[mine + i], send_sem=ag_send, recv_sem=ag_recv.at[i],
            device_id=(up, r), device_id_type=MESH)

    def forward(i):
        return pltpu.make_async_remote_copy(
            src_ref=wg_out.at[mine + i], dst_ref=wg_out.at[mine + i], send_sem=fwd_send, recv_sem=fwd_recv,
            device_id=(sibling, r), device_id_type=MESH)

    @pl.when(m < share)
    def _():
        whole(z_in, 7, z_send, z_recv).wait_recv()
        total = z_in[0]
        for i in range(1, 8):
            total = total + z_in[i]
        total = total * (1.0 / math.sqrt(G * SPACE * VOX))
        blank = jnp.zeros((X - C, X), F32)
        for octet in range(3):
            trans[...] = jnp.concatenate([total[octet * C:(octet + 1) * C], blank], 0).T
            for side in range(2):
                joined = None
                for j in range(8):
                    rows = trans[pl.ds(side * 8 + j, 8, stride=C), :]
                    rows = rows if j == 0 else pltpu.roll(rows, j * C, 1)
                    joined = rows if joined is None else joined + rows
                wg_out[mine + m, octet * 8:(octet + 1) * 8, side * X:(side + 1) * X] = joined
        for d in (10, 9, 11, 6, 14, 5, 7, 13, 15, 8, 2, 1, 3, 4, 12):
            ag_copy(d).start()
        forward(m).start()

    both_sides(part_in, 1, pt_send, pt_recv, lambda copy: copy.wait_recv())
    for y in range(Y):
        cols = slice(y * X, (y + 1) * X)
        lay[pl.ds(y, ROWS, stride=Y), :] = part[1, :, cols] + part_in[0, :, cols] + part_in[1, :, cols]
    fg_out[...] = lay[...].reshape(ROWS, Y, X).astype(BF16)
    for i in range(16):
        @pl.when(jnp.logical_and(m != i, i < share))
        def _():
            arrival(i).wait_recv()
            forward(i).start()

    by_core(lambda count: whole(wg_out, TAPS - count, fwd_send, fwd_recv).wait_recv())

    for half in parts:
        rot_sent[half].wait_send()
    both_sides(feats, LOCAL, halo_send, halo_recv, lambda copy: copy.wait_send())
    both_sides(part_in, 1, pt_send, pt_recv, lambda copy: copy.wait_send())
    whole(core_in, 16, core_send, core_recv.at[0]).wait_send()
    by_core(lambda count: whole(wg_out, count, fwd_send, fwd_recv).wait_send())

    @pl.when(relays)
    def _():
        along_y().wait_send()


    @pl.when(m < share)
    def _():
        by_core(lambda count: whole(core_in, count - 1, xy_send, xy_recv).wait_send())
        whole(z_in, 7, z_send, z_recv).wait_send()
        whole(xy_in, 15, ag_send, ag_recv.at[0]).wait_send()

    @pl.when(m >= share)
    def _():
        by_core(lambda count: whole(core_in, count, xy_send, xy_recv).wait_send())


def finish(fg_in, wg_in, fg_out, wg_out, sem):
    pieces = [pltpu.make_async_copy(fg_in, fg_out, sem.at[0])]
    for i in range(3):
        some = pl.ds(9 * i, 9)
        pieces.append(pltpu.make_async_copy(wg_in.at[some], wg_out.at[some], sem.at[i + 1]))
    for copy in pieces:
        copy.start()
    for copy in pieces:
        copy.wait()


def local(features, cotangent, weight, relative, offset_perm):
    any_spec = pl.BlockSpec(memory_space=pl.ANY)
    vmem = pl.BlockSpec(memory_space=pltpu.VMEM)
    hbm = functools.partial(pltpu.with_memory_space_constraint, memory_space=pltpu.HBM)
    dma = pltpu.SemaphoreType.DMA
    fg, wg = pl.pallas_call(
        kernel,
        out_shape=(
            pltpu.VMEM((ROWS, Y, X), BF16),
            pltpu.VMEM((TAPS, G, C * C), F32),
        ),
        in_specs=[any_spec] * 5,
        out_specs=(vmem, vmem),
        scratch_shapes=[
            pltpu.SMEM((G, G), jnp.int32),
            pltpu.SMEM((G, TAPS), jnp.int32),
            pltpu.VMEM((2, ROWS, Y, X), BF16),
            pltpu.VMEM((TAPS, G, C * C), BF16),
            pltpu.VMEM((ROWS * Y, X), F32),
            *[pltpu.VMEM((G, C, (last - first) * X), BF16) for first, last in PARTS],
            pltpu.VMEM((3 * LOCAL, C, VOX), BF16),
            pltpu.VMEM((LOCAL, TAPS * C, VOX), BF16),
            pltpu.VMEM((LOCAL, G * C, VOX), BF16),
            pltpu.VMEM((656, C * C), F32),
            pltpu.VMEM((656, C * C), BF16),
            pltpu.VMEM((TAPS, G, C, X), F32),
            pltpu.VMEM((TAPS, ROWS, G * C), F32),
            pltpu.VMEM((9 * ROWS, G * C), BF16),
            pltpu.VMEM((LOCAL, 3, TAPS, C, X), F32),
            pltpu.SMEM((LOCAL * G,), jnp.int32),
            pltpu.VMEM((12, 6, 8, X), jnp.int32),
            pltpu.VMEM((2, 16, UNIT, X), F32),
            pltpu.VMEM((16, UNIT, X), F32),
            pltpu.VMEM((16, UNIT, X), F32),
            pltpu.VMEM((8, UNIT, X), F32),
            pltpu.VMEM((UNIT, X), F32),
            pltpu.VMEM((X, X), F32),
            pltpu.VMEM((9 * ROWS, VOX), F32),
            pltpu.VMEM((3, ROWS, VOX), F32),
            pltpu.VMEM((2, ROWS, VOX), F32),
            pltpu.VMEM((ROWS, VOX), F32),
            dma((5,)), dma, dma((2,)), dma((2,)), dma, dma, dma, dma((4,)),
            dma, dma, dma, dma, dma, dma((16,)), dma, dma, dma, dma, dma, dma,
        ],
        compiler_params=pltpu.CompilerParams(
            collective_id=0, has_side_effects=True, vmem_limit_bytes=48 * 1024 * 1024
        ),
    )(
        hbm(relative), hbm(offset_perm),
        hbm(cotangent.reshape(ROWS, Y, X)), hbm(features.reshape(ROWS, Y, X)), hbm(weight),
    )
    fg, wg = pl.pallas_call(
        finish,
        out_shape=(
            jax.ShapeDtypeStruct((ROWS, Y, X), BF16),
            jax.ShapeDtypeStruct((TAPS, G, C * C), F32),
        ),
        in_specs=[vmem] * 2,
        out_specs=(any_spec, any_spec),
        scratch_shapes=[dma((4,))],
        compiler_params=pltpu.CompilerParams(vmem_limit_bytes=8 * 1024 * 1024),
    )(fg, wg)
    return fg.reshape(features.shape), wg


def solution(mesh):
    field = P("rot", None, "space", None, None)
    return jax.shard_map(
        local,
        mesh=mesh,
        in_specs=(field, field, P(), P(), P()),
        out_specs=(field, P()),
        check_vma=False,
    )
```

```python
import functools
import math

import jax
import jax.numpy as jnp
from jax import lax
from jax.experimental import pallas as pl
from jax.experimental.pallas import tpu as pltpu
from jax.sharding import PartitionSpec as P

MESH = pl.DeviceIdType.MESH
F32 = jnp.float32
BF16 = jnp.bfloat16
G, C, TAPS, Y, X = 24, 16, 27, 8, 128
ROT, SPACE = 8, 32
LOCAL = G // ROT
ROWS = LOCAL * C
VOX = Y * X
PARTS = ((0, 4), (4, 8))
SHARES = (11, 16)
CODED = 64
UNIT = 48


def lane_iota(rows):
    return lax.broadcasted_iota(jnp.int32, (rows, X), 1)


def turn(blocks, flips, swap, once, twice):
    def at(a, b, c):
        return blocks[a * 9 + b * 3 + c]

    digits = [(a, b, c) for a in range(3) for b in range(3) for c in range(3)]
    for axis in range(3):
        step = (9, 3, 1)[axis]
        blocks = [
            v if digits[o][axis] == 1 else jnp.where(flips[axis], blocks[o + 2 * step * (1 - digits[o][axis])], v)
            for o, v in enumerate(blocks)
        ]
    blocks = [at(a, b, c) if a == b else jnp.where(swap, at(b, a, c), at(a, b, c)) for a, b, c in digits]
    return [
        at(a, b, c) if a == b == c else jnp.where(once, at(b, c, a), jnp.where(twice, at(c, a, b), at(a, b, c)))
        for a, b, c in digits
    ]


def to_steps(sums):
    top = jnp.max(jnp.max(jnp.abs(sums), axis=0, keepdims=True), axis=1, keepdims=True)
    power = jnp.ceil(jnp.log2(jnp.maximum(jnp.broadcast_to(top, (8, X)), 2.0**-110)))
    steps = jnp.round(sums * jnp.concatenate([jnp.exp2(15.0 - power)] * (UNIT // 8), 0))
    steps = jnp.minimum(jnp.maximum(steps, -32767.0), 32767.0)
    return jnp.concatenate([steps, power, power], 0).astype(jnp.int32).astype(jnp.int16)


def from_steps(coded):
    wide = coded.astype(jnp.int32).astype(F32)
    return wide[:UNIT] * jnp.concatenate([jnp.exp2(wide[UNIT:UNIT + 8] - 15.0)] * (UNIT // 8), 0)


def kernel(rel_in, perm_in, cot_in, feat_in, w_in, fg_out, wg_out,
           rel, perm, stage, win, lay, cot_0, cot_1, feats, f27, pc, w32, w16, wsrc, wturn, wmat, quad, table, turns,
           sums, core_in, xy_in, xy_out, z_in, unit, trans, coded, fgm, part, part_in, passing,
           in_sem, rot_send, rot_recv, across_recv, halo_send, halo_recv, core_send, core_recv,
           xy_send, xy_recv, z_send, z_recv, ag_send, ag_recv, fwd_send, fwd_recv,
           pt_send, pt_recv, pass_send, pass_recv):
    s = lax.axis_index("space")
    r = lax.axis_index("rot")
    core = lax.rem(s, 2)
    yy = lax.rem(s // 2, 4)
    z_hi = s // 8
    xx = lax.rem(r, 4)
    z_lo = r // 4
    m = lax.rem(yy * 4 + xx + 8, 16)
    zz = z_hi * 2 + z_lo
    up, down = lax.rem(s + 1, SPACE), lax.rem(s + SPACE - 1, SPACE)
    sibling = s + 1 - 2 * core

    def xy_dev(i):
        return ((z_hi * 4 + lax.rem(i // 4 + 2, 4)) * 2 + core, z_lo * 4 + lax.rem(i, 4))

    def z_dev(i):
        return (((i // 2) * 4 + yy) * 2 + core, lax.rem(i, 2) * 4 + xx)

    barrier = pltpu.get_barrier_semaphore()
    for d in (4, 3, 5, 2, 6, 1, 7):
        pl.semaphore_signal(barrier, inc=1, device_id=z_dev(lax.rem(zz + d, 8)), device_id_type=MESH)
    for d in (10, 9, 11, 6, 14, 5, 7, 13, 15, 8, 2, 1, 3, 4, 12):
        near = lax.rem(yy + d // 4 + 2, 4) * 4 + lax.rem(xx + d % 4, 4)
        pl.semaphore_signal(barrier, inc=1, device_id=xy_dev(near), device_id_type=MESH)
    for d in (6, 5, 7, 2, 4, 1, 3):
        peer = lax.rem(z_lo + d // 4, 2) * 4 + lax.rem(xx + d % 4, 4)
        pl.semaphore_signal(barrier, inc=1, device_id=(s, peer), device_id_type=MESH)
    for other in (up, down):
        pl.semaphore_signal(barrier, inc=1, device_id=(other, r), device_id_type=MESH)
    at_end = lax.rem(s, 8) == 7 * core

    @pl.when(at_end)
    def _():
        pl.semaphore_signal(barrier, inc=1, device_id=(s + 7 - 14 * core, r), device_id_type=MESH)

    cot_copy = pltpu.make_async_copy(cot_in, stage.at[0], in_sem.at[0])
    feat_copy = pltpu.make_async_copy(feat_in, stage.at[1], in_sem.at[1])
    w_copy = pltpu.make_async_copy(w_in, win, in_sem.at[2])
    cot_copy.start()
    feat_copy.start()
    rel_copy = pltpu.make_async_copy(rel_in, rel, in_sem.at[3])
    perm_copy = pltpu.make_async_copy(perm_in, perm, in_sem.at[4])
    rel_copy.start()
    perm_copy.start()
    w_copy.start()
    cot = (cot_0, cot_1)
    part_of_row = [n for n, (first, last) in enumerate(PARTS) for _ in range(first, last)]
    parts = range(len(PARTS))

    def flatten_plane(index, place):
        lay[...] = stage[index].astype(F32).reshape(ROWS * Y, X)
        for y in range(Y):
            column = lay[pl.ds(y, ROWS, stride=Y), :].astype(BF16)
            place(y, column.reshape(LOCAL, C, X))

    own = r * LOCAL
    cot_copy.wait()

    def place_cot(y, column):
        n = part_of_row[y]
        at = (y - PARTS[n][0]) * X
        cot[n][pl.ds(own, LOCAL), :, at:at + X] = column

    flatten_plane(0, place_cot)
    feat_copy.wait()

    def place_feats(y, column):
        feats[LOCAL:2 * LOCAL, :, y * X:(y + 1) * X] = column

    flatten_plane(1, place_feats)
    pl.semaphore_wait(barrier, jnp.where(at_end, 32, 31))

    across = lax.rem(r + 4, ROT)

    def across_copy(half):
        block = cot[half].at[pl.ds(own, LOCAL)]
        return pltpu.make_async_remote_copy(
            src_ref=block, dst_ref=block, send_sem=rot_send, recv_sem=across_recv.at[half],
            device_id=(s, across), device_id_type=MESH)

    def rot_copy(owner_of, d, half):
        block = cot[half].at[pl.ds(owner_of * LOCAL, LOCAL)]
        return pltpu.make_async_remote_copy(
            src_ref=block, dst_ref=block, send_sem=rot_send, recv_sem=rot_recv.at[half],
            device_id=(s, z_lo * 4 + lax.rem(xx + d, 4)), device_id_type=MESH)

    def whole(buffer, count, sent, got):
        some = buffer.at[pl.ds(0, count)]
        return pltpu.make_async_remote_copy(
            src_ref=some, dst_ref=some, send_sem=sent, recv_sem=got, device_id=(up, r), device_id_type=MESH)

    rot_sent = [whole(cot[half], G - LOCAL, rot_send, rot_recv.at[half]) for half in parts]
    rot_all = [whole(cot[half], G - 2 * LOCAL, rot_send, rot_recv.at[half]) for half in parts]

    def halo_copy(side):
        return pltpu.make_async_remote_copy(
            src_ref=feats.at[pl.ds(LOCAL, LOCAL)], dst_ref=feats.at[pl.ds(2 * LOCAL * side, LOCAL)],
            send_sem=halo_send, recv_sem=halo_recv,
            device_id=(up if side == 0 else down, r), device_id_type=MESH)

    def each_side(act):
        @pl.when(s < SPACE - 1)
        def _():
            act(0)

        @pl.when(s > 0)
        def _():
            act(1)

    def both_sides(buffer, size, sent, got, act):
        inside = jnp.logical_and(s > 0, s < SPACE - 1)

        @pl.when(inside)
        def _():
            act(whole(buffer, 2 * size, sent, got))

        @pl.when(jnp.logical_not(inside))
        def _():
            act(whole(buffer, size, sent, got))

    @pl.when(s == 0)
    def _():
        feats[0:LOCAL] = jnp.zeros((LOCAL, C, VOX), BF16)
        part_in[0] = jnp.zeros((ROWS, VOX), F32)

    @pl.when(s == SPACE - 1)
    def _():
        feats[2 * LOCAL:] = jnp.zeros((LOCAL, C, VOX), BF16)
        part_in[1] = jnp.zeros((ROWS, VOX), F32)

    each_side(lambda side: halo_copy(side).start())
    for half in parts:
        across_copy(half).start()
    for half in parts:
        for d in (2, 1, 3):
            rot_copy(r, d, half).start()

    rel_copy.wait()
    perm_copy.wait()
    same = rel[0, 0]

    group8 = lane_iota(8) // C
    basis = (22, 16, 14)

    def keep_turn(slot, images):
        sizes = [jnp.abs(v) for v in images]
        once, twice = sizes[0] == 1, sizes[1] == 1
        none = jnp.logical_not(jnp.logical_or(once, twice))
        swap = jnp.logical_or(
            jnp.logical_and(none, sizes[1] == 9),
            jnp.logical_or(jnp.logical_and(once, sizes[2] == 9), jnp.logical_and(twice, sizes[0] == 9)))
        lowest = [jnp.minimum(jnp.minimum(jnp.where(sizes[0] == n, images[0], n), jnp.where(sizes[1] == n, images[1], n)),
                              jnp.where(sizes[2] == n, images[2], n)) < 0 for n in (9, 3, 1)]
        for i, mask in enumerate((*lowest, swap, once, twice)):
            turns[slot, i] = jnp.where(mask, 1, 0)

    def turn_of(slot):
        f0, f1, f2, swap, once, twice = [turns[slot, i] != 0 for i in range(6)]
        return (f0, f1, f2), swap, once, twice

    def fill_turns(slot, carry):
        g, octet = slot // 3, lax.rem(slot, 3)
        base = rel[r * LOCAL + g, same]
        images = [jnp.zeros((8, X), jnp.int32) for _ in basis]
        for j in range(8):
            k = octet * 8 + j
            h = rel[base, rel[k, same]]
            back = rel[h, same]
            table[g * G + k] = h
            images = [jnp.where(group8 == j, perm[back, o] - 13, v) for v, o in zip(images, basis)]
        keep_turn(slot, images)
        return carry

    lax.fori_loop(0, LOCAL * 3, fill_turns, 0)

    def fill_own_turns(octet, carry):
        images = [jnp.zeros((8, X), jnp.int32) for _ in basis]
        for j in range(8):
            images = [jnp.where(group8 == j, perm[octet * 8 + j, o] - 13, v) for v, o in zip(images, basis)]
        keep_turn(LOCAL * 3 + octet, images)
        return carry

    lax.fori_loop(0, 3, fill_own_turns, 0)

    w_copy.wait()

    def widen(q, carry):
        w32[pl.ds(pl.multiple_of(q * G, 8), G), :] = win[q].astype(F32)
        return carry

    lax.fori_loop(0, TAPS, widen, 0)
    w32[TAPS * G:, :] = jnp.zeros((8, C * C), F32)
    w16[...] = w32[...].astype(BF16)
    row_id = lax.broadcasted_iota(jnp.int32, (C * C, 2 * X), 0)
    col_id = lax.broadcasted_iota(jnp.int32, (C * C, 2 * X), 1)
    same_co = row_id // C == lax.rem(col_id, C)
    row_ci = lax.rem(row_id, C) - col_id // X

    rows = wsrc.reshape(TAPS * G * C, X)

    def pass_on(half):
        whole(cot[half], LOCAL, rot_send, across_recv.at[half]).wait_recv()
        for d in (2, 1, 3):
            rot_copy(across, d, half).start()

    def spread(step, carry):
        hot = jnp.where(jnp.logical_and(same_co, row_ci == 2 * step), 1.0, 0.0).astype(BF16)
        picked = jnp.dot(w16[...], hot, preferred_element_type=F32)
        for side in range(2):
            rows[pl.ds(2 * step + side, TAPS * G, stride=C), :] = picked[:TAPS * G, side * X:(side + 1) * X]
        return carry

    lax.fori_loop(0, 4, spread, 0)
    pass_on(0)
    lax.fori_loop(4, 6, spread, 0)
    pass_on(1)
    lax.fori_loop(6, C // 2, spread, 0)


    def fill_filter(step, carry):
        g, octet = step // 3, lax.rem(step, 3)
        labels = [rel[octet * 8 + j, r * LOCAL + g] for j in range(8)]
        turned = turn_of(LOCAL * 3 + octet)
        lanes = pl.ds(pl.multiple_of(octet * X, X), X)
        for part_of in range(2):
            blocks = []
            for q in range(TAPS):
                merged = None
                for j in range(8):
                    block = wsrc[q, labels[j], 8 * part_of:8 * part_of + 8]
                    merged = block if merged is None else jnp.where(group8 == j, block, merged)
                blocks.append(merged)
            at = pl.ds(pl.multiple_of(g * C + 8 * part_of, 8), 8)
            for o, block in enumerate(turn(blocks, *turned)):
                wturn[o, at, lanes] = block
        return carry

    lax.fori_loop(0, LOCAL * 3, fill_filter, 0)

    both_sides(feats, LOCAL, halo_send, halo_recv, lambda copy: copy.wait_recv())
    lane48 = lane_iota(ROWS)

    def fill_shifts(a, carry):
        blank = jnp.zeros((C, X), BF16)
        for y in range(Y):
            plane = feats[pl.ds(a * LOCAL, LOCAL), :, y * X:(y + 1) * X].astype(F32).reshape(ROWS, X)
            for c in range(3):
                if c == 0:
                    moved = jnp.where(lane48 == 0, 0.0, pltpu.roll(plane, 1, 1))
                elif c == 2:
                    moved = jnp.where(lane48 == X - 1, 0.0, pltpu.roll(plane, X - 1, 1))
                else:
                    moved = plane
                moved = moved.astype(BF16)
                for b in range(3):
                    target = y - (b - 1)
                    at = pl.multiple_of((a * 9 + b * 3 + c) * C, 16)
                    for g in range(LOCAL):
                        if 0 <= target < Y:
                            f27[g, pl.ds(at, C), target * X:(target + 1) * X] = moved[g * C:(g + 1) * C]
                        if (b == 2 and y == Y - 1) or (b == 0 and y == 0):
                            f27[g, pl.ds(at, C), y * X:(y + 1) * X] = blank
        return carry

    lax.fori_loop(0, 3, fill_shifts, 0)

    for half in parts:
        voxels = slice(PARTS[half][0] * X, PARTS[half][1] * X)
        rot_all[half].wait_recv()

        def reorder(k, carry):
            for g in range(LOCAL):
                pc[g, pl.ds(pl.multiple_of(k * C, 16), C), voxels] = cot[half][table[g * G + k]]
            return carry

        lax.fori_loop(0, G, reorder, 0)

        def pair_sums(g, carry):
            product = lax.dot_general(
                f27[g, :, voxels], pc[g, :, voxels], (((1,), (1,)), ((), ())), preferred_element_type=F32)
            for octet in range(3):
                some = product[:, octet * X:(octet + 1) * X].reshape(TAPS, C, X)
                if half == 0:
                    quad[g, octet] = some
                else:
                    quad[g, octet] += some
            return carry

        lax.fori_loop(0, LOCAL, pair_sums, 0)

    def relabel(step, carry):
        octet, part_of = step // 2, lax.rem(step, 2)
        at = pl.ds(pl.multiple_of(octet * C + 8 * part_of, 8), 8)
        half_at = pl.ds(pl.multiple_of(8 * part_of, 8), 8)
        for g in range(LOCAL):
            turned = turn([quad[g, octet, o, half_at] for o in range(TAPS)], *turn_of(g * 3 + octet))
            for q in range(TAPS):
                if g == 0:
                    sums[int(q >= SHARES[0]), q - SHARES[0] * int(q >= SHARES[0]), at] = turned[q]
                else:
                    sums[int(q >= SHARES[0]), q - SHARES[0] * int(q >= SHARES[0]), at] += turned[q]
        return carry

    for i in range(SHARES[0], 16):
        sums[0, i] = jnp.zeros((UNIT, X), F32)
    lax.fori_loop(0, 6, relabel, 0)

    mine = core * SHARES[0]
    share = SHARES[0] + core * (SHARES[1] - SHARES[0])

    def by_core(act):
        for side in range(2):
            @pl.when(core == side)
            def _():
                act(SHARES[side])


    def row_of(chunk):
        dy = (2, 3, 1, 0)[chunk]
        return lax.rem(yy + dy + 2, 4)

    def owner(step):
        row, column = 3 - step // 4, 3 - step % 4
        return row_of(step // 4) * 4 + lax.rem(xx + (2, 3, 1, 0)[step % 4], 4)

    def xy_copy(step):
        return pltpu.make_async_remote_copy(
            src_ref=xy_out.at[owner(step)], dst_ref=xy_in.at[m], send_sem=xy_send, recv_sem=xy_recv,
            device_id=xy_dev(owner(step)), device_id_type=MESH)

    def core_copy(chunk):
        return pltpu.make_async_remote_copy(
            src_ref=sums.at[1 - core, pl.ds(row_of(chunk) * 4, 4)], dst_ref=core_in.at[pl.ds(row_of(chunk) * 4, 4)],
            send_sem=core_send, recv_sem=core_recv.at[chunk],
            device_id=(sibling, r), device_id_type=MESH)

    for chunk in range(4):
        core_copy(chunk).start()
    for chunk in range(4):
        core_copy(chunk).wait_recv()
        for step in range(chunk * 4, chunk * 4 + 4):
            i = owner(step)
            if step < 15:
                xy_out[i] = to_steps(sums[core, i] + core_in[i])
        for step in range(chunk * 4, min(chunk * 4 + 4, 15)):
            @pl.when(owner(step) < share)
            def _():
                xy_copy(step).start()

    def input_part(a):
        wmat[...] = wturn[pl.ds(a * 9, 9)].reshape(9 * ROWS, G * C).astype(BF16)

        for n in parts:
            for at in range(0, (PARTS[n][1] - PARTS[n][0]) * X, 256):
                first = PARTS[n][0] * X + at
                fgm[:, first:first + 256] = jnp.dot(
                    wmat[...], cot[n][:, :, at:at + 256].reshape(G * C, 256), preferred_element_type=F32)
        for y in range(Y):
            total = None
            for c in range(3):
                column = None
                for b in range(3):
                    source = y - (b - 1)
                    if 0 <= source < Y:
                        term = fgm[(b * 3 + c) * ROWS:(b * 3 + c + 1) * ROWS, source * X:(source + 1) * X]
                        column = term if column is None else column + term
                if c == 0:
                    column = jnp.where(lane48 == X - 1, 0.0, pltpu.roll(column, X - 1, 1))
                elif c == 2:
                    column = jnp.where(lane48 == 0, 0.0, pltpu.roll(column, 1, 1))
                total = column if total is None else total + column
            part[a, :, y * X:(y + 1) * X] = total

    def part_copy(side):
        return pltpu.make_async_remote_copy(
            src_ref=part.at[2 - 2 * side], dst_ref=part_in.at[side], send_sem=pt_send,
            recv_sem=pt_recv, device_id=(up if side == 0 else down, r), device_id_type=MESH)

    crosses_z = at_end
    onward = s + 8 * (2 * core - 1)
    behind = s - 8 * (2 * core - 1)
    relays = jnp.logical_and(crosses_z, jnp.logical_and(behind >= 0, behind < SPACE))

    def along_z():
        return pltpu.make_async_remote_copy(
            src_ref=part.at[2 * core], dst_ref=passing, send_sem=pt_send, recv_sem=pass_recv,
            device_id=(onward, r), device_id_type=MESH)

    def along_y():
        return pltpu.make_async_remote_copy(
            src_ref=passing, dst_ref=part_in.at[1 - core], send_sem=pass_send, recv_sem=pt_recv,
            device_id=(s + 7 - 14 * core, r), device_id_type=MESH)

    def send_part(side, when):
        @pl.when(jnp.logical_and(s < SPACE - 1 if side == 0 else s > 0, when))
        def _():
            part_copy(side).start()

    input_part(2 * core)

    @pl.when(jnp.logical_and(crosses_z, jnp.logical_and(onward >= 0, onward < SPACE)))
    def _():
        along_z().start()

    input_part(2 - 2 * core)
    input_part(1)

    def z_copy(d):
        peer = lax.rem(zz + d, 8)
        return pltpu.make_async_remote_copy(
            src_ref=z_in.at[zz], dst_ref=z_in.at[zz], send_sem=z_send, recv_sem=z_recv,
            device_id=z_dev(peer), device_id_type=MESH)

    @pl.when(m < share)
    def _():
        unit[...] = sums[core, m] + core_in[m]
        whole(xy_in, 15, xy_send, xy_recv).wait_recv()
        for d in range(1, 16):
            unit[...] += from_steps(xy_in[lax.rem(m + d, 16)])
        z_in[zz] = to_steps(unit[...])
        for d in (4, 3, 5, 2, 6, 1, 7):
            z_copy(d).start()


    for side in range(2):
        send_part(side, jnp.logical_not(jnp.logical_and(crosses_z, core == 1 - side)))

    @pl.when(relays)
    def _():
        along_z().wait_recv()
        along_y().start()

    def ag_copy(d):
        return pltpu.make_async_remote_copy(
            src_ref=coded.at[mine + m], dst_ref=coded.at[mine + m], send_sem=ag_send, recv_sem=ag_recv.at[m],
            device_id=xy_dev(lax.rem(yy + d // 4 + 2, 4) * 4 + lax.rem(xx + d % 4, 4)), device_id_type=MESH)

    def finish_offset(q):
        block = from_steps(coded[q])
        wg_out[q, :, :X] = block[:G]
        wg_out[q, :, X:] = block[G:]

    def arrival(i):
        return pltpu.make_async_remote_copy(
            src_ref=coded.at[mine + i], dst_ref=coded.at[mine + i], send_sem=ag_send, recv_sem=ag_recv.at[i],
            device_id=(up, r), device_id_type=MESH)

    def forward(i):
        return pltpu.make_async_remote_copy(
            src_ref=coded.at[mine + i], dst_ref=coded.at[mine + i], send_sem=fwd_send, recv_sem=fwd_recv,
            device_id=(sibling, r), device_id_type=MESH)

    @pl.when(m < share)
    def _():
        whole(z_in, 7, z_send, z_recv).wait_recv()
        total = from_steps(z_in[0])
        for i in range(1, 8):
            total = total + from_steps(z_in[i])
        total = total * (1.0 / math.sqrt(G * SPACE * VOX))
        blank = jnp.zeros((X - C, X), F32)
        sides = [[], []]
        for octet in range(3):
            trans[...] = jnp.concatenate([total[octet * C:(octet + 1) * C], blank], 0).T
            for side in range(2):
                joined = None
                for j in range(8):
                    rows = trans[pl.ds(side * 8 + j, 8, stride=C), :]
                    rows = rows if j == 0 else pltpu.roll(rows, j * C, 1)
                    joined = rows if joined is None else joined + rows
                sides[side].append(joined)
        coded[mine + m] = to_steps(jnp.concatenate(sides[0] + sides[1], 0))
        for d in (10, 9, 11, 6, 14, 5, 7, 13, 15, 8, 2, 1, 3, 4, 12):
            ag_copy(d).start()
        forward(m).start()

    both_sides(part_in, 1, pt_send, pt_recv, lambda copy: copy.wait_recv())
    for y in range(Y):
        cols = slice(y * X, (y + 1) * X)
        lay[pl.ds(y, ROWS, stride=Y), :] = part[1, :, cols] + part_in[0, :, cols] + part_in[1, :, cols]
    fg_out[...] = lay[...].reshape(ROWS, Y, X).astype(BF16)
    for i in range(16):
        @pl.when(jnp.logical_and(m != i, i < share))
        def _():
            arrival(i).wait_recv()
            forward(i).start()
            finish_offset(mine + i)

    @pl.when(m < share)
    def _():
        finish_offset(mine + m)

    by_core(lambda count: whole(coded, TAPS - count, fwd_send, fwd_recv).wait_recv())

    @pl.when(core == 0)
    def _():
        for q in range(SHARES[0], TAPS):
            finish_offset(q)

    @pl.when(core == 1)
    def _():
        for q in range(SHARES[0]):
            finish_offset(q)


    for half in parts:
        rot_sent[half].wait_send()
    both_sides(feats, LOCAL, halo_send, halo_recv, lambda copy: copy.wait_send())
    both_sides(part_in, 1, pt_send, pt_recv, lambda copy: copy.wait_send())
    whole(core_in, 16, core_send, core_recv.at[0]).wait_send()
    by_core(lambda count: whole(coded, count, fwd_send, fwd_recv).wait_send())

    @pl.when(relays)
    def _():
        along_y().wait_send()


    @pl.when(m < share)
    def _():
        by_core(lambda count: whole(xy_in, count - 1, xy_send, xy_recv).wait_send())
        whole(z_in, 7, z_send, z_recv).wait_send()
        whole(xy_in, 15, ag_send, ag_recv.at[0]).wait_send()

    @pl.when(m >= share)
    def _():
        by_core(lambda count: whole(xy_in, count, xy_send, xy_recv).wait_send())


def finish(fg_in, wg_in, fg_out, wg_out, sem):
    pieces = [pltpu.make_async_copy(fg_in, fg_out, sem.at[0])]
    for i in range(3):
        some = pl.ds(9 * i, 9)
        pieces.append(pltpu.make_async_copy(wg_in.at[some], wg_out.at[some], sem.at[i + 1]))
    for copy in pieces:
        copy.start()
    for copy in pieces:
        copy.wait()


def local(features, cotangent, weight, relative, offset_perm):
    any_spec = pl.BlockSpec(memory_space=pl.ANY)
    vmem = pl.BlockSpec(memory_space=pltpu.VMEM)
    hbm = functools.partial(pltpu.with_memory_space_constraint, memory_space=pltpu.HBM)
    dma = pltpu.SemaphoreType.DMA
    fg, wg = pl.pallas_call(
        kernel,
        out_shape=(
            pltpu.VMEM((ROWS, Y, X), BF16),
            pltpu.VMEM((TAPS, G, C * C), F32),
        ),
        in_specs=[any_spec] * 5,
        out_specs=(vmem, vmem),
        scratch_shapes=[
            pltpu.SMEM((G, G), jnp.int32),
            pltpu.SMEM((G, TAPS), jnp.int32),
            pltpu.VMEM((2, ROWS, Y, X), BF16),
            pltpu.VMEM((TAPS, G, C * C), BF16),
            pltpu.VMEM((ROWS * Y, X), F32),
            *[pltpu.VMEM((G, C, (last - first) * X), BF16) for first, last in PARTS],
            pltpu.VMEM((3 * LOCAL, C, VOX), BF16),
            pltpu.VMEM((LOCAL, TAPS * C, VOX), BF16),
            pltpu.VMEM((LOCAL, G * C, VOX), BF16),
            pltpu.VMEM((656, C * C), F32),
            pltpu.VMEM((656, C * C), BF16),
            pltpu.VMEM((TAPS, G, C, X), F32),
            pltpu.VMEM((TAPS, ROWS, G * C), F32),
            pltpu.VMEM((9 * ROWS, G * C), BF16),
            pltpu.VMEM((LOCAL, 3, TAPS, C, X), F32),
            pltpu.SMEM((LOCAL * G,), jnp.int32),
            pltpu.VMEM((12, 6, 8, X), jnp.int32),
            pltpu.VMEM((2, 16, UNIT, X), F32),
            pltpu.VMEM((16, UNIT, X), F32),
            pltpu.VMEM((16, CODED, X), jnp.int16),
            pltpu.VMEM((16, CODED, X), jnp.int16),
            pltpu.VMEM((8, CODED, X), jnp.int16),
            pltpu.VMEM((UNIT, X), F32),
            pltpu.VMEM((X, X), F32),
            pltpu.VMEM((TAPS, CODED, X), jnp.int16),
            pltpu.VMEM((9 * ROWS, VOX), F32),
            pltpu.VMEM((3, ROWS, VOX), F32),
            pltpu.VMEM((2, ROWS, VOX), F32),
            pltpu.VMEM((ROWS, VOX), F32),
            dma((5,)), dma, dma((2,)), dma((2,)), dma, dma, dma, dma((4,)),
            dma, dma, dma, dma, dma, dma((16,)), dma, dma, dma, dma, dma, dma,
        ],
        compiler_params=pltpu.CompilerParams(
            collective_id=0, has_side_effects=True, vmem_limit_bytes=48 * 1024 * 1024
        ),
    )(
        hbm(relative), hbm(offset_perm),
        hbm(cotangent.reshape(ROWS, Y, X)), hbm(features.reshape(ROWS, Y, X)), hbm(weight),
    )
    fg, wg = pl.pallas_call(
        finish,
        out_shape=(
            jax.ShapeDtypeStruct((ROWS, Y, X), BF16),
            jax.ShapeDtypeStruct((TAPS, G, C * C), F32),
        ),
        in_specs=[vmem] * 2,
        out_specs=(any_spec, any_spec),
        scratch_shapes=[dma((4,))],
        compiler_params=pltpu.CompilerParams(vmem_limit_bytes=8 * 1024 * 1024),
    )(fg, wg)
    return fg.reshape(features.shape), wg


def solution(mesh):
    field = P("rot", None, "space", None, None)
    return jax.shard_map(
        local,
        mesh=mesh,
        in_specs=(field, field, P(), P(), P()),
        out_specs=(field, P()),
        check_vma=False,
    )
```

```python
import functools
import math

import jax
import jax.numpy as jnp
from jax import lax
from jax.experimental import pallas as pl
from jax.experimental.pallas import tpu as pltpu
from jax.sharding import PartitionSpec as P

MESH = pl.DeviceIdType.MESH
F32 = jnp.float32
BF16 = jnp.bfloat16
G, C, TAPS, Y, X = 24, 16, 27, 8, 128
ROT, SPACE = 8, 32
LOCAL = G // ROT
ROWS = LOCAL * C
VOX = Y * X
PARTS = ((0, 4), (4, 8))
SHARES = (11, 16)
CODED = 64
UNIT = 48


def lane_iota(rows):
    return lax.broadcasted_iota(jnp.int32, (rows, X), 1)


def turn(blocks, flips, swap, once, twice):
    def at(a, b, c):
        return blocks[a * 9 + b * 3 + c]

    digits = [(a, b, c) for a in range(3) for b in range(3) for c in range(3)]
    for axis in range(3):
        step = (9, 3, 1)[axis]
        blocks = [
            v if digits[o][axis] == 1 else jnp.where(flips[axis], blocks[o + 2 * step * (1 - digits[o][axis])], v)
            for o, v in enumerate(blocks)
        ]
    blocks = [at(a, b, c) if a == b else jnp.where(swap, at(b, a, c), at(a, b, c)) for a, b, c in digits]
    return [
        at(a, b, c) if a == b == c else jnp.where(once, at(b, c, a), jnp.where(twice, at(c, a, b), at(a, b, c)))
        for a, b, c in digits
    ]


def to_steps(sums):
    top = jnp.max(jnp.max(jnp.abs(sums), axis=0, keepdims=True), axis=1, keepdims=True)
    power = jnp.ceil(jnp.log2(jnp.maximum(jnp.broadcast_to(top, (8, X)), 2.0**-110)))
    steps = jnp.round(sums * jnp.concatenate([jnp.exp2(15.0 - power)] * (UNIT // 8), 0))
    steps = jnp.minimum(jnp.maximum(steps, -32767.0), 32767.0)
    return jnp.concatenate([steps, power, power], 0).astype(jnp.int32).astype(jnp.int16)


def from_steps(coded):
    wide = coded.astype(jnp.int32).astype(F32)
    return wide[:UNIT] * jnp.concatenate([jnp.exp2(wide[UNIT:UNIT + 8] - 15.0)] * (UNIT // 8), 0)


def kernel(rel_in, perm_in, cot_in, feat_in, w_in, fg_out, wg_out,
           rel, perm, stage, win, lay, cot_0, cot_1, feats, f27, pc, w32, w16, wsrc, wturn, wmat, quad, table, turns,
           sums, core_in, xy_in, xy_out, z_in, unit, trans, coded, fgm, part, part_in, passing,
           in_sem, rot_send, rot_recv, across_recv, halo_send, halo_recv, core_send, core_recv,
           xy_send, xy_recv, z_send, z_recv, ag_send, ag_recv, fwd_send, fwd_recv,
           pt_send, pt_recv, pass_send, pass_recv):
    s = lax.axis_index("space")
    r = lax.axis_index("rot")
    core = lax.rem(s, 2)
    yy = lax.rem(s // 2, 4)
    z_hi = s // 8
    xx = lax.rem(r, 4)
    z_lo = r // 4
    m = lax.rem(yy * 4 + xx + 8, 16)
    zz = z_hi * 2 + z_lo
    up, down = lax.rem(s + 1, SPACE), lax.rem(s + SPACE - 1, SPACE)
    sibling = s + 1 - 2 * core

    def xy_dev(i):
        return ((z_hi * 4 + lax.rem(i // 4 + 2, 4)) * 2 + core, z_lo * 4 + lax.rem(i, 4))

    def z_dev(i):
        return (((i // 2) * 4 + yy) * 2 + core, lax.rem(i, 2) * 4 + xx)

    barrier = pltpu.get_barrier_semaphore()
    for d in (4, 3, 5, 2, 6, 1, 7):
        pl.semaphore_signal(barrier, inc=1, device_id=z_dev(lax.rem(zz + d, 8)), device_id_type=MESH)
    for d in (10, 9, 11, 6, 14, 5, 7, 13, 15, 8, 2, 1, 3, 4, 12):
        near = lax.rem(yy + d // 4 + 2, 4) * 4 + lax.rem(xx + d % 4, 4)
        pl.semaphore_signal(barrier, inc=1, device_id=xy_dev(near), device_id_type=MESH)
    for d in (6, 5, 7, 2, 4, 1, 3):
        peer = lax.rem(z_lo + d // 4, 2) * 4 + lax.rem(xx + d % 4, 4)
        pl.semaphore_signal(barrier, inc=1, device_id=(s, peer), device_id_type=MESH)
    for other in (up, down):
        pl.semaphore_signal(barrier, inc=1, device_id=(other, r), device_id_type=MESH)
    at_end = lax.rem(s, 8) == 7 * core

    @pl.when(at_end)
    def _():
        pl.semaphore_signal(barrier, inc=1, device_id=(s + 7 - 14 * core, r), device_id_type=MESH)

    cot_copy = pltpu.make_async_copy(cot_in, stage.at[0], in_sem.at[0])
    feat_copy = pltpu.make_async_copy(feat_in, stage.at[1], in_sem.at[1])
    w_copy = pltpu.make_async_copy(w_in, win, in_sem.at[2])
    cot_copy.start()
    feat_copy.start()
    rel_copy = pltpu.make_async_copy(rel_in, rel, in_sem.at[3])
    perm_copy = pltpu.make_async_copy(perm_in, perm, in_sem.at[4])
    rel_copy.start()
    perm_copy.start()
    w_copy.start()
    cot = (cot_0, cot_1)
    part_of_row = [n for n, (first, last) in enumerate(PARTS) for _ in range(first, last)]
    parts = range(len(PARTS))

    def flatten_plane(index, place):
        lay[...] = stage[index].astype(F32).reshape(ROWS * Y, X)
        for y in range(Y):
            column = lay[pl.ds(y, ROWS, stride=Y), :].astype(BF16)
            place(y, column.reshape(LOCAL, C, X))

    own = r * LOCAL
    cot_copy.wait()

    def place_cot(y, column):
        n = part_of_row[y]
        at = (y - PARTS[n][0]) * X
        cot[n][pl.ds(own, LOCAL), :, at:at + X] = column

    flatten_plane(0, place_cot)
    feat_copy.wait()

    def place_feats(y, column):
        feats[LOCAL:2 * LOCAL, :, y * X:(y + 1) * X] = column

    flatten_plane(1, place_feats)
    pl.semaphore_wait(barrier, jnp.where(at_end, 32, 31))

    across = lax.rem(r + 4, ROT)

    def across_copy(half):
        block = cot[half].at[pl.ds(own, LOCAL)]
        return pltpu.make_async_remote_copy(
            src_ref=block, dst_ref=block, send_sem=rot_send, recv_sem=across_recv.at[half],
            device_id=(s, across), device_id_type=MESH)

    def rot_copy(owner_of, d, half):
        block = cot[half].at[pl.ds(owner_of * LOCAL, LOCAL)]
        return pltpu.make_async_remote_copy(
            src_ref=block, dst_ref=block, send_sem=rot_send, recv_sem=rot_recv.at[half],
            device_id=(s, z_lo * 4 + lax.rem(xx + d, 4)), device_id_type=MESH)

    def whole(buffer, count, sent, got):
        some = buffer.at[pl.ds(0, count)]
        return pltpu.make_async_remote_copy(
            src_ref=some, dst_ref=some, send_sem=sent, recv_sem=got, device_id=(up, r), device_id_type=MESH)

    rot_sent = [whole(cot[half], G - LOCAL, rot_send, rot_recv.at[half]) for half in parts]
    rot_all = [whole(cot[half], G - 2 * LOCAL, rot_send, rot_recv.at[half]) for half in parts]

    def halo_copy(side):
        return pltpu.make_async_remote_copy(
            src_ref=feats.at[pl.ds(LOCAL, LOCAL)], dst_ref=feats.at[pl.ds(2 * LOCAL * side, LOCAL)],
            send_sem=halo_send, recv_sem=halo_recv,
            device_id=(up if side == 0 else down, r), device_id_type=MESH)

    def each_side(act):
        @pl.when(s < SPACE - 1)
        def _():
            act(0)

        @pl.when(s > 0)
        def _():
            act(1)

    def both_sides(buffer, size, sent, got, act):
        inside = jnp.logical_and(s > 0, s < SPACE - 1)

        @pl.when(inside)
        def _():
            act(whole(buffer, 2 * size, sent, got))

        @pl.when(jnp.logical_not(inside))
        def _():
            act(whole(buffer, size, sent, got))

    @pl.when(s == 0)
    def _():
        feats[0:LOCAL] = jnp.zeros((LOCAL, C, VOX), BF16)
        part_in[0] = jnp.zeros((ROWS, VOX), F32)

    @pl.when(s == SPACE - 1)
    def _():
        feats[2 * LOCAL:] = jnp.zeros((LOCAL, C, VOX), BF16)
        part_in[1] = jnp.zeros((ROWS, VOX), F32)

    each_side(lambda side: halo_copy(side).start())
    for half in parts:
        across_copy(half).start()
    for half in parts:
        for d in (2, 1, 3):
            rot_copy(r, d, half).start()

    rel_copy.wait()
    perm_copy.wait()
    same = rel[0, 0]

    group8 = lane_iota(8) // C
    basis = (22, 16, 14)

    def keep_turn(slot, images):
        sizes = [jnp.abs(v) for v in images]
        once, twice = sizes[0] == 1, sizes[1] == 1
        none = jnp.logical_not(jnp.logical_or(once, twice))
        swap = jnp.logical_or(
            jnp.logical_and(none, sizes[1] == 9),
            jnp.logical_or(jnp.logical_and(once, sizes[2] == 9), jnp.logical_and(twice, sizes[0] == 9)))
        lowest = [jnp.minimum(jnp.minimum(jnp.where(sizes[0] == n, images[0], n), jnp.where(sizes[1] == n, images[1], n)),
                              jnp.where(sizes[2] == n, images[2], n)) < 0 for n in (9, 3, 1)]
        for i, mask in enumerate((*lowest, swap, once, twice)):
            turns[slot, i] = jnp.where(mask, 1, 0)

    def turn_of(slot):
        f0, f1, f2, swap, once, twice = [turns[slot, i] != 0 for i in range(6)]
        return (f0, f1, f2), swap, once, twice

    def fill_turns(slot, carry):
        g, octet = slot // 3, lax.rem(slot, 3)
        base = rel[r * LOCAL + g, same]
        images = [jnp.zeros((8, X), jnp.int32) for _ in basis]
        for j in range(8):
            k = octet * 8 + j
            h = rel[base, rel[k, same]]
            back = rel[h, same]
            table[g * G + k] = h
            images = [jnp.where(group8 == j, perm[back, o] - 13, v) for v, o in zip(images, basis)]
        keep_turn(slot, images)
        return carry

    lax.fori_loop(0, LOCAL * 3, fill_turns, 0)

    def fill_own_turns(octet, carry):
        images = [jnp.zeros((8, X), jnp.int32) for _ in basis]
        for j in range(8):
            images = [jnp.where(group8 == j, perm[octet * 8 + j, o] - 13, v) for v, o in zip(images, basis)]
        keep_turn(LOCAL * 3 + octet, images)
        return carry

    lax.fori_loop(0, 3, fill_own_turns, 0)

    w_copy.wait()

    def widen(q, carry):
        w32[pl.ds(pl.multiple_of(q * G, 8), G), :] = win[q].astype(F32)
        return carry

    lax.fori_loop(0, TAPS, widen, 0)
    w32[TAPS * G:, :] = jnp.zeros((8, C * C), F32)
    w16[...] = w32[...].astype(BF16)
    row_id = lax.broadcasted_iota(jnp.int32, (C * C, 2 * X), 0)
    col_id = lax.broadcasted_iota(jnp.int32, (C * C, 2 * X), 1)
    same_co = row_id // C == lax.rem(col_id, C)
    row_ci = lax.rem(row_id, C) - col_id // X

    rows = wsrc.reshape(TAPS * G * C, X)

    def pass_on(half):
        whole(cot[half], LOCAL, rot_send, across_recv.at[half]).wait_recv()
        for d in (2, 1, 3):
            rot_copy(across, d, half).start()

    def spread(step, carry):
        hot = jnp.where(jnp.logical_and(same_co, row_ci == 2 * step), 1.0, 0.0).astype(BF16)
        picked = jnp.dot(w16[...], hot, preferred_element_type=F32)
        for side in range(2):
            rows[pl.ds(2 * step + side, TAPS * G, stride=C), :] = picked[:TAPS * G, side * X:(side + 1) * X]
        return carry

    lax.fori_loop(0, 4, spread, 0)
    pass_on(0)
    lax.fori_loop(4, 6, spread, 0)
    pass_on(1)
    lax.fori_loop(6, C // 2, spread, 0)


    def fill_filter(step, carry):
        g, octet = step // 3, lax.rem(step, 3)
        labels = [rel[octet * 8 + j, r * LOCAL + g] for j in range(8)]
        turned = turn_of(LOCAL * 3 + octet)
        lanes = pl.ds(pl.multiple_of(octet * X, X), X)
        for part_of in range(2):
            blocks = []
            for q in range(TAPS):
                merged = None
                for j in range(8):
                    block = wsrc[q, labels[j], 8 * part_of:8 * part_of + 8]
                    merged = block if merged is None else jnp.where(group8 == j, block, merged)
                blocks.append(merged)
            at = pl.ds(pl.multiple_of(g * C + 8 * part_of, 8), 8)
            for o, block in enumerate(turn(blocks, *turned)):
                wturn[o, at, lanes] = block
        return carry

    lax.fori_loop(0, LOCAL * 3, fill_filter, 0)

    both_sides(feats, LOCAL, halo_send, halo_recv, lambda copy: copy.wait_recv())
    lane48 = lane_iota(ROWS)

    def fill_shifts(a, carry):
        blank = jnp.zeros((C, X), BF16)
        for y in range(Y):
            plane = feats[pl.ds(a * LOCAL, LOCAL), :, y * X:(y + 1) * X].astype(F32).reshape(ROWS, X)
            for c in range(3):
                if c == 0:
                    moved = jnp.where(lane48 == 0, 0.0, pltpu.roll(plane, 1, 1))
                elif c == 2:
                    moved = jnp.where(lane48 == X - 1, 0.0, pltpu.roll(plane, X - 1, 1))
                else:
                    moved = plane
                moved = moved.astype(BF16)
                for b in range(3):
                    target = y - (b - 1)
                    at = pl.multiple_of((a * 9 + b * 3 + c) * C, 16)
                    for g in range(LOCAL):
                        if 0 <= target < Y:
                            f27[g, pl.ds(at, C), target * X:(target + 1) * X] = moved[g * C:(g + 1) * C]
                        if (b == 2 and y == Y - 1) or (b == 0 and y == 0):
                            f27[g, pl.ds(at, C), y * X:(y + 1) * X] = blank
        return carry

    lax.fori_loop(0, 3, fill_shifts, 0)

    for half in parts:
        voxels = slice(PARTS[half][0] * X, PARTS[half][1] * X)
        rot_all[half].wait_recv()

        for g in range(LOCAL):
            for k in range(G):
                pc[g, k * C:(k + 1) * C, voxels] = cot[half][table[g * G + k]]

        for g in range(LOCAL):
            product = lax.dot_general(
                f27[g, :, voxels], pc[g, :, voxels], (((1,), (1,)), ((), ())), preferred_element_type=F32)
            for octet in range(3):
                some = product[:, octet * X:(octet + 1) * X].reshape(TAPS, C, X)
                if half == 0:
                    quad[g, octet] = some
                else:
                    quad[g, octet] += some

    def relabel(step):
        octet, part_of = step // 2, step % 2
        at = pl.ds(octet * C + 8 * part_of, 8)
        half_at = pl.ds(8 * part_of, 8)
        for g in range(LOCAL):
            turned = turn([quad[g, octet, o, half_at] for o in range(TAPS)], *turn_of(g * 3 + octet))
            for q in range(TAPS):
                if g == 0:
                    sums[int(q >= SHARES[0]), q - SHARES[0] * int(q >= SHARES[0]), at] = turned[q]
                else:
                    sums[int(q >= SHARES[0]), q - SHARES[0] * int(q >= SHARES[0]), at] += turned[q]

    for i in range(SHARES[0], 16):
        sums[0, i] = jnp.zeros((UNIT, X), F32)
    for step in range(6):
        relabel(step)

    mine = core * SHARES[0]
    share = SHARES[0] + core * (SHARES[1] - SHARES[0])

    def by_core(act):
        for side in range(2):
            @pl.when(core == side)
            def _():
                act(SHARES[side])


    def row_of(chunk):
        dy = (2, 3, 1, 0)[chunk]
        return lax.rem(yy + dy + 2, 4)

    def owner(step):
        row, column = 3 - step // 4, 3 - step % 4
        return row_of(step // 4) * 4 + lax.rem(xx + (2, 3, 1, 0)[step % 4], 4)

    def xy_copy(step):
        return pltpu.make_async_remote_copy(
            src_ref=xy_out.at[owner(step)], dst_ref=xy_in.at[m], send_sem=xy_send, recv_sem=xy_recv,
            device_id=xy_dev(owner(step)), device_id_type=MESH)

    def core_copy(chunk):
        return pltpu.make_async_remote_copy(
            src_ref=sums.at[1 - core, pl.ds(row_of(chunk) * 4, 4)], dst_ref=core_in.at[pl.ds(row_of(chunk) * 4, 4)],
            send_sem=core_send, recv_sem=core_recv.at[chunk],
            device_id=(sibling, r), device_id_type=MESH)

    for chunk in range(4):
        core_copy(chunk).start()
    for chunk in range(4):
        core_copy(chunk).wait_recv()
        for step in range(chunk * 4, chunk * 4 + 4):
            i = owner(step)
            if step < 15:
                xy_out[i] = to_steps(sums[core, i] + core_in[i])
        for step in range(chunk * 4, min(chunk * 4 + 4, 15)):
            @pl.when(owner(step) < share)
            def _():
                xy_copy(step).start()

    def input_part(a):
        wmat[...] = wturn[pl.ds(a * 9, 9)].reshape(9 * ROWS, G * C).astype(BF16)

        for n in parts:
            for at in range(0, (PARTS[n][1] - PARTS[n][0]) * X, 256):
                first = PARTS[n][0] * X + at
                fgm[:, first:first + 256] = jnp.dot(
                    wmat[...], cot[n][:, :, at:at + 256].reshape(G * C, 256), preferred_element_type=F32)
        for y in range(Y):
            total = None
            for c in range(3):
                column = None
                for b in range(3):
                    source = y - (b - 1)
                    if 0 <= source < Y:
                        term = fgm[(b * 3 + c) * ROWS:(b * 3 + c + 1) * ROWS, source * X:(source + 1) * X]
                        column = term if column is None else column + term
                if c == 0:
                    column = jnp.where(lane48 == X - 1, 0.0, pltpu.roll(column, X - 1, 1))
                elif c == 2:
                    column = jnp.where(lane48 == 0, 0.0, pltpu.roll(column, 1, 1))
                total = column if total is None else total + column
            part[a, :, y * X:(y + 1) * X] = total

    def part_copy(side):
        return pltpu.make_async_remote_copy(
            src_ref=part.at[2 - 2 * side], dst_ref=part_in.at[side], send_sem=pt_send,
            recv_sem=pt_recv, device_id=(up if side == 0 else down, r), device_id_type=MESH)

    crosses_z = at_end
    onward = s + 8 * (2 * core - 1)
    behind = s - 8 * (2 * core - 1)
    relays = jnp.logical_and(crosses_z, jnp.logical_and(behind >= 0, behind < SPACE))

    def along_z():
        return pltpu.make_async_remote_copy(
            src_ref=part.at[2 * core], dst_ref=passing, send_sem=pt_send, recv_sem=pass_recv,
            device_id=(onward, r), device_id_type=MESH)

    def along_y():
        return pltpu.make_async_remote_copy(
            src_ref=passing, dst_ref=part_in.at[1 - core], send_sem=pass_send, recv_sem=pt_recv,
            device_id=(s + 7 - 14 * core, r), device_id_type=MESH)

    def send_part(side, when):
        @pl.when(jnp.logical_and(s < SPACE - 1 if side == 0 else s > 0, when))
        def _():
            part_copy(side).start()

    input_part(2 * core)

    @pl.when(jnp.logical_and(crosses_z, jnp.logical_and(onward >= 0, onward < SPACE)))
    def _():
        along_z().start()

    for side in range(2):
        send_part(side, jnp.logical_and(jnp.logical_not(crosses_z), core == 1 - side))
    input_part(2 - 2 * core)
    for side in range(2):
        send_part(side, core == side)
    input_part(1)

    def z_copy(d):
        peer = lax.rem(zz + d, 8)
        return pltpu.make_async_remote_copy(
            src_ref=z_in.at[zz], dst_ref=z_in.at[zz], send_sem=z_send, recv_sem=z_recv,
            device_id=z_dev(peer), device_id_type=MESH)

    @pl.when(m < share)
    def _():
        unit[...] = sums[core, m] + core_in[m]
        whole(xy_in, 15, xy_send, xy_recv).wait_recv()
        for d in range(1, 16):
            unit[...] += from_steps(xy_in[lax.rem(m + d, 16)])
        z_in[zz] = to_steps(unit[...])
        for d in (4, 3, 5, 2, 6, 1, 7):
            z_copy(d).start()


    @pl.when(relays)
    def _():
        along_z().wait_recv()
        along_y().start()

    def ag_copy(d):
        return pltpu.make_async_remote_copy(
            src_ref=coded.at[mine + m], dst_ref=coded.at[mine + m], send_sem=ag_send, recv_sem=ag_recv.at[m],
            device_id=xy_dev(lax.rem(yy + d // 4 + 2, 4) * 4 + lax.rem(xx + d % 4, 4)), device_id_type=MESH)

    def finish_offset(q):
        block = from_steps(coded[q])
        wg_out[q, :, :X] = block[:G]
        wg_out[q, :, X:] = block[G:]

    def arrival(i):
        return pltpu.make_async_remote_copy(
            src_ref=coded.at[mine + i], dst_ref=coded.at[mine + i], send_sem=ag_send, recv_sem=ag_recv.at[i],
            device_id=(up, r), device_id_type=MESH)

    def forward(i):
        return pltpu.make_async_remote_copy(
            src_ref=coded.at[mine + i], dst_ref=coded.at[mine + i], send_sem=fwd_send, recv_sem=fwd_recv,
            device_id=(sibling, r), device_id_type=MESH)

    @pl.when(m < share)
    def _():
        whole(z_in, 7, z_send, z_recv).wait_recv()
        total = from_steps(z_in[0])
        for i in range(1, 8):
            total = total + from_steps(z_in[i])
        total = total * (1.0 / math.sqrt(G * SPACE * VOX))
        blank = jnp.zeros((X - C, X), F32)
        sides = [[], []]
        for octet in range(3):
            trans[...] = jnp.concatenate([total[octet * C:(octet + 1) * C], blank], 0).T
            for side in range(2):
                joined = None
                for j in range(8):
                    rows = trans[pl.ds(side * 8 + j, 8, stride=C), :]
                    rows = rows if j == 0 else pltpu.roll(rows, j * C, 1)
                    joined = rows if joined is None else joined + rows
                sides[side].append(joined)
        coded[mine + m] = to_steps(jnp.concatenate(sides[0] + sides[1], 0))
        for d in (10, 9, 11, 6, 14, 5, 7, 13, 15, 8, 2, 1, 3, 4, 12):
            ag_copy(d).start()
        forward(m).start()

    for i in range(16):
        @pl.when(jnp.logical_and(m != i, i < share))
        def _():
            arrival(i).wait_recv()
            forward(i).start()
            finish_offset(mine + i)

    @pl.when(m < share)
    def _():
        finish_offset(mine + m)

    both_sides(part_in, 1, pt_send, pt_recv, lambda copy: copy.wait_recv())
    for y in range(Y):
        cols = slice(y * X, (y + 1) * X)
        lay[pl.ds(y, ROWS, stride=Y), :] = part[1, :, cols] + part_in[0, :, cols] + part_in[1, :, cols]
    fg_out[...] = lay[...].reshape(ROWS, Y, X).astype(BF16)

    by_core(lambda count: whole(coded, TAPS - count, fwd_send, fwd_recv).wait_recv())

    @pl.when(core == 0)
    def _():
        for q in range(SHARES[0], TAPS):
            finish_offset(q)

    @pl.when(core == 1)
    def _():
        for q in range(SHARES[0]):
            finish_offset(q)


    for half in parts:
        rot_sent[half].wait_send()
    both_sides(feats, LOCAL, halo_send, halo_recv, lambda copy: copy.wait_send())
    both_sides(part_in, 1, pt_send, pt_recv, lambda copy: copy.wait_send())
    whole(core_in, 16, core_send, core_recv.at[0]).wait_send()
    by_core(lambda count: whole(coded, count, fwd_send, fwd_recv).wait_send())

    @pl.when(relays)
    def _():
        along_y().wait_send()


    @pl.when(m < share)
    def _():
        by_core(lambda count: whole(xy_in, count - 1, xy_send, xy_recv).wait_send())
        whole(z_in, 7, z_send, z_recv).wait_send()
        whole(xy_in, 15, ag_send, ag_recv.at[0]).wait_send()

    @pl.when(m >= share)
    def _():
        by_core(lambda count: whole(xy_in, count, xy_send, xy_recv).wait_send())


def finish(fg_in, wg_in, fg_out, wg_out, sem):
    pieces = [pltpu.make_async_copy(fg_in, fg_out, sem.at[0])]
    for i in range(3):
        some = pl.ds(9 * i, 9)
        pieces.append(pltpu.make_async_copy(wg_in.at[some], wg_out.at[some], sem.at[i + 1]))
    for copy in pieces:
        copy.start()
    for copy in pieces:
        copy.wait()


def local(features, cotangent, weight, relative, offset_perm):
    any_spec = pl.BlockSpec(memory_space=pl.ANY)
    vmem = pl.BlockSpec(memory_space=pltpu.VMEM)
    hbm = functools.partial(pltpu.with_memory_space_constraint, memory_space=pltpu.HBM)
    dma = pltpu.SemaphoreType.DMA
    fg, wg = pl.pallas_call(
        kernel,
        out_shape=(
            pltpu.VMEM((ROWS, Y, X), BF16),
            pltpu.VMEM((TAPS, G, C * C), F32),
        ),
        in_specs=[any_spec] * 5,
        out_specs=(vmem, vmem),
        scratch_shapes=[
            pltpu.SMEM((G, G), jnp.int32),
            pltpu.SMEM((G, TAPS), jnp.int32),
            pltpu.VMEM((2, ROWS, Y, X), BF16),
            pltpu.VMEM((TAPS, G, C * C), BF16),
            pltpu.VMEM((ROWS * Y, X), F32),
            *[pltpu.VMEM((G, C, (last - first) * X), BF16) for first, last in PARTS],
            pltpu.VMEM((3 * LOCAL, C, VOX), BF16),
            pltpu.VMEM((LOCAL, TAPS * C, VOX), BF16),
            pltpu.VMEM((LOCAL, G * C, VOX), BF16),
            pltpu.VMEM((656, C * C), F32),
            pltpu.VMEM((656, C * C), BF16),
            pltpu.VMEM((TAPS, G, C, X), F32),
            pltpu.VMEM((TAPS, ROWS, G * C), F32),
            pltpu.VMEM((9 * ROWS, G * C), BF16),
            pltpu.VMEM((LOCAL, 3, TAPS, C, X), F32),
            pltpu.SMEM((LOCAL * G,), jnp.int32),
            pltpu.VMEM((12, 6, 8, X), jnp.int32),
            pltpu.VMEM((2, 16, UNIT, X), F32),
            pltpu.VMEM((16, UNIT, X), F32),
            pltpu.VMEM((16, CODED, X), jnp.int16),
            pltpu.VMEM((16, CODED, X), jnp.int16),
            pltpu.VMEM((8, CODED, X), jnp.int16),
            pltpu.VMEM((UNIT, X), F32),
            pltpu.VMEM((X, X), F32),
            pltpu.VMEM((TAPS, CODED, X), jnp.int16),
            pltpu.VMEM((9 * ROWS, VOX), F32),
            pltpu.VMEM((3, ROWS, VOX), F32),
            pltpu.VMEM((2, ROWS, VOX), F32),
            pltpu.VMEM((ROWS, VOX), F32),
            dma((5,)), dma, dma((2,)), dma((2,)), dma, dma, dma, dma((4,)),
            dma, dma, dma, dma, dma, dma((16,)), dma, dma, dma, dma, dma, dma,
        ],
        compiler_params=pltpu.CompilerParams(
            collective_id=0, has_side_effects=True, vmem_limit_bytes=48 * 1024 * 1024
        ),
    )(
        hbm(relative), hbm(offset_perm),
        hbm(cotangent.reshape(ROWS, Y, X)), hbm(features.reshape(ROWS, Y, X)), hbm(weight),
    )
    fg, wg = pl.pallas_call(
        finish,
        out_shape=(
            jax.ShapeDtypeStruct((ROWS, Y, X), BF16),
            jax.ShapeDtypeStruct((TAPS, G, C * C), F32),
        ),
        in_specs=[vmem] * 2,
        out_specs=(any_spec, any_spec),
        scratch_shapes=[dma((4,))],
        compiler_params=pltpu.CompilerParams(vmem_limit_bytes=8 * 1024 * 1024),
    )(fg, wg)
    return fg.reshape(features.shape), wg


def solution(mesh):
    field = P("rot", None, "space", None, None)
    return jax.shard_map(
        local,
        mesh=mesh,
        in_specs=(field, field, P(), P(), P()),
        out_specs=(field, P()),
        check_vma=False,
    )
```

```python
import functools
import math

import jax
import jax.numpy as jnp
from jax import lax
from jax.experimental import pallas as pl
from jax.experimental.pallas import tpu as pltpu
from jax.sharding import PartitionSpec as P

MESH = pl.DeviceIdType.MESH
F32 = jnp.float32
BF16 = jnp.bfloat16
G, C, TAPS, Y, X = 24, 16, 27, 8, 128
ROT, SPACE = 8, 32
LOCAL = G // ROT
ROWS = LOCAL * C
VOX = Y * X
PARTS = ((0, 4), (4, 8))
SHARES = (11, 16)
CODED = 64
UNIT = 48


def lane_iota(rows):
    return lax.broadcasted_iota(jnp.int32, (rows, X), 1)


def turn(blocks, flips, swap, once, twice):
    def at(a, b, c):
        return blocks[a * 9 + b * 3 + c]

    digits = [(a, b, c) for a in range(3) for b in range(3) for c in range(3)]
    for axis in range(3):
        step = (9, 3, 1)[axis]
        blocks = [
            v if digits[o][axis] == 1 else jnp.where(flips[axis], blocks[o + 2 * step * (1 - digits[o][axis])], v)
            for o, v in enumerate(blocks)
        ]
    blocks = [at(a, b, c) if a == b else jnp.where(swap, at(b, a, c), at(a, b, c)) for a, b, c in digits]
    return [
        at(a, b, c) if a == b == c else jnp.where(once, at(b, c, a), jnp.where(twice, at(c, a, b), at(a, b, c)))
        for a, b, c in digits
    ]


def to_steps(sums):
    top = jnp.max(jnp.max(jnp.abs(sums), axis=0, keepdims=True), axis=1, keepdims=True)
    power = jnp.ceil(jnp.log2(jnp.maximum(jnp.broadcast_to(top, (8, X)), 2.0**-110)))
    steps = jnp.round(sums * jnp.concatenate([jnp.exp2(15.0 - power)] * (UNIT // 8), 0))
    steps = jnp.minimum(jnp.maximum(steps, -32767.0), 32767.0)
    return jnp.concatenate([steps, power, power], 0).astype(jnp.int32).astype(jnp.int16)


def from_steps(coded):
    wide = coded.astype(jnp.int32).astype(F32)
    return wide[:UNIT] * jnp.concatenate([jnp.exp2(wide[UNIT:UNIT + 8] - 15.0)] * (UNIT // 8), 0)


def kernel(rel_in, perm_in, cot_in, feat_in, w_in, fg_out, wg_out,
           rel, perm, stage, win, lay, cot_0, cot_1, feats, f27, pc, w32, w16, wsrc, wturn, wmat, quad, table, turns,
           sums, core_in, xy_in, xy_out, z_in, unit, trans, coded, fgm, part, part_in, passing,
           in_sem, rot_send, rot_recv, across_recv, halo_send, halo_recv, core_send, core_recv,
           xy_send, xy_recv, z_send, z_recv, ag_send, ag_recv, fwd_send, fwd_recv,
           pt_send, pt_recv, pass_send, pass_recv):
    s = lax.axis_index("space")
    r = lax.axis_index("rot")
    core = lax.rem(s, 2)
    yy = lax.rem(s // 2, 4)
    z_hi = s // 8
    xx = lax.rem(r, 4)
    z_lo = r // 4
    m = lax.rem(yy * 4 + xx + 8, 16)
    zz = z_hi * 2 + z_lo
    up, down = lax.rem(s + 1, SPACE), lax.rem(s + SPACE - 1, SPACE)
    sibling = s + 1 - 2 * core

    def xy_dev(i):
        return ((z_hi * 4 + lax.rem(i // 4 + 2, 4)) * 2 + core, z_lo * 4 + lax.rem(i, 4))

    def z_dev(i):
        return (((i // 2) * 4 + yy) * 2 + core, lax.rem(i, 2) * 4 + xx)

    barrier = pltpu.get_barrier_semaphore()
    for d in (4, 3, 5, 2, 6, 1, 7):
        pl.semaphore_signal(barrier, inc=1, device_id=z_dev(lax.rem(zz + d, 8)), device_id_type=MESH)
    for d in (10, 9, 11, 6, 14, 5, 7, 13, 15, 8, 2, 1, 3, 4, 12):
        near = lax.rem(yy + d // 4 + 2, 4) * 4 + lax.rem(xx + d % 4, 4)
        pl.semaphore_signal(barrier, inc=1, device_id=xy_dev(near), device_id_type=MESH)
    for d in (6, 5, 7, 2, 4, 1, 3):
        peer = lax.rem(z_lo + d // 4, 2) * 4 + lax.rem(xx + d % 4, 4)
        pl.semaphore_signal(barrier, inc=1, device_id=(s, peer), device_id_type=MESH)
    for other in (up, down):
        pl.semaphore_signal(barrier, inc=1, device_id=(other, r), device_id_type=MESH)
    at_end = lax.rem(s, 8) == 7 * core

    @pl.when(at_end)
    def _():
        pl.semaphore_signal(barrier, inc=1, device_id=(s + 7 - 14 * core, r), device_id_type=MESH)

    cot_copy = pltpu.make_async_copy(cot_in, stage.at[0], in_sem.at[0])
    feat_copy = pltpu.make_async_copy(feat_in, stage.at[1], in_sem.at[1])
    w_copy = pltpu.make_async_copy(w_in, win, in_sem.at[2])
    cot_copy.start()
    feat_copy.start()
    rel_copy = pltpu.make_async_copy(rel_in, rel, in_sem.at[3])
    perm_copy = pltpu.make_async_copy(perm_in, perm, in_sem.at[4])
    rel_copy.start()
    perm_copy.start()
    w_copy.start()
    cot = (cot_0, cot_1)
    part_of_row = [n for n, (first, last) in enumerate(PARTS) for _ in range(first, last)]
    parts = range(len(PARTS))

    def flatten_plane(index, place):
        lay[...] = stage[index].astype(F32).reshape(ROWS * Y, X)
        for y in range(Y):
            column = lay[pl.ds(y, ROWS, stride=Y), :].astype(BF16)
            place(y, column.reshape(LOCAL, C, X))

    own = r * LOCAL
    cot_copy.wait()

    def place_cot(y, column):
        n = part_of_row[y]
        at = (y - PARTS[n][0]) * X
        cot[n][pl.ds(own, LOCAL), :, at:at + X] = column

    flatten_plane(0, place_cot)
    feat_copy.wait()

    def place_feats(y, column):
        feats[LOCAL:2 * LOCAL, :, y * X:(y + 1) * X] = column

    flatten_plane(1, place_feats)
    pl.semaphore_wait(barrier, jnp.where(at_end, 32, 31))

    across = lax.rem(r + 4, ROT)

    def across_copy(half):
        block = cot[half].at[pl.ds(own, LOCAL)]
        return pltpu.make_async_remote_copy(
            src_ref=block, dst_ref=block, send_sem=rot_send, recv_sem=across_recv.at[half],
            device_id=(s, across), device_id_type=MESH)

    def rot_copy(owner_of, d, half):
        block = cot[half].at[pl.ds(owner_of * LOCAL, LOCAL)]
        return pltpu.make_async_remote_copy(
            src_ref=block, dst_ref=block, send_sem=rot_send, recv_sem=rot_recv.at[half],
            device_id=(s, z_lo * 4 + lax.rem(xx + d, 4)), device_id_type=MESH)

    def whole(buffer, count, sent, got):
        some = buffer.at[pl.ds(0, count)]
        return pltpu.make_async_remote_copy(
            src_ref=some, dst_ref=some, send_sem=sent, recv_sem=got, device_id=(up, r), device_id_type=MESH)

    rot_sent = [whole(cot[half], G - LOCAL, rot_send, rot_recv.at[half]) for half in parts]
    rot_all = [whole(cot[half], G - 2 * LOCAL, rot_send, rot_recv.at[half]) for half in parts]

    def halo_copy(side):
        return pltpu.make_async_remote_copy(
            src_ref=feats.at[pl.ds(LOCAL, LOCAL)], dst_ref=feats.at[pl.ds(2 * LOCAL * side, LOCAL)],
            send_sem=halo_send, recv_sem=halo_recv,
            device_id=(up if side == 0 else down, r), device_id_type=MESH)

    def each_side(act):
        @pl.when(s < SPACE - 1)
        def _():
            act(0)

        @pl.when(s > 0)
        def _():
            act(1)

    def both_sides(buffer, size, sent, got, act):
        inside = jnp.logical_and(s > 0, s < SPACE - 1)

        @pl.when(inside)
        def _():
            act(whole(buffer, 2 * size, sent, got))

        @pl.when(jnp.logical_not(inside))
        def _():
            act(whole(buffer, size, sent, got))

    @pl.when(s == 0)
    def _():
        feats[0:LOCAL] = jnp.zeros((LOCAL, C, VOX), BF16)
        part_in[0] = jnp.zeros((ROWS, VOX), F32)

    @pl.when(s == SPACE - 1)
    def _():
        feats[2 * LOCAL:] = jnp.zeros((LOCAL, C, VOX), BF16)
        part_in[1] = jnp.zeros((ROWS, VOX), F32)

    each_side(lambda side: halo_copy(side).start())
    for half in parts:
        across_copy(half).start()
    for half in parts:
        for d in (2, 1, 3):
            rot_copy(r, d, half).start()

    rel_copy.wait()
    perm_copy.wait()
    same = rel[0, 0]

    group8 = lane_iota(8) // C
    basis = (22, 16, 14)

    def keep_turn(slot, images):
        sizes = [jnp.abs(v) for v in images]
        once, twice = sizes[0] == 1, sizes[1] == 1
        none = jnp.logical_not(jnp.logical_or(once, twice))
        swap = jnp.logical_or(
            jnp.logical_and(none, sizes[1] == 9),
            jnp.logical_or(jnp.logical_and(once, sizes[2] == 9), jnp.logical_and(twice, sizes[0] == 9)))
        lowest = [jnp.minimum(jnp.minimum(jnp.where(sizes[0] == n, images[0], n), jnp.where(sizes[1] == n, images[1], n)),
                              jnp.where(sizes[2] == n, images[2], n)) < 0 for n in (9, 3, 1)]
        for i, mask in enumerate((*lowest, swap, once, twice)):
            turns[slot, i] = jnp.where(mask, 1, 0)

    def turn_of(slot):
        f0, f1, f2, swap, once, twice = [turns[slot, i] != 0 for i in range(6)]
        return (f0, f1, f2), swap, once, twice

    def fill_turns(slot, carry):
        g, octet = slot // 3, lax.rem(slot, 3)
        base = rel[r * LOCAL + g, same]
        images = [jnp.zeros((8, X), jnp.int32) for _ in basis]
        for j in range(8):
            k = octet * 8 + j
            h = rel[base, rel[k, same]]
            back = rel[h, same]
            table[g * G + k] = h
            images = [jnp.where(group8 == j, perm[back, o] - 13, v) for v, o in zip(images, basis)]
        keep_turn(slot, images)
        return carry

    lax.fori_loop(0, LOCAL * 3, fill_turns, 0)

    def fill_own_turns(octet, carry):
        images = [jnp.zeros((8, X), jnp.int32) for _ in basis]
        for j in range(8):
            images = [jnp.where(group8 == j, perm[octet * 8 + j, o] - 13, v) for v, o in zip(images, basis)]
        keep_turn(LOCAL * 3 + octet, images)
        return carry

    lax.fori_loop(0, 3, fill_own_turns, 0)

    w_copy.wait()

    def widen(q, carry):
        w32[pl.ds(pl.multiple_of(q * G, 8), G), :] = win[q].astype(F32)
        return carry

    lax.fori_loop(0, TAPS, widen, 0)
    w32[TAPS * G:, :] = jnp.zeros((8, C * C), F32)
    w16[...] = w32[...].astype(BF16)
    row_id = lax.broadcasted_iota(jnp.int32, (C * C, 2 * X), 0)
    col_id = lax.broadcasted_iota(jnp.int32, (C * C, 2 * X), 1)
    same_co = row_id // C == lax.rem(col_id, C)
    row_ci = lax.rem(row_id, C) - col_id // X

    rows = wsrc.reshape(TAPS * G * C, X)

    def pass_on(half):
        whole(cot[half], LOCAL, rot_send, across_recv.at[half]).wait_recv()
        for d in (2, 1, 3):
            rot_copy(across, d, half).start()

    def spread(step, carry):
        hot = jnp.where(jnp.logical_and(same_co, row_ci == 2 * step), 1.0, 0.0).astype(BF16)
        picked = jnp.dot(w16[...], hot, preferred_element_type=F32)
        for side in range(2):
            rows[pl.ds(2 * step + side, TAPS * G, stride=C), :] = picked[:TAPS * G, side * X:(side + 1) * X]
        return carry

    lax.fori_loop(0, 4, spread, 0)
    pass_on(0)
    lax.fori_loop(4, 6, spread, 0)
    pass_on(1)
    lax.fori_loop(6, C // 2, spread, 0)


    def fill_filter(step, carry):
        g, octet = step // 3, lax.rem(step, 3)
        labels = [rel[octet * 8 + j, r * LOCAL + g] for j in range(8)]
        turned = turn_of(LOCAL * 3 + octet)
        lanes = pl.ds(pl.multiple_of(octet * X, X), X)
        for part_of in range(2):
            blocks = []
            for q in range(TAPS):
                merged = None
                for j in range(8):
                    block = wsrc[q, labels[j], 8 * part_of:8 * part_of + 8]
                    merged = block if merged is None else jnp.where(group8 == j, block, merged)
                blocks.append(merged)
            at = pl.ds(pl.multiple_of(g * C + 8 * part_of, 8), 8)
            for o, block in enumerate(turn(blocks, *turned)):
                wturn[o, at, lanes] = block
        return carry

    lax.fori_loop(0, LOCAL * 3, fill_filter, 0)

    both_sides(feats, LOCAL, halo_send, halo_recv, lambda copy: copy.wait_recv())
    lane48 = lane_iota(ROWS)

    def fill_shifts(a, carry):
        blank = jnp.zeros((C, X), BF16)
        for y in range(Y):
            plane = feats[pl.ds(a * LOCAL, LOCAL), :, y * X:(y + 1) * X].astype(F32).reshape(ROWS, X)
            for c in range(3):
                if c == 0:
                    moved = jnp.where(lane48 == 0, 0.0, pltpu.roll(plane, 1, 1))
                elif c == 2:
                    moved = jnp.where(lane48 == X - 1, 0.0, pltpu.roll(plane, X - 1, 1))
                else:
                    moved = plane
                moved = moved.astype(BF16)
                for b in range(3):
                    target = y - (b - 1)
                    at = pl.multiple_of((a * 9 + b * 3 + c) * C, 16)
                    for g in range(LOCAL):
                        if 0 <= target < Y:
                            f27[g, pl.ds(at, C), target * X:(target + 1) * X] = moved[g * C:(g + 1) * C]
                        if (b == 2 and y == Y - 1) or (b == 0 and y == 0):
                            f27[g, pl.ds(at, C), y * X:(y + 1) * X] = blank
        return carry

    lax.fori_loop(0, 3, fill_shifts, 0)

    for half in parts:
        voxels = slice(PARTS[half][0] * X, PARTS[half][1] * X)
        rot_all[half].wait_recv()

        for g in range(LOCAL):
            for k in range(G):
                pc[g, k * C:(k + 1) * C, voxels] = cot[half][table[g * G + k]]

        for g in range(LOCAL):
            product = lax.dot_general(
                f27[g, :, voxels], pc[g, :, voxels], (((1,), (1,)), ((), ())), preferred_element_type=F32)
            for octet in range(3):
                some = product[:, octet * X:(octet + 1) * X].reshape(TAPS, C, X)
                quad[half, g, octet] = some

    def relabel(step):
        octet, part_of = step // 2, step % 2
        at = pl.ds(octet * C + 8 * part_of, 8)
        half_at = pl.ds(8 * part_of, 8)
        for g in range(LOCAL):
            turned = turn([quad[0, g, octet, o, half_at] + quad[1, g, octet, o, half_at] for o in range(TAPS)], *turn_of(g * 3 + octet))
            for q in range(TAPS):
                if g == 0:
                    sums[int(q >= SHARES[0]), q - SHARES[0] * int(q >= SHARES[0]), at] = turned[q]
                else:
                    sums[int(q >= SHARES[0]), q - SHARES[0] * int(q >= SHARES[0]), at] += turned[q]

    for i in range(SHARES[0], 16):
        sums[0, i] = jnp.zeros((UNIT, X), F32)
    for step in range(6):
        relabel(step)

    mine = core * SHARES[0]
    share = SHARES[0] + core * (SHARES[1] - SHARES[0])

    def by_core(act):
        for side in range(2):
            @pl.when(core == side)
            def _():
                act(SHARES[side])


    def row_of(chunk):
        dy = (2, 3, 1, 0)[chunk]
        return lax.rem(yy + dy + 2, 4)

    def owner(step):
        row, column = 3 - step // 4, 3 - step % 4
        return row_of(step // 4) * 4 + lax.rem(xx + (2, 3, 1, 0)[step % 4], 4)

    def xy_copy(step):
        return pltpu.make_async_remote_copy(
            src_ref=xy_out.at[owner(step)], dst_ref=xy_in.at[m], send_sem=xy_send, recv_sem=xy_recv.at[int(step >= 11)],
            device_id=xy_dev(owner(step)), device_id_type=MESH)

    def core_copy(chunk):
        return pltpu.make_async_remote_copy(
            src_ref=sums.at[1 - core, pl.ds(row_of(chunk) * 4, 4)], dst_ref=core_in.at[pl.ds(row_of(chunk) * 4, 4)],
            send_sem=core_send, recv_sem=core_recv.at[chunk],
            device_id=(sibling, r), device_id_type=MESH)

    for chunk in range(4):
        core_copy(chunk).start()
    for chunk in range(4):
        core_copy(chunk).wait_recv()
        for step in range(chunk * 4, chunk * 4 + 4):
            i = owner(step)
            if step < 15:
                xy_out[i] = to_steps(sums[core, i] + core_in[i])
        for step in range(chunk * 4, min(chunk * 4 + 4, 15)):
            @pl.when(owner(step) < share)
            def _():
                xy_copy(step).start()

    def input_part(a):
        wmat[...] = wturn[pl.ds(a * 9, 9)].reshape(9 * ROWS, G * C).astype(BF16)

        for n in parts:
            for at in range(0, (PARTS[n][1] - PARTS[n][0]) * X, 256):
                first = PARTS[n][0] * X + at
                fgm[:, first:first + 256] = jnp.dot(
                    wmat[...], cot[n][:, :, at:at + 256].reshape(G * C, 256), preferred_element_type=F32)
        for y in range(Y):
            total = None
            for c in range(3):
                column = None
                for b in range(3):
                    source = y - (b - 1)
                    if 0 <= source < Y:
                        term = fgm[(b * 3 + c) * ROWS:(b * 3 + c + 1) * ROWS, source * X:(source + 1) * X]
                        column = term if column is None else column + term
                if c == 0:
                    column = jnp.where(lane48 == X - 1, 0.0, pltpu.roll(column, X - 1, 1))
                elif c == 2:
                    column = jnp.where(lane48 == 0, 0.0, pltpu.roll(column, 1, 1))
                total = column if total is None else total + column
            part[a, :, y * X:(y + 1) * X] = total

    def part_copy(side):
        return pltpu.make_async_remote_copy(
            src_ref=part.at[2 - 2 * side], dst_ref=part_in.at[side], send_sem=pt_send,
            recv_sem=pt_recv, device_id=(up if side == 0 else down, r), device_id_type=MESH)

    crosses_z = at_end
    onward = s + 8 * (2 * core - 1)
    behind = s - 8 * (2 * core - 1)
    relays = jnp.logical_and(crosses_z, jnp.logical_and(behind >= 0, behind < SPACE))

    def along_z():
        return pltpu.make_async_remote_copy(
            src_ref=part.at[2 * core], dst_ref=passing, send_sem=pt_send, recv_sem=pass_recv,
            device_id=(onward, r), device_id_type=MESH)

    def along_y():
        return pltpu.make_async_remote_copy(
            src_ref=passing, dst_ref=part_in.at[1 - core], send_sem=pass_send, recv_sem=pt_recv,
            device_id=(s + 7 - 14 * core, r), device_id_type=MESH)

    def send_part(side, when):
        @pl.when(jnp.logical_and(s < SPACE - 1 if side == 0 else s > 0, when))
        def _():
            part_copy(side).start()

    input_part(2 * core)

    @pl.when(jnp.logical_and(crosses_z, jnp.logical_and(onward >= 0, onward < SPACE)))
    def _():
        along_z().start()

    for side in range(2):
        send_part(side, jnp.logical_and(jnp.logical_not(crosses_z), core == 1 - side))
    input_part(2 - 2 * core)
    for side in range(2):
        send_part(side, core == side)
    input_part(1)

    def z_copy(d):
        peer = lax.rem(zz + d, 8)
        return pltpu.make_async_remote_copy(
            src_ref=z_in.at[zz], dst_ref=z_in.at[zz], send_sem=z_send, recv_sem=z_recv,
            device_id=z_dev(peer), device_id_type=MESH)

    @pl.when(m < share)
    def _():
        unit[...] = sums[core, m] + core_in[m]
        for first, last in ((0, 11), (11, 15)):
            whole(xy_in, last - first, xy_send, xy_recv.at[int(first > 0)]).wait_recv()
            for step in range(first, last):
                dx, dy = (2, 3, 1, 0)[step % 4], (2, 3, 1, 0)[step // 4]
                unit[...] += from_steps(xy_in[lax.rem(yy - dy + 6, 4) * 4 + lax.rem(xx - dx + 4, 4)])
        z_in[zz] = to_steps(unit[...])
        for d in (4, 3, 5, 2, 6, 1, 7):
            z_copy(d).start()


    @pl.when(relays)
    def _():
        along_z().wait_recv()
        along_y().start()

    def ag_copy(d):
        return pltpu.make_async_remote_copy(
            src_ref=coded.at[mine + m], dst_ref=coded.at[mine + m], send_sem=ag_send, recv_sem=ag_recv.at[m],
            device_id=xy_dev(lax.rem(yy + d // 4 + 2, 4) * 4 + lax.rem(xx + d % 4, 4)), device_id_type=MESH)

    def finish_offset(q):
        block = from_steps(coded[q])
        wg_out[q, :, :X] = block[:G]
        wg_out[q, :, X:] = block[G:]

    def arrival(i):
        return pltpu.make_async_remote_copy(
            src_ref=coded.at[mine + i], dst_ref=coded.at[mine + i], send_sem=ag_send, recv_sem=ag_recv.at[i],
            device_id=(up, r), device_id_type=MESH)

    def forward(i):
        return pltpu.make_async_remote_copy(
            src_ref=coded.at[mine + i], dst_ref=coded.at[mine + i], send_sem=fwd_send, recv_sem=fwd_recv,
            device_id=(sibling, r), device_id_type=MESH)

    @pl.when(m < share)
    def _():
        whole(z_in, 7, z_send, z_recv).wait_recv()
        total = from_steps(z_in[0])
        for i in range(1, 8):
            total = total + from_steps(z_in[i])
        total = total * (1.0 / math.sqrt(G * SPACE * VOX))
        blank = jnp.zeros((X - C, X), F32)
        sides = [[], []]
        for octet in range(3):
            trans[...] = jnp.concatenate([total[octet * C:(octet + 1) * C], blank], 0).T
            for side in range(2):
                joined = None
                for j in range(8):
                    rows = trans[pl.ds(side * 8 + j, 8, stride=C), :]
                    rows = rows if j == 0 else pltpu.roll(rows, j * C, 1)
                    joined = rows if joined is None else joined + rows
                sides[side].append(joined)
        coded[mine + m] = to_steps(jnp.concatenate(sides[0] + sides[1], 0))
        for d in (10, 9, 11, 6, 14, 5, 7, 13, 15, 8, 2, 1, 3, 4, 12):
            ag_copy(d).start()
        forward(m).start()

    for i in range(16):
        @pl.when(jnp.logical_and(m != i, i < share))
        def _():
            arrival(i).wait_recv()
            forward(i).start()
            finish_offset(mine + i)

    @pl.when(m < share)
    def _():
        finish_offset(mine + m)

    both_sides(part_in, 1, pt_send, pt_recv, lambda copy: copy.wait_recv())
    for y in range(Y):
        cols = slice(y * X, (y + 1) * X)
        lay[pl.ds(y, ROWS, stride=Y), :] = part[1, :, cols] + part_in[0, :, cols] + part_in[1, :, cols]
    fg_out[...] = lay[...].reshape(ROWS, Y, X).astype(BF16)

    by_core(lambda count: whole(coded, TAPS - count, fwd_send, fwd_recv).wait_recv())

    @pl.when(core == 0)
    def _():
        for q in range(SHARES[0], TAPS):
            finish_offset(q)

    @pl.when(core == 1)
    def _():
        for q in range(SHARES[0]):
            finish_offset(q)


    for half in parts:
        rot_sent[half].wait_send()
    both_sides(feats, LOCAL, halo_send, halo_recv, lambda copy: copy.wait_send())
    both_sides(part_in, 1, pt_send, pt_recv, lambda copy: copy.wait_send())
    whole(core_in, 16, core_send, core_recv.at[0]).wait_send()
    by_core(lambda count: whole(coded, count, fwd_send, fwd_recv).wait_send())

    @pl.when(relays)
    def _():
        along_y().wait_send()


    @pl.when(m < share)
    def _():
        by_core(lambda count: whole(xy_in, count - 1, xy_send, xy_recv.at[0]).wait_send())
        whole(z_in, 7, z_send, z_recv).wait_send()
        whole(xy_in, 15, ag_send, ag_recv.at[0]).wait_send()

    @pl.when(m >= share)
    def _():
        by_core(lambda count: whole(xy_in, count, xy_send, xy_recv.at[0]).wait_send())


def finish(fg_in, wg_in, fg_out, wg_out, sem):
    pieces = [pltpu.make_async_copy(fg_in, fg_out, sem.at[0])]
    for i in range(3):
        some = pl.ds(9 * i, 9)
        pieces.append(pltpu.make_async_copy(wg_in.at[some], wg_out.at[some], sem.at[i + 1]))
    for copy in pieces:
        copy.start()
    for copy in pieces:
        copy.wait()


def local(features, cotangent, weight, relative, offset_perm):
    any_spec = pl.BlockSpec(memory_space=pl.ANY)
    vmem = pl.BlockSpec(memory_space=pltpu.VMEM)
    hbm = functools.partial(pltpu.with_memory_space_constraint, memory_space=pltpu.HBM)
    dma = pltpu.SemaphoreType.DMA
    fg, wg = pl.pallas_call(
        kernel,
        out_shape=(
            pltpu.VMEM((ROWS, Y, X), BF16),
            pltpu.VMEM((TAPS, G, C * C), F32),
        ),
        in_specs=[any_spec] * 5,
        out_specs=(vmem, vmem),
        scratch_shapes=[
            pltpu.SMEM((G, G), jnp.int32),
            pltpu.SMEM((G, TAPS), jnp.int32),
            pltpu.VMEM((2, ROWS, Y, X), BF16),
            pltpu.VMEM((TAPS, G, C * C), BF16),
            pltpu.VMEM((ROWS * Y, X), F32),
            *[pltpu.VMEM((G, C, (last - first) * X), BF16) for first, last in PARTS],
            pltpu.VMEM((3 * LOCAL, C, VOX), BF16),
            pltpu.VMEM((LOCAL, TAPS * C, VOX), BF16),
            pltpu.VMEM((LOCAL, G * C, VOX), BF16),
            pltpu.VMEM((656, C * C), F32),
            pltpu.VMEM((656, C * C), BF16),
            pltpu.VMEM((TAPS, G, C, X), F32),
            pltpu.VMEM((TAPS, ROWS, G * C), F32),
            pltpu.VMEM((9 * ROWS, G * C), BF16),
            pltpu.VMEM((2, LOCAL, 3, TAPS, C, X), F32),
            pltpu.SMEM((LOCAL * G,), jnp.int32),
            pltpu.VMEM((12, 6, 8, X), jnp.int32),
            pltpu.VMEM((2, 16, UNIT, X), F32),
            pltpu.VMEM((16, UNIT, X), F32),
            pltpu.VMEM((16, CODED, X), jnp.int16),
            pltpu.VMEM((16, CODED, X), jnp.int16),
            pltpu.VMEM((8, CODED, X), jnp.int16),
            pltpu.VMEM((UNIT, X), F32),
            pltpu.VMEM((X, X), F32),
            pltpu.VMEM((TAPS, CODED, X), jnp.int16),
            pltpu.VMEM((9 * ROWS, VOX), F32),
            pltpu.VMEM((3, ROWS, VOX), F32),
            pltpu.VMEM((2, ROWS, VOX), F32),
            pltpu.VMEM((ROWS, VOX), F32),
            dma((5,)), dma, dma((2,)), dma((2,)), dma, dma, dma, dma((4,)),
            dma, dma((2,)), dma, dma, dma, dma((16,)), dma, dma, dma, dma, dma, dma,
        ],
        compiler_params=pltpu.CompilerParams(
            collective_id=0, has_side_effects=True, vmem_limit_bytes=48 * 1024 * 1024
        ),
    )(
        hbm(relative), hbm(offset_perm),
        hbm(cotangent.reshape(ROWS, Y, X)), hbm(features.reshape(ROWS, Y, X)), hbm(weight),
    )
    fg, wg = pl.pallas_call(
        finish,
        out_shape=(
            jax.ShapeDtypeStruct((ROWS, Y, X), BF16),
            jax.ShapeDtypeStruct((TAPS, G, C * C), F32),
        ),
        in_specs=[vmem] * 2,
        out_specs=(any_spec, any_spec),
        scratch_shapes=[dma((4,))],
        compiler_params=pltpu.CompilerParams(vmem_limit_bytes=8 * 1024 * 1024),
    )(fg, wg)
    return fg.reshape(features.shape), wg


def solution(mesh):
    field = P("rot", None, "space", None, None)
    return jax.shard_map(
        local,
        mesh=mesh,
        in_specs=(field, field, P(), P(), P()),
        out_specs=(field, P()),
        check_vma=False,
    )
```

```python
import functools
import math

import jax
import jax.numpy as jnp
from jax import lax
from jax.experimental import pallas as pl
from jax.experimental.pallas import tpu as pltpu
from jax.sharding import PartitionSpec as P

MESH = pl.DeviceIdType.MESH
F32 = jnp.float32
BF16 = jnp.bfloat16
G, C, TAPS, Y, X = 24, 16, 27, 8, 128
ROT, SPACE = 8, 32
LOCAL = G // ROT
ROWS = LOCAL * C
VOX = Y * X
PARTS = ((0, 4), (4, 8))
SHARES = (11, 16)
CODED = 64
UNIT = 48


def lane_iota(rows):
    return lax.broadcasted_iota(jnp.int32, (rows, X), 1)


def turn(blocks, flips, swap, once, twice):
    def at(a, b, c):
        return blocks[a * 9 + b * 3 + c]

    digits = [(a, b, c) for a in range(3) for b in range(3) for c in range(3)]
    for axis in range(3):
        step = (9, 3, 1)[axis]
        blocks = [
            v if digits[o][axis] == 1 else jnp.where(flips[axis], blocks[o + 2 * step * (1 - digits[o][axis])], v)
            for o, v in enumerate(blocks)
        ]
    blocks = [at(a, b, c) if a == b else jnp.where(swap, at(b, a, c), at(a, b, c)) for a, b, c in digits]
    return [
        at(a, b, c) if a == b == c else jnp.where(once, at(b, c, a), jnp.where(twice, at(c, a, b), at(a, b, c)))
        for a, b, c in digits
    ]


def to_steps(sums):
    top = jnp.max(jnp.max(jnp.abs(sums), axis=0, keepdims=True), axis=1, keepdims=True)
    power = jnp.ceil(jnp.log2(jnp.maximum(jnp.broadcast_to(top, (8, X)), 2.0**-110)))
    steps = jnp.round(sums * jnp.concatenate([jnp.exp2(15.0 - power)] * (UNIT // 8), 0))
    steps = jnp.minimum(jnp.maximum(steps, -32767.0), 32767.0)
    return jnp.concatenate([steps, power, power], 0).astype(jnp.int32).astype(jnp.int16)


def from_steps(coded):
    wide = coded.astype(jnp.int32).astype(F32)
    return wide[:UNIT] * jnp.concatenate([jnp.exp2(wide[UNIT:UNIT + 8] - 15.0)] * (UNIT // 8), 0)


def kernel(rel_in, perm_in, cot_in, feat_in, w_in, fg_out, wg_out,
           rel, perm, stage, win, lay, cot_0, cot_1, feats, f27, pc, w32, w16, wsrc, wturn, wmat, quad, table, turns,
           sums, core_in, xy_in, xy_out, z_in, unit, trans, coded, fgm, part, part_in, passing,
           in_sem, rot_send, rot_recv, across_recv, halo_send, halo_recv, core_send, core_recv,
           xy_send, xy_recv, z_send, z_recv, ag_send, ag_recv, fwd_send, fwd_recv,
           pt_send, pt_recv, pass_send, pass_recv):
    s = lax.axis_index("space")
    r = lax.axis_index("rot")
    core = lax.rem(s, 2)
    yy = lax.rem(s // 2, 4)
    z_hi = s // 8
    xx = lax.rem(r, 4)
    z_lo = r // 4
    m = lax.rem(yy * 4 + xx + 8, 16)
    zz = z_hi * 2 + z_lo
    up, down = lax.rem(s + 1, SPACE), lax.rem(s + SPACE - 1, SPACE)
    sibling = s + 1 - 2 * core

    def xy_dev(i):
        return ((z_hi * 4 + lax.rem(i // 4 + 2, 4)) * 2 + core, z_lo * 4 + lax.rem(i, 4))

    def z_dev(i):
        return (((i // 2) * 4 + yy) * 2 + core, lax.rem(i, 2) * 4 + xx)

    barrier = pltpu.get_barrier_semaphore()
    for d in (4, 3, 5, 2, 6, 1, 7):
        pl.semaphore_signal(barrier, inc=1, device_id=z_dev(lax.rem(zz + d, 8)), device_id_type=MESH)
    for d in (10, 9, 11, 6, 14, 5, 7, 13, 15, 8, 2, 1, 3, 4, 12):
        near = lax.rem(yy + d // 4 + 2, 4) * 4 + lax.rem(xx + d % 4, 4)
        pl.semaphore_signal(barrier, inc=1, device_id=xy_dev(near), device_id_type=MESH)
    for d in (6, 5, 7, 2, 4, 1, 3):
        peer = lax.rem(z_lo + d // 4, 2) * 4 + lax.rem(xx + d % 4, 4)
        pl.semaphore_signal(barrier, inc=1, device_id=(s, peer), device_id_type=MESH)
    for other in (up, down):
        pl.semaphore_signal(barrier, inc=1, device_id=(other, r), device_id_type=MESH)
    at_end = lax.rem(s, 8) == 7 * core

    @pl.when(at_end)
    def _():
        pl.semaphore_signal(barrier, inc=1, device_id=(s + 7 - 14 * core, r), device_id_type=MESH)

    cot_copy = pltpu.make_async_copy(cot_in, stage.at[0], in_sem.at[0])
    feat_copy = pltpu.make_async_copy(feat_in, stage.at[1], in_sem.at[1])
    w_copy = pltpu.make_async_copy(w_in, win, in_sem.at[2])
    cot_copy.start()
    feat_copy.start()
    rel_copy = pltpu.make_async_copy(rel_in, rel, in_sem.at[3])
    perm_copy = pltpu.make_async_copy(perm_in, perm, in_sem.at[4])
    rel_copy.start()
    perm_copy.start()
    w_copy.start()
    cot = (cot_0, cot_1)
    part_of_row = [n for n, (first, last) in enumerate(PARTS) for _ in range(first, last)]
    parts = range(len(PARTS))

    def flatten_plane(index, place):
        lay[...] = stage[index].astype(F32).reshape(ROWS * Y, X)
        for y in range(Y):
            column = lay[pl.ds(y, ROWS, stride=Y), :].astype(BF16)
            place(y, column.reshape(LOCAL, C, X))

    own = r * LOCAL
    cot_copy.wait()

    def place_cot(y, column):
        n = part_of_row[y]
        at = (y - PARTS[n][0]) * X
        cot[n][pl.ds(own, LOCAL), :, at:at + X] = column

    flatten_plane(0, place_cot)
    feat_copy.wait()

    def place_feats(y, column):
        feats[LOCAL:2 * LOCAL, :, y * X:(y + 1) * X] = column

    flatten_plane(1, place_feats)
    pl.semaphore_wait(barrier, jnp.where(at_end, 32, 31))

    across = lax.rem(r + 4, ROT)

    def across_copy(half):
        block = cot[half].at[pl.ds(own, LOCAL)]
        return pltpu.make_async_remote_copy(
            src_ref=block, dst_ref=block, send_sem=rot_send, recv_sem=across_recv.at[half],
            device_id=(s, across), device_id_type=MESH)

    def rot_copy(owner_of, d, half):
        block = cot[half].at[pl.ds(owner_of * LOCAL, LOCAL)]
        return pltpu.make_async_remote_copy(
            src_ref=block, dst_ref=block, send_sem=rot_send, recv_sem=rot_recv.at[half],
            device_id=(s, z_lo * 4 + lax.rem(xx + d, 4)), device_id_type=MESH)

    def whole(buffer, count, sent, got):
        some = buffer.at[pl.ds(0, count)]
        return pltpu.make_async_remote_copy(
            src_ref=some, dst_ref=some, send_sem=sent, recv_sem=got, device_id=(up, r), device_id_type=MESH)

    rot_sent = [whole(cot[half], G - LOCAL, rot_send, rot_recv.at[half]) for half in parts]
    rot_all = [whole(cot[half], G - 2 * LOCAL, rot_send, rot_recv.at[half]) for half in parts]

    def halo_copy(side):
        return pltpu.make_async_remote_copy(
            src_ref=feats.at[pl.ds(LOCAL, LOCAL)], dst_ref=feats.at[pl.ds(2 * LOCAL * side, LOCAL)],
            send_sem=halo_send, recv_sem=halo_recv,
            device_id=(up if side == 0 else down, r), device_id_type=MESH)

    def each_side(act):
        @pl.when(s < SPACE - 1)
        def _():
            act(0)

        @pl.when(s > 0)
        def _():
            act(1)

    def both_sides(buffer, size, sent, got, act):
        inside = jnp.logical_and(s > 0, s < SPACE - 1)

        @pl.when(inside)
        def _():
            act(whole(buffer, 2 * size, sent, got))

        @pl.when(jnp.logical_not(inside))
        def _():
            act(whole(buffer, size, sent, got))

    @pl.when(s == 0)
    def _():
        feats[0:LOCAL] = jnp.zeros((LOCAL, C, VOX), BF16)
        part_in[0] = jnp.zeros((ROWS, VOX), F32)

    @pl.when(s == SPACE - 1)
    def _():
        feats[2 * LOCAL:] = jnp.zeros((LOCAL, C, VOX), BF16)
        part_in[1] = jnp.zeros((ROWS, VOX), F32)

    each_side(lambda side: halo_copy(side).start())
    for half in parts:
        across_copy(half).start()
    for half in parts:
        for d in (2, 1, 3):
            rot_copy(r, d, half).start()

    rel_copy.wait()
    perm_copy.wait()
    same = rel[0, 0]

    group8 = lane_iota(8) // C
    basis = (22, 16, 14)

    def keep_turn(slot, images):
        sizes = [jnp.abs(v) for v in images]
        once, twice = sizes[0] == 1, sizes[1] == 1
        none = jnp.logical_not(jnp.logical_or(once, twice))
        swap = jnp.logical_or(
            jnp.logical_and(none, sizes[1] == 9),
            jnp.logical_or(jnp.logical_and(once, sizes[2] == 9), jnp.logical_and(twice, sizes[0] == 9)))
        lowest = [jnp.minimum(jnp.minimum(jnp.where(sizes[0] == n, images[0], n), jnp.where(sizes[1] == n, images[1], n)),
                              jnp.where(sizes[2] == n, images[2], n)) < 0 for n in (9, 3, 1)]
        for i, mask in enumerate((*lowest, swap, once, twice)):
            turns[slot, i] = jnp.where(mask, 1, 0)

    def turn_of(slot):
        f0, f1, f2, swap, once, twice = [turns[slot, i] != 0 for i in range(6)]
        return (f0, f1, f2), swap, once, twice

    def fill_turns(slot, carry):
        g, octet = slot // 3, lax.rem(slot, 3)
        base = rel[r * LOCAL + g, same]
        images = [jnp.zeros((8, X), jnp.int32) for _ in basis]
        for j in range(8):
            k = octet * 8 + j
            h = rel[base, rel[k, same]]
            back = rel[h, same]
            table[g * G + k] = h
            images = [jnp.where(group8 == j, perm[back, o] - 13, v) for v, o in zip(images, basis)]
        keep_turn(slot, images)
        return carry

    lax.fori_loop(0, LOCAL * 3, fill_turns, 0)

    def fill_own_turns(octet, carry):
        images = [jnp.zeros((8, X), jnp.int32) for _ in basis]
        for j in range(8):
            images = [jnp.where(group8 == j, perm[octet * 8 + j, o] - 13, v) for v, o in zip(images, basis)]
        keep_turn(LOCAL * 3 + octet, images)
        return carry

    lax.fori_loop(0, 3, fill_own_turns, 0)

    w_copy.wait()

    def widen(q, carry):
        w32[pl.ds(pl.multiple_of(q * G, 8), G), :] = win[q].astype(F32)
        return carry

    lax.fori_loop(0, TAPS, widen, 0)
    w32[TAPS * G:, :] = jnp.zeros((8, C * C), F32)
    w16[...] = w32[...].astype(BF16)
    row_id = lax.broadcasted_iota(jnp.int32, (C * C, 2 * X), 0)
    col_id = lax.broadcasted_iota(jnp.int32, (C * C, 2 * X), 1)
    same_co = row_id // C == lax.rem(col_id, C)
    row_ci = lax.rem(row_id, C) - col_id // X

    rows = wsrc.reshape(TAPS * G * C, X)

    def pass_on(half):
        whole(cot[half], LOCAL, rot_send, across_recv.at[half]).wait_recv()
        for d in (2, 1, 3):
            rot_copy(across, d, half).start()

    def spread(step, carry):
        hot = jnp.where(jnp.logical_and(same_co, row_ci == 2 * step), 1.0, 0.0).astype(BF16)
        picked = jnp.dot(w16[...], hot, preferred_element_type=F32)
        for side in range(2):
            rows[pl.ds(2 * step + side, TAPS * G, stride=C), :] = picked[:TAPS * G, side * X:(side + 1) * X]
        return carry

    lax.fori_loop(0, 4, spread, 0)
    pass_on(0)
    lax.fori_loop(4, 6, spread, 0)
    pass_on(1)
    lax.fori_loop(6, C // 2, spread, 0)


    def fill_filter(step, carry):
        g, octet = step // 3, lax.rem(step, 3)
        labels = [rel[octet * 8 + j, r * LOCAL + g] for j in range(8)]
        turned = turn_of(LOCAL * 3 + octet)
        lanes = pl.ds(pl.multiple_of(octet * X, X), X)
        for part_of in range(2):
            blocks = []
            for q in range(TAPS):
                merged = None
                for j in range(8):
                    block = wsrc[q, labels[j], 8 * part_of:8 * part_of + 8]
                    merged = block if merged is None else jnp.where(group8 == j, block, merged)
                blocks.append(merged)
            at = pl.ds(pl.multiple_of(g * C + 8 * part_of, 8), 8)
            for o, block in enumerate(turn(blocks, *turned)):
                wturn[o, at, lanes] = block
        return carry

    lax.fori_loop(0, LOCAL * 3, fill_filter, 0)

    both_sides(feats, LOCAL, halo_send, halo_recv, lambda copy: copy.wait_recv())
    lane48 = lane_iota(ROWS)

    def fill_shifts(a, carry):
        blank = jnp.zeros((C, X), BF16)
        for y in range(Y):
            plane = feats[pl.ds(a * LOCAL, LOCAL), :, y * X:(y + 1) * X].astype(F32).reshape(ROWS, X)
            for c in range(3):
                if c == 0:
                    moved = jnp.where(lane48 == 0, 0.0, pltpu.roll(plane, 1, 1))
                elif c == 2:
                    moved = jnp.where(lane48 == X - 1, 0.0, pltpu.roll(plane, X - 1, 1))
                else:
                    moved = plane
                moved = moved.astype(BF16)
                for b in range(3):
                    target = y - (b - 1)
                    at = pl.multiple_of((a * 9 + b * 3 + c) * C, 16)
                    for g in range(LOCAL):
                        if 0 <= target < Y:
                            f27[g, pl.ds(at, C), target * X:(target + 1) * X] = moved[g * C:(g + 1) * C]
                        if (b == 2 and y == Y - 1) or (b == 0 and y == 0):
                            f27[g, pl.ds(at, C), y * X:(y + 1) * X] = blank
        return carry

    lax.fori_loop(0, 3, fill_shifts, 0)

    for half in parts:
        voxels = slice(PARTS[half][0] * X, PARTS[half][1] * X)
        rot_all[half].wait_recv()

        for g in range(LOCAL):
            for k in range(G):
                pc[g, k * C:(k + 1) * C, voxels] = cot[half][table[g * G + k]]

        for g in range(LOCAL):
            product = lax.dot_general(
                f27[g, :, voxels], pc[g, :, voxels], (((1,), (1,)), ((), ())), preferred_element_type=F32)
            for octet in range(3):
                some = product[:, octet * X:(octet + 1) * X].reshape(TAPS, C, X)
                if half == 0:
                    quad[g, octet] = some
                else:
                    quad[g, octet] += some

    def relabel(step):
        octet, part_of = step // 2, step % 2
        at = pl.ds(octet * C + 8 * part_of, 8)
        half_at = pl.ds(8 * part_of, 8)
        for g in range(LOCAL):
            turned = turn([quad[g, octet, o, half_at] for o in range(TAPS)], *turn_of(g * 3 + octet))
            for q in range(TAPS):
                if g == 0:
                    sums[int(q >= SHARES[0]), q - SHARES[0] * int(q >= SHARES[0]), at] = turned[q]
                else:
                    sums[int(q >= SHARES[0]), q - SHARES[0] * int(q >= SHARES[0]), at] += turned[q]

    for i in range(SHARES[0], 16):
        sums[0, i] = jnp.zeros((UNIT, X), F32)
    for step in range(6):
        relabel(step)

    mine = core * SHARES[0]
    share = SHARES[0] + core * (SHARES[1] - SHARES[0])

    def by_core(act):
        for side in range(2):
            @pl.when(core == side)
            def _():
                act(SHARES[side])


    def row_of(chunk):
        dy = (2, 3, 1, 0)[chunk]
        return lax.rem(yy + dy + 2, 4)

    def owner(step):
        row, column = 3 - step // 4, 3 - step % 4
        return row_of(step // 4) * 4 + lax.rem(xx + (2, 3, 1, 0)[step % 4], 4)

    def xy_copy(step):
        return pltpu.make_async_remote_copy(
            src_ref=xy_out.at[owner(step)], dst_ref=xy_in.at[m], send_sem=xy_send, recv_sem=xy_recv,
            device_id=xy_dev(owner(step)), device_id_type=MESH)

    def core_copy(chunk):
        return pltpu.make_async_remote_copy(
            src_ref=sums.at[1 - core, pl.ds(row_of(chunk) * 4, 4)], dst_ref=core_in.at[pl.ds(row_of(chunk) * 4, 4)],
            send_sem=core_send, recv_sem=core_recv.at[chunk],
            device_id=(sibling, r), device_id_type=MESH)

    for chunk in range(4):
        core_copy(chunk).start()
    for chunk in range(4):
        core_copy(chunk).wait_recv()
        for step in range(chunk * 4, chunk * 4 + 4):
            i = owner(step)
            if step < 15:
                xy_out[i] = to_steps(sums[core, i] + core_in[i])
        for step in range(chunk * 4, min(chunk * 4 + 4, 15)):
            @pl.when(owner(step) < share)
            def _():
                xy_copy(step).start()

    def input_part(a):
        wmat[...] = wturn[pl.ds(a * 9, 9)].reshape(9 * ROWS, G * C).astype(BF16)

        for n in parts:
            for at in range(0, (PARTS[n][1] - PARTS[n][0]) * X, 256):
                first = PARTS[n][0] * X + at
                fgm[:, first:first + 256] = jnp.dot(
                    wmat[...], cot[n][:, :, at:at + 256].reshape(G * C, 256), preferred_element_type=F32)
        for y in range(Y):
            total = None
            for c in range(3):
                column = None
                for b in range(3):
                    source = y - (b - 1)
                    if 0 <= source < Y:
                        term = fgm[(b * 3 + c) * ROWS:(b * 3 + c + 1) * ROWS, source * X:(source + 1) * X]
                        column = term if column is None else column + term
                if c == 0:
                    column = jnp.where(lane48 == X - 1, 0.0, pltpu.roll(column, X - 1, 1))
                elif c == 2:
                    column = jnp.where(lane48 == 0, 0.0, pltpu.roll(column, 1, 1))
                total = column if total is None else total + column
            part[a, :, y * X:(y + 1) * X] = total

    def part_copy(side):
        return pltpu.make_async_remote_copy(
            src_ref=part.at[2 - 2 * side], dst_ref=part_in.at[side], send_sem=pt_send,
            recv_sem=pt_recv, device_id=(up if side == 0 else down, r), device_id_type=MESH)

    crosses_z = at_end
    onward = s + 8 * (2 * core - 1)
    behind = s - 8 * (2 * core - 1)
    relays = jnp.logical_and(crosses_z, jnp.logical_and(behind >= 0, behind < SPACE))

    def along_z():
        return pltpu.make_async_remote_copy(
            src_ref=part.at[2 * core], dst_ref=passing, send_sem=pt_send, recv_sem=pass_recv,
            device_id=(onward, r), device_id_type=MESH)

    def along_y():
        return pltpu.make_async_remote_copy(
            src_ref=passing, dst_ref=part_in.at[1 - core], send_sem=pass_send, recv_sem=pt_recv,
            device_id=(s + 7 - 14 * core, r), device_id_type=MESH)

    def send_part(side, when):
        @pl.when(jnp.logical_and(s < SPACE - 1 if side == 0 else s > 0, when))
        def _():
            part_copy(side).start()

    input_part(2 * core)

    @pl.when(jnp.logical_and(crosses_z, jnp.logical_and(onward >= 0, onward < SPACE)))
    def _():
        along_z().start()

    for side in range(2):
        send_part(side, jnp.logical_and(jnp.logical_not(crosses_z), core == 1 - side))
    input_part(2 - 2 * core)
    for side in range(2):
        send_part(side, core == side)
    input_part(1)

    def z_copy(d):
        peer = lax.rem(zz + d, 8)
        return pltpu.make_async_remote_copy(
            src_ref=z_in.at[zz], dst_ref=z_in.at[zz], send_sem=z_send, recv_sem=z_recv,
            device_id=z_dev(peer), device_id_type=MESH)

    @pl.when(m < share)
    def _():
        unit[...] = sums[core, m] + core_in[m]
        whole(xy_in, 15, xy_send, xy_recv).wait_recv()
        for d in range(1, 16):
            unit[...] += from_steps(xy_in[lax.rem(m + d, 16)])
        z_in[zz] = to_steps(unit[...])
        for d in (4, 3, 5, 2, 6, 1, 7):
            z_copy(d).start()


    def ag_copy(d):
        return pltpu.make_async_remote_copy(
            src_ref=coded.at[mine + m], dst_ref=coded.at[mine + m], send_sem=ag_send, recv_sem=ag_recv.at[m],
            device_id=xy_dev(lax.rem(yy + d // 4 + 2, 4) * 4 + lax.rem(xx + d % 4, 4)), device_id_type=MESH)

    def finish_offset(q):
        block = from_steps(coded[q])
        wg_out[q, :, :X] = block[:G]
        wg_out[q, :, X:] = block[G:]

    def arrival(i):
        return pltpu.make_async_remote_copy(
            src_ref=coded.at[mine + i], dst_ref=coded.at[mine + i], send_sem=ag_send, recv_sem=ag_recv.at[i],
            device_id=(up, r), device_id_type=MESH)

    def forward(i):
        return pltpu.make_async_remote_copy(
            src_ref=coded.at[mine + i], dst_ref=coded.at[mine + i], send_sem=fwd_send, recv_sem=fwd_recv,
            device_id=(sibling, r), device_id_type=MESH)

    @pl.when(m < share)
    def _():
        whole(z_in, 7, z_send, z_recv).wait_recv()
        total = from_steps(z_in[0])
        for i in range(1, 8):
            total = total + from_steps(z_in[i])
        total = total * (1.0 / math.sqrt(G * SPACE * VOX))
        blank = jnp.zeros((X - C, X), F32)
        sides = [[], []]
        for octet in range(3):
            trans[...] = jnp.concatenate([total[octet * C:(octet + 1) * C], blank], 0).T
            for side in range(2):
                joined = None
                for j in range(8):
                    rows = trans[pl.ds(side * 8 + j, 8, stride=C), :]
                    rows = rows if j == 0 else pltpu.roll(rows, j * C, 1)
                    joined = rows if joined is None else joined + rows
                sides[side].append(joined)
        coded[mine + m] = to_steps(jnp.concatenate(sides[0] + sides[1], 0))
        for d in (10, 9, 11, 6, 14, 5, 7, 13, 15, 8, 2, 1, 3, 4, 12):
            ag_copy(d).start()
        forward(m).start()

    @pl.when(relays)
    def _():
        along_z().wait_recv()
        along_y().start()

    for i in range(16):
        @pl.when(jnp.logical_and(m != i, i < share))
        def _():
            arrival(i).wait_recv()
            forward(i).start()
            finish_offset(mine + i)

    @pl.when(m < share)
    def _():
        finish_offset(mine + m)

    both_sides(part_in, 1, pt_send, pt_recv, lambda copy: copy.wait_recv())
    for y in range(Y):
        cols = slice(y * X, (y + 1) * X)
        lay[pl.ds(y, ROWS, stride=Y), :] = part[1, :, cols] + part_in[0, :, cols] + part_in[1, :, cols]
    fg_out[...] = lay[...].reshape(ROWS, Y, X).astype(BF16)

    by_core(lambda count: whole(coded, TAPS - count, fwd_send, fwd_recv).wait_recv())

    @pl.when(core == 0)
    def _():
        for q in range(SHARES[0], TAPS):
            finish_offset(q)

    @pl.when(core == 1)
    def _():
        for q in range(SHARES[0]):
            finish_offset(q)


    for half in parts:
        rot_sent[half].wait_send()
    both_sides(feats, LOCAL, halo_send, halo_recv, lambda copy: copy.wait_send())
    both_sides(part_in, 1, pt_send, pt_recv, lambda copy: copy.wait_send())
    whole(core_in, 16, core_send, core_recv.at[0]).wait_send()
    by_core(lambda count: whole(coded, count, fwd_send, fwd_recv).wait_send())

    @pl.when(relays)
    def _():
        along_y().wait_send()


    @pl.when(m < share)
    def _():
        by_core(lambda count: whole(xy_in, count - 1, xy_send, xy_recv).wait_send())
        whole(z_in, 7, z_send, z_recv).wait_send()
        whole(xy_in, 15, ag_send, ag_recv.at[0]).wait_send()

    @pl.when(m >= share)
    def _():
        by_core(lambda count: whole(xy_in, count, xy_send, xy_recv).wait_send())


def finish(fg_in, wg_in, fg_out, wg_out, sem):
    pieces = [pltpu.make_async_copy(fg_in, fg_out, sem.at[0])]
    for i in range(3):
        some = pl.ds(9 * i, 9)
        pieces.append(pltpu.make_async_copy(wg_in.at[some], wg_out.at[some], sem.at[i + 1]))
    for copy in pieces:
        copy.start()
    for copy in pieces:
        copy.wait()


def local(features, cotangent, weight, relative, offset_perm):
    any_spec = pl.BlockSpec(memory_space=pl.ANY)
    vmem = pl.BlockSpec(memory_space=pltpu.VMEM)
    hbm = functools.partial(pltpu.with_memory_space_constraint, memory_space=pltpu.HBM)
    dma = pltpu.SemaphoreType.DMA
    fg, wg = pl.pallas_call(
        kernel,
        out_shape=(
            pltpu.VMEM((ROWS, Y, X), BF16),
            pltpu.VMEM((TAPS, G, C * C), F32),
        ),
        in_specs=[any_spec] * 5,
        out_specs=(vmem, vmem),
        scratch_shapes=[
            pltpu.SMEM((G, G), jnp.int32),
            pltpu.SMEM((G, TAPS), jnp.int32),
            pltpu.VMEM((2, ROWS, Y, X), BF16),
            pltpu.VMEM((TAPS, G, C * C), BF16),
            pltpu.VMEM((ROWS * Y, X), F32),
            *[pltpu.VMEM((G, C, (last - first) * X), BF16) for first, last in PARTS],
            pltpu.VMEM((3 * LOCAL, C, VOX), BF16),
            pltpu.VMEM((LOCAL, TAPS * C, VOX), BF16),
            pltpu.VMEM((LOCAL, G * C, VOX), BF16),
            pltpu.VMEM((656, C * C), F32),
            pltpu.VMEM((656, C * C), BF16),
            pltpu.VMEM((TAPS, G, C, X), F32),
            pltpu.VMEM((TAPS, ROWS, G * C), F32),
            pltpu.VMEM((9 * ROWS, G * C), BF16),
            pltpu.VMEM((LOCAL, 3, TAPS, C, X), F32),
            pltpu.SMEM((LOCAL * G,), jnp.int32),
            pltpu.VMEM((12, 6, 8, X), jnp.int32),
            pltpu.VMEM((2, 16, UNIT, X), F32),
            pltpu.VMEM((16, UNIT, X), F32),
            pltpu.VMEM((16, CODED, X), jnp.int16),
            pltpu.VMEM((16, CODED, X), jnp.int16),
            pltpu.VMEM((8, CODED, X), jnp.int16),
            pltpu.VMEM((UNIT, X), F32),
            pltpu.VMEM((X, X), F32),
            pltpu.VMEM((TAPS, CODED, X), jnp.int16),
            pltpu.VMEM((9 * ROWS, VOX), F32),
            pltpu.VMEM((3, ROWS, VOX), F32),
            pltpu.VMEM((2, ROWS, VOX), F32),
            pltpu.VMEM((ROWS, VOX), F32),
            dma((5,)), dma, dma((2,)), dma((2,)), dma, dma, dma, dma((4,)),
            dma, dma, dma, dma, dma, dma((16,)), dma, dma, dma, dma, dma, dma,
        ],
        compiler_params=pltpu.CompilerParams(
            collective_id=0, has_side_effects=True, vmem_limit_bytes=48 * 1024 * 1024
        ),
    )(
        hbm(relative), hbm(offset_perm),
        hbm(cotangent.reshape(ROWS, Y, X)), hbm(features.reshape(ROWS, Y, X)), hbm(weight),
    )
    fg, wg = pl.pallas_call(
        finish,
        out_shape=(
            jax.ShapeDtypeStruct((ROWS, Y, X), BF16),
            jax.ShapeDtypeStruct((TAPS, G, C * C), F32),
        ),
        in_specs=[vmem] * 2,
        out_specs=(any_spec, any_spec),
        scratch_shapes=[dma((4,))],
        compiler_params=pltpu.CompilerParams(vmem_limit_bytes=8 * 1024 * 1024),
    )(fg, wg)
    return fg.reshape(features.shape), wg


def solution(mesh):
    field = P("rot", None, "space", None, None)
    return jax.shard_map(
        local,
        mesh=mesh,
        in_specs=(field, field, P(), P(), P()),
        out_specs=(field, P()),
        check_vma=False,
    )
```
